32 devices in a mesh: dp: 8 (over z, core), shard: 4 (over y, x).
Axes of the slice: x: 2, y: 2, z: 4, core: 2. Of those that a mesh axis runs over, the one named last changes fastest.
Arguments:
- x_input: bfloat16 [256, 32, 28, 192], P('dp', 'shard'), may hold values from -6 to 6
- image_counts: int32 [8], P('dp'), may hold values from 16 to 32, as said below
- kernel_one: bfloat16 [3, 3, 192, 384], replicated, may hold values from -0.15625 to 0.15625
- point_one: bfloat16 [192, 384], replicated, may hold values from -0.4375 to 0.4375
- block_one_norm_gains: float32 [2, 384], replicated, may hold values from 0.5 to 1.5
- block_one_norm_shifts: float32 [2, 384], replicated, may hold values from -3 to 3
- kernel_two: bfloat16 [3, 3, 384, 384], P(None, None, 'shard'), may hold values from -0.109375 to 0.109375
- point_two: bfloat16 [384, 384], P('shard'), may hold values from -0.3125 to 0.3125
- block_two_norm_gains: float32 [3, 384], P(None, 'shard'), may hold values from 0.5 to 1.5
- shifts_two: float32 [3, 384], P(None, 'shard'), may hold values from -3 to 3
- cotangent: bfloat16 [256, 16, 14, 384], P('dp', None, None, 'shard'), may hold values from -6 to 6
Outputs:
- block_out: float32 [256, 16, 14, 384], P('dp', None, None, 'shard')
- grad_input: float32 [256, 32, 28, 192], P('dp', 'shard')
- grad_kernel_one: float32 [3, 3, 192, 384], replicated
- grad_point_one: float32 [192, 384], replicated
- grad_gains_one: float32 [2, 384], replicated
- grad_shifts_one: float32 [2, 384], replicated
- grad_kernel_two: float32 [3, 3, 384, 384], P(None, None, 'shard')
- grad_point_two: float32 [384, 384], P('shard')
- grad_gains_two: float32 [3, 384], P(None, 'shard')
- grad_shifts_two: float32 [3, 384], P(None, 'shard')
The draws below stay inside these ranges and needn't reach their ends.
Inputs may be any that keep to these rules, and one draw needn't show every extreme that they name: `image_counts`: A group's slots are alive from slot 0 up to its count, micro-batch by micro-batch; at least one group has all 32 alive.
All inputs are finite; a program needn't handle non-finite values.
Results may differ from the reference program's by a relative error of at most 0.02.
Values may be sent and summed in bfloat16 or wider, within the bound.
A program may use at most 256 MiB of HBM per device.

```python
import jax
import jax.numpy as jnp
from jax import lax

C_IN = 192
C_MID = 384
IN_COLS = 28
IMG_MB = 16
MICRO = 2
OUT_COLS = 14
OUT_ROWS = 16
IN_ROWS = 32
GROUPS = 8
IMAGES = 256


def draw_image_counts(key, part):
    key = jax.random.fold_in(key, 7)
    first_key, second_key = jax.random.split(key)
    slots = IMG_MB * MICRO
    counts = jax.random.randint(first_key, (GROUPS,), slots // 2, slots + 1).astype(jnp.int32)
    full_group = jax.random.randint(second_key, (), 0, GROUPS)
    group_index = jnp.arange(GROUPS)
    return jnp.where(group_index == full_group, slots, counts).astype(jnp.int32)


def levels(stream_key, shape, shards, low, top_value):
    loudness = 1.0
    for axis_at, shards_of in shards:
        steps = jax.random.uniform(jax.random.fold_in(jax.random.fold_in(stream_key, 6), axis_at), (shards_of,), jnp.float32, low / len(shards), top_value / len(shards))
        loudness = loudness * jnp.repeat(jnp.exp(steps), shape[axis_at] // shards_of).reshape((-1,) + (1,) * (len(shape) - 1 - axis_at))
    return loudness


def normal_values(stream_key, dims, width, bound, pieces=(), dtype=jnp.bfloat16):
    entries = width * jax.random.normal(stream_key, dims, jnp.float32)
    if pieces:
        entries = entries * levels(stream_key, dims, pieces, -0.22, 0.18)
    return jnp.clip(entries, -bound, bound).astype(dtype)


def setup_inputs(seed: int = 0) -> dict:
    streams_of = jax.random.split(jax.random.key(seed), 12)
    return {
        "x_input": normal_values(streams_of[0], (IMAGES, IN_ROWS, IN_COLS, C_IN), 1.0, 6.0, ((0, 8), (1, 4))),
        "image_counts": draw_image_counts(jax.random.fold_in(streams_of[11], 71), 0),
        "kernel_one": normal_values(streams_of[2], (3, 3, C_IN, C_MID), (9 * C_IN) ** -0.5, 0.15625),
        "point_one": normal_values(streams_of[3], (C_IN, C_MID), C_IN ** -0.5, 0.4375),
        "block_one_norm_gains": jnp.clip(1.0 + 0.1 * jax.random.normal(streams_of[4], (2, C_MID), jnp.float32), 0.5, 1.5),
        "block_one_norm_shifts": normal_values(streams_of[5], (2, C_MID), 0.5, 3.0, (), jnp.float32),
        "kernel_two": normal_values(streams_of[6], (3, 3, C_MID, C_MID), (9 * C_MID) ** -0.5, 0.109375, ((2, 4),)),
        "point_two": normal_values(streams_of[7], (C_MID, C_MID), C_MID ** -0.5, 0.3125, ((0, 4),)),
        "block_two_norm_gains": jnp.clip(1.0 + 0.1 * jax.random.normal(streams_of[8], (3, C_MID), jnp.float32), 0.5, 1.5),
        "shifts_two": normal_values(streams_of[9], (3, C_MID), 0.5, 3.0, ((1, 4),), jnp.float32),
        "cotangent": normal_values(streams_of[10], (IMAGES, OUT_ROWS, OUT_COLS, C_MID), 1.0, 6.0, ((0, 8), (3, 4))),
    }


@jax.custom_vjp
def low(v):
    return lax.optimization_barrier(v.astype(jnp.bfloat16)).astype(jnp.float32)

@jax.custom_vjp
def low_back(v):
    return v

def low_keep(v):
    return (low(v), None)

def low_pass(kept, grad):
    return (grad,)

def back_keep(v):
    return (v, None)

def back_low(kept, grad):
    return (low(grad),)
low.defvjp(low_keep, low_pass)
low_back.defvjp(back_keep, back_low)
EPSILON = 1e-05

def convolve(value, kernel, stride):
    return lax.conv_general_dilated(value, kernel, (stride, stride), ((1, 1), (1, 1)), dimension_numbers=('NHWC', 'HWIO', 'NHWC'), precision=lax.Precision.HIGHEST)

def batch_norm(value, alive_map, pixel_count_total, norm_gain_value, shift):
    center = lax.optimization_barrier(jnp.sum(value * alive_map, axis=(0, 1, 2))) / pixel_count_total
    square = lax.optimization_barrier(jnp.sum(value * value * alive_map, axis=(0, 1, 2))) / pixel_count_total
    scaled_inverse_std = lax.rsqrt(square - center * center + EPSILON)
    return (value - center) * scaled_inverse_std * norm_gain_value + shift

def forward(images, alive, kernel_one, point_one, block_one_norm_gains, block_one_norm_shifts, kernel_two, point_two, block_two_norm_gains, shifts_two):
    row_real = (jnp.arange(OUT_ROWS) < IN_COLS // 2).astype(jnp.float32)[None, :, None, None]
    alive_map = alive[:, None, None, None] * row_real
    pixel_count_total = jnp.sum(alive) * (IN_COLS // 2) * OUT_COLS
    z3a = low_back(convolve(images, kernel_one, 2))
    z1a = low_back(jnp.einsum('irwc,cd->irwd', images[:, ::2, ::2], point_one, precision=lax.Precision.HIGHEST))
    first = batch_norm(z3a, alive_map, pixel_count_total, block_one_norm_gains[0], block_one_norm_shifts[0]) + batch_norm(z1a, alive_map, pixel_count_total, block_one_norm_gains[1], block_one_norm_shifts[1])
    hidden = low_back(low(row_real * jax.nn.silu(first)))
    threebythree_output_second = low_back(convolve(hidden, kernel_two, 1))
    pointwise_output_second = low_back(jnp.einsum('irwc,cd->irwd', hidden, point_two, precision=lax.Precision.HIGHEST))
    second = batch_norm(threebythree_output_second, alive_map, pixel_count_total, block_two_norm_gains[0], shifts_two[0])
    second = second + batch_norm(pointwise_output_second, alive_map, pixel_count_total, block_two_norm_gains[1], shifts_two[1])
    second = second + batch_norm(hidden, alive_map, pixel_count_total, block_two_norm_gains[2], shifts_two[2])
    return alive_map * jax.nn.silu(second)

def reference(x_input, image_counts, kernel_one, point_one, block_one_norm_gains, block_one_norm_shifts, kernel_two, point_two, block_two_norm_gains, shifts_two, cotangent):
    slots = IMG_MB * MICRO
    slot_index = jnp.arange(slots).astype(jnp.int32)
    alive_all = (slot_index[None, :] < image_counts[:, None]).astype(jnp.float32)
    alive_all = alive_all.reshape(GROUPS, MICRO, IMG_MB)
    images_all = x_input.reshape(GROUPS, MICRO, IMG_MB, IN_ROWS, IN_COLS, C_IN)
    cot_all = cotangent.reshape(GROUPS, MICRO, IMG_MB, OUT_ROWS, OUT_COLS, C_MID)
    params = tuple((p.astype(jnp.float32) for p in (kernel_one, point_one, block_one_norm_gains, block_one_norm_shifts, kernel_two, point_two, block_two_norm_gains, shifts_two)))
    outputs = []
    input_grads = []
    totals = tuple((jnp.zeros_like(p) for p in params))
    for step_index in range(MICRO):
        images = images_all[:, step_index].reshape(GROUPS * IMG_MB, IN_ROWS, IN_COLS, C_IN).astype(jnp.float32)
        alive = alive_all[:, step_index].reshape(GROUPS * IMG_MB)
        cot_here = cot_all[:, step_index].reshape(GROUPS * IMG_MB, OUT_ROWS, OUT_COLS, C_MID).astype(jnp.float32)
        result, pull = jax.vjp(lambda xv, *pv: forward(xv, alive, *pv), images, *params)
        grads = pull(cot_here)
        outputs.append(result.reshape(GROUPS, 1, IMG_MB, OUT_ROWS, OUT_COLS, C_MID))
        input_grads.append(grads[0].reshape(GROUPS, 1, IMG_MB, IN_ROWS, IN_COLS, C_IN))
        totals = tuple((a + b for a, b in zip(totals, grads[1:])))
    block_out = jnp.concatenate(outputs, axis=1).reshape(IMAGES, OUT_ROWS, OUT_COLS, C_MID)
    grad_input = jnp.concatenate(input_grads, axis=1).reshape(IMAGES, IN_ROWS, IN_COLS, C_IN)
    return (block_out, grad_input, totals[0], totals[1], totals[2], totals[3], totals[4], totals[5], totals[6], totals[7])
```

```python
import functools

import jax
import jax.numpy as jnp
from jax import lax
from jax.experimental import pallas as pl
from jax.experimental.pallas import tpu as pltpu
from jax.sharding import PartitionSpec as P

MICRO = 2
EPSILON = 1e-05
KEPT = 16
PAYLOAD = 24
MESH = pl.DeviceIdType.MESH
BF16 = jnp.bfloat16
F32 = jnp.float32


def up_to(value, step):
    return (value + step - 1) // step * step


def flat(value):
    return value.reshape(-1, value.shape[-1])


def dot(a, b):
    return jnp.dot(a, b, preferred_element_type=F32)


def dot_nt(a, b):
    return lax.dot_general(a, b, (((1,), (1,)), ((), ())), preferred_element_type=F32)


def dot_tn(a, b):
    return lax.dot_general(a, b, (((0,), (0,)), ((), ())), preferred_element_type=F32)


def eight(value):
    rows, lanes = value.shape
    return jnp.sum(value.reshape(rows // 8, 8, lanes), axis=0)


def sigmoid(value):
    return 0.5 * jnp.tanh(0.5 * value) + 0.5


class Sizes:
    def __init__(self, mesh, x_input, cotangent, point_one):
        self.groups, self.parts = mesh.shape["dp"], mesh.shape["shard"]
        self.images = x_input.shape[0] // self.groups
        self.in_rows = x_input.shape[1] // self.parts
        self.in_cols, self.c_in = x_input.shape[2:]
        self.rows = self.in_rows // 2
        self.cols = self.in_cols // 2
        self.c_mid = point_one.shape[1]
        self.c_local = self.c_mid // self.parts
        self.c_pad = up_to(self.c_local, 16)
        self.batch = self.images // MICRO
        self.tile = max(1, min(self.batch, 512 // (self.rows * KEPT)))
        self.tiles = self.images // self.tile
        self.pair = 2 if self.groups % 2 == 0 else 1
        self.depth = self.groups // self.pair
        self.half = -(-10 // self.pair)
        self.sub_two = up_to(self.half * self.c_pad, 16 * self.depth) // self.depth
        self.piece_two = self.sub_two * self.depth
        real = 10 * self.c_in
        self.sub_one = up_to(real, 16 * self.depth * self.parts * self.pair) // (
            self.depth * self.parts * self.pair
        )
        self.piece_one = self.sub_one * self.depth


class Sender:
    def __init__(self):
        self.open = []

    def start(self, make, *given, when=None):
        if when is None:
            make(*given).start()
        else:
            pl.when(when)(make(*given).start)
        self.open.append((make, given, when))

    def finish(self):
        for make, given, when in self.open:
            if when is None:
                make(*given).wait_send()
            else:
                pl.when(when)(make(*given).wait_send)
        self.open = []


def kernel(
    z,
    count,
    x_hbm,
    k1_hbm,
    p1_hbm,
    norm_one,
    k2_hbm,
    p2_hbm,
    norm_two,
    cot_hbm,
    out_hbm,
    grad_in_hbm,
    grad_one_hbm,
    grad_two_hbm,
    small,
    odd_win,
    even_win,
    k1_win,
    k1_own,
    p1_win,
    z3a,
    z1a,
    x_above,
    halo,
    wide,
    cut,
    slope,
    mask,
    acc,
    par,
    pay,
    slots_a,
    slots_z,
    totals,
    g_one,
    one_r2,
    one_s,
    one_r3,
    one_r4,
    two_r1,
    two_r2,
    two_s,
    two_r3,
    two_r4,
    local_sem,
    x_sem,
    hid_sem,
    dz_sem,
    e_sem,
    ag_sem,
    ag_pair_sem,
    cot_sem,
    out_sem,
    ea_send,
    ea_recv,
    ez_send,
    ez_recv,
    ar_one,
    ar_two,
    gi_sem,
):
    n, pair, depth = z.parts, z.pair, z.depth
    rows, c_mid, c_in, tile = z.rows, z.c_mid, z.c_in, z.tile
    batch, images = z.batch, z.images
    dp = lax.axis_index("dp")
    sh = lax.axis_index("shard")
    core = lax.rem(dp, pair)
    deep = lax.div(dp, pair)
    sibling = (dp + 1 - 2 * core, sh)
    me = core * n + sh
    has_above = sh > 0
    has_below = sh < n - 1
    above, below = (dp, sh - 1), (dp, sh + 1)
    per_batch = batch // tile

    def plane(k):
        return lax.rem(sh + k, n)

    def group_peer(k):
        slot = lax.rem(me + k, pair * n)
        return slot, (dp - core + lax.div(slot, n), lax.rem(slot, n))

    def deep_peer(k):
        other = lax.rem(deep + k, depth)
        return other, (other * pair + core, sh)

    def remote(src, dst, send, recv, device):
        return pltpu.make_async_remote_copy(
            src_ref=src,
            dst_ref=dst,
            send_sem=send,
            recv_sem=recv,
            device_id=device,
            device_id_type=MESH,
        )

    barrier = pltpu.get_barrier_semaphore()
    for k in range(1, pair * n):
        pl.semaphore_signal(barrier, 1, device_id=group_peer(k)[1], device_id_type=MESH)
    for k in range(1, depth):
        pl.semaphore_signal(barrier, 1, device_id=deep_peer(k)[1], device_id_type=MESH)

    own_loads = []

    def load(src, dst):
        copy = pltpu.make_async_copy(src, dst, local_sem.at[len(own_loads)])
        copy.start()
        own_loads.append(copy)

    def wide_rows(half, part, offset, length):
        start = (half * n + part) * z.piece_two + offset
        if not isinstance(start, int):
            start = pl.multiple_of(start, 16)
        return wide.at[pl.ds(start, length)]

    taps = [k2_hbm.at[t // 3, t % 3] for t in range(9)] + [p2_hbm]
    for t in range(10):
        load(taps[t], wide_rows(t // z.half, sh, t % z.half * z.c_pad, z.c_pad))
    n_wide = len(own_loads)
    for d in range(3):
        load(k1_hbm.at[d, 1], k1_win.at[d, pl.ds(0, 192)])
        load(k1_hbm.at[d, 0, pl.ds(128, 64)], k1_win.at[d, pl.ds(192, 64)])
        load(k1_hbm.at[d, 0, pl.ds(0, 128)], k1_win.at[d, pl.ds(256, 128)])
        load(k1_hbm.at[d, 2], k1_win.at[d, pl.ds(384, 192)])
    load(p1_hbm, p1_win.at[pl.ds(0, 192)])
    load(k1_hbm, k1_own)

    pl.semaphore_wait(barrier, pair * n - 1 + depth - 1)

    sender = Sender()
    gather = Sender()

    def x_copy():
        return remote(x_hbm.at[:, z.in_rows - 1], x_above, x_sem.at[0], x_sem.at[1], below)

    sender.start(x_copy, when=has_below)

    row_at = lax.broadcasted_iota(jnp.int32, mask.shape, 0) + sh * rows
    col_at = lax.broadcasted_iota(jnp.int32, mask.shape, 1)
    mask[...] = jnp.where((row_at < z.cols) & (col_at < z.cols), 1.0, 0.0)

    @pl.when(jnp.logical_not(has_above))
    def _():
        x_above[...] = jnp.zeros_like(x_above)
        halo[0] = jnp.zeros(halo.shape[1:], BF16)

    @pl.when(jnp.logical_not(has_below))
    def _():
        halo[1] = jnp.zeros(halo.shape[1:], BF16)

    for d in range(3):
        k1_win[d, 576:640] = jnp.zeros((64, c_mid), BF16)
    p1_win[192:256] = jnp.zeros((64, c_mid), BF16)

    for copy in own_loads[:n_wide]:
        copy.wait()
    ag_length = z.half * z.c_pad

    def gather_copy(k):
        own = wide_rows(core, sh, 0, ag_length)
        return remote(own, own, ag_sem.at[0, k], ag_sem.at[1, sh], (dp, plane(k)))

    for k in range(1, n):
        gather.start(gather_copy, k)

    def three(value):
        return jnp.concatenate([value] * (c_mid // 128), axis=-1)

    def images_at(t):
        return pl.ds(pl.multiple_of(t * tile, tile), tile)

    def mask_at(t):
        shape = (tile, rows, KEPT, 128)
        image_at = lax.broadcasted_iota(jnp.int32, shape, 0) + t * tile
        return three(flat(jnp.where(image_at < count[0], mask[...][None], 0.0)))

    def pixels_at():
        return three(flat(jnp.broadcast_to(mask[...][None], (tile, rows, KEPT, 128))))

    def shaped(value, count_=None):
        return value.reshape(-1, rows, KEPT, value.shape[-1])

    def add_to(batch_at, at, value):
        acc[batch_at, at] = acc[batch_at, at] + eight(value)

    def exchange(e):
        pay[e, 0:16] = jnp.sum(acc[...], axis=2).reshape(16, c_mid)
        pay[e, 16:24] = norm_two[...] if e == 0 else jnp.zeros((8, c_mid), F32)
        slots_a[e, me] = pay[e]
        copies = []
        for k in range(1, pair * n):
            copies.append(
                remote(
                    pay.at[e],
                    slots_a.at[e, me],
                    ea_send.at[e, k],
                    ea_recv.at[e, me],
                    group_peer(k)[1],
                )
            )
        for copy in copies:
            copy.start()
        for k in range(1, pair * n):
            slot, device = group_peer(k)
            remote(
                pay.at[e], slots_a.at[e, slot], ea_send.at[e, k], ea_recv.at[e, slot], device
            ).wait_recv()
        total = slots_a[e, 0]
        for slot in range(1, pair * n):
            total = total + slots_a[e, slot]
        slots_z[e, deep] = total
        for k in range(1, depth):
            copy = remote(
                slots_z.at[e, deep],
                slots_z.at[e, deep],
                ez_send.at[e, k],
                ez_recv.at[e, deep],
                deep_peer(k)[1],
            )
            copy.start()
            copies.append(copy)
        for k in range(1, depth):
            other, device = deep_peer(k)
            remote(
                slots_z.at[e, deep], slots_z.at[e, other], ez_send.at[e, k], ez_recv.at[e, other], device
            ).wait_recv()
        total = slots_z[e, 0]
        for other in range(1, depth):
            total = total + slots_z[e, other]
        totals[e] = total
        for copy in copies:
            copy.wait_send()

    def moments(e, base, at, pixels):
        center = totals[e, base + at : base + at + 1] / pixels
        square = totals[e, base + at + 1 : base + at + 2] / pixels
        return center, lax.rsqrt(square - center * center + EPSILON)

    def first_part(x_own, x_wide):
        loads = []
        step = 8 if images % 8 == 0 else images
        for at in range(0, images, step):
            copy = pltpu.make_async_copy(
                x_hbm.at[pl.ds(at, step)], x_own.at[pl.ds(at, step)], gi_sem.at[at // step]
            )
            copy.start()
            loads.append(copy)
        x_wide[...] = jnp.zeros_like(x_wide)

        def windows(value):
            g = value.shape[0]
            x_wide[0, 0:g, 0 : z.in_cols, :] = value[:, :, 0:128].astype(F32)
            x_wide[1, 0:g, 0 : z.in_cols, 0:64] = value[:, :, 128:192].astype(F32)
            even = [x_wide[i, 0:g, pl.ds(0, KEPT, stride=2), :] for i in (0, 1)]
            odd = [x_wide[i, 0:g, pl.ds(1, KEPT, stride=2), :] for i in (0, 1)]
            even = [flat(v) for v in even]
            odd = [flat(v) for v in odd]
            before = [pltpu.roll(v, 1, 0) for v in odd]
            mixed = even[1] + pltpu.roll(before[1], 64, 1)
            parts = [even[0], mixed, before[0], odd[0], odd[1]]
            return jnp.concatenate([v.astype(BF16) for v in parts], axis=1).reshape(g, KEPT, 640)

        group = max(1, 32 // z.in_rows)
        for at in range(0, images, step):
            loads[at // step].wait()

            def extract(i, carry):
                here = at + i * group
                value = x_own[pl.ds(here, group)].reshape(group * z.in_rows, z.in_cols, c_in)
                window = windows(value).reshape(group, rows, 2, KEPT, 640)
                even_win[pl.ds(here, group)] = window[:, :, 0]
                odd_win[pl.ds(here, group), 1 : rows + 1] = window[:, :, 1]
                return carry

            lax.fori_loop(0, step // group, extract, 0)

        pl.when(has_above)(x_copy().wait_recv)

        def extract_above(i, carry):
            odd_win[pl.ds(i * 32, 32), 0] = windows(x_above[pl.ds(i * 32, 32)])
            return carry

        lax.fori_loop(0, images // 32, extract_above, 0)

    pl.run_scoped(
        first_part,
        pltpu.VMEM((images, z.in_rows, z.in_cols, c_in), BF16),
        pltpu.VMEM((2, 32, 32, 128), F32),
    )

    for copy in own_loads[n_wide:]:
        copy.wait()
    acc[...] = jnp.zeros_like(acc)

    def forward_one(t, carry):
        here = images_at(t)
        b = t // per_batch
        side = flat(even_win[here])
        three_branch = dot(flat(odd_win[here, 0:rows]), k1_win[0])
        three_branch = three_branch + dot(side, k1_win[1])
        three_branch = three_branch + dot(flat(odd_win[here, 1 : rows + 1]), k1_win[2])
        point_branch = dot(side[:, 0:256], p1_win[...])
        z3a[here] = shaped(three_branch)
        z1a[here] = shaped(point_branch)
        m = mask_at(t)
        masked = three_branch * m
        add_to(b, 0, masked)
        add_to(b, 1, masked * three_branch)
        masked = point_branch * m
        add_to(b, 2, masked)
        add_to(b, 3, masked * point_branch)
        add_to(b, 4, m)
        return carry

    lax.fori_loop(0, z.tiles, forward_one, 0)

    def cot_copy(k):
        to = plane(k)
        return remote(
            cot_hbm.at[:, pl.ds(to * rows, rows)],
            cut.at[sh],
            cot_sem.at[0, k],
            cot_sem.at[1, sh],
            (dp, to),
        )

    for k in range(1, n):
        sender.start(cot_copy, k)
    cot_own = pltpu.make_async_copy(
        cot_hbm.at[:, pl.ds(sh * rows, rows)], cut.at[sh], cot_sem.at[1, sh]
    )
    cot_own.start()

    exchange(0)

    def pass_copy(k):
        part = plane(k)
        piece = wide_rows(core, part, 0, ag_length)
        return remote(piece, piece, ag_pair_sem.at[0, k], ag_pair_sem.at[1, part], sibling)

    for k in range(1, n):
        part = plane(k)
        piece = wide_rows(core, part, 0, ag_length)
        remote(piece, piece, ag_sem.at[0, k], ag_sem.at[1, part], (dp, part)).wait_recv()
        if pair == 2:
            gather.start(pass_copy, k)

    for b in range(MICRO):
        pixels = totals[0, b * 8 + 4 : b * 8 + 5]
        center_three, rstd_three = moments(0, b * 8, 0, pixels)
        center_point, rstd_point = moments(0, b * 8, 2, pixels)
        scale_three = norm_one[0:1] * rstd_three
        scale_point = norm_one[1:2] * rstd_point
        par[0, b, 0:1] = scale_three
        par[0, b, 1:2] = scale_point
        par[0, b, 2:3] = (norm_one[2:3] - center_three * scale_three) + (
            norm_one[3:4] - center_point * scale_point
        )
        par[0, b, 3:4] = center_three
        par[0, b, 4:5] = center_point
        par[0, b, 5:6] = rstd_three
        par[0, b, 6:7] = rstd_point
        par[0, b, 7:8] = pixels

    def first_sum(here, b):
        return (
            flat(z3a[here]) * par[0, b, 0:1]
            + flat(z1a[here]) * par[0, b, 1:2]
            + par[0, b, 2:3]
        )

    def put_three(target, here, at, count_, value):
        length = value.shape[0]
        shape = (-1, count_, KEPT, c_mid)
        before = pltpu.roll(value, 1, 0)
        after = pltpu.roll(value, length - 1, 0)
        target[here, at : at + count_, :, 0:c_mid] = before.astype(BF16).reshape(shape)
        target[here, at : at + count_, :, c_mid : 2 * c_mid] = value.astype(BF16).reshape(shape)
        target[here, at : at + count_, :, 2 * c_mid : 3 * c_mid] = after.astype(BF16).reshape(shape)

    def send_rims(source, sems):
        copies = []
        center = pl.ds(c_mid, c_mid)
        for b in range(MICRO):
            some = pl.ds(b * batch, batch)
            copies.append(
                (
                    remote(
                        source.at[some, 1, :, center],
                        halo.at[1, some],
                        sems.at[0, b],
                        sems.at[1, b],
                        above,
                    ),
                    remote(
                        source.at[some, rows, :, center],
                        halo.at[0, some],
                        sems.at[2, b],
                        sems.at[3, b],
                        below,
                    ),
                )
            )
        return copies

    def spread_halo(target, t):
        here = images_at(t)
        put_three(target, here, 0, 1, flat(halo[0, here]).astype(F32))
        put_three(target, here, rows + 1, 1, flat(halo[1, here]).astype(F32))

    def start_rims(copies, b):
        pl.when(has_above)(copies[b][0].start)
        pl.when(has_below)(copies[b][1].start)

    def take_rims(copies, b):
        pl.when(has_below)(copies[b][0].wait_recv)
        pl.when(has_above)(copies[b][1].wait_recv)

    def close_rims(copies):
        for b in range(MICRO):
            pl.when(has_above)(copies[b][0].wait_send)
            pl.when(has_below)(copies[b][1].wait_send)

    class Reduce:
        def __init__(self, g, r1, r2, s, r3, r4, sems, piece, sub):
            self.g, self.r1, self.r2, self.s, self.r3, self.r4 = g, r1, r2, s, r3, r4
            self.sems, self.piece, self.sub = sems, piece, sub

        def at(self, half, part):
            return pl.ds(pl.multiple_of((half * n + part) * self.piece, 16), self.piece)

        def pair_copy(self):
            start = pl.multiple_of((1 - core) * n * self.piece, 16)
            return remote(
                self.g.at[pl.ds(start, n * self.piece)],
                self.r1,
                self.sems.at[0, 0],
                self.sems.at[1, 0],
                sibling,
            )

        def start_pair(self):
            if pair == 2:
                sender.start(self.pair_copy)

        def start_plane(self):
            if pair == 2:
                self.pair_copy().wait_recv()

                def join(part, carry):
                    at = self.at(core, part)
                    arrived = self.r1[
                        pl.ds(pl.multiple_of(part * self.piece, 16), self.piece)
                    ]
                    self.g[at] = (self.g[at].astype(F32) + arrived.astype(F32)).astype(BF16)
                    return carry

                lax.fori_loop(0, n, join, 0)
            self.r2[sh] = self.g[self.at(core, sh)]

            def plane_copy(k):
                to = plane(k)
                return remote(
                    self.g.at[self.at(core, to)],
                    self.r2.at[sh],
                    self.sems.at[2, k],
                    self.sems.at[3, sh],
                    (dp, to),
                )

            for k in range(1, n):
                sender.start(plane_copy, k)

        def start_deep(self):
            for k in range(1, n):
                part = plane(k)
                remote(
                    self.r2.at[part],
                    self.r2.at[part],
                    self.sems.at[2, k],
                    self.sems.at[3, part],
                    (dp, part),
                ).wait_recv()
            total = self.r2[0].astype(F32)
            for part in range(1, n):
                total = total + self.r2[part].astype(F32)
            self.s[...] = total.astype(BF16).reshape(self.s.shape)
            self.r3[deep] = self.s[deep]

            def deep_copy(k):
                other, device = deep_peer(k)
                return remote(
                    self.s.at[other],
                    self.r3.at[deep],
                    self.sems.at[4, k],
                    self.sems.at[5, deep],
                    device,
                )

            for k in range(1, depth):
                sender.start(deep_copy, k)

        def start_back(self):
            for k in range(1, depth):
                other, device = deep_peer(k)
                remote(
                    self.r3.at[other],
                    self.r3.at[other],
                    self.sems.at[4, k],
                    self.sems.at[5, other],
                    device,
                ).wait_recv()
            total = self.r3[0].astype(F32)
            for other in range(1, depth):
                total = total + self.r3[other].astype(F32)
            self.r4[deep] = total.astype(BF16)

            def back_copy(k):
                own = self.r4.at[deep]
                return remote(
                    own, own, self.sems.at[6, k], self.sems.at[7, deep], deep_peer(k)[1]
                )

            for k in range(1, depth):
                sender.start(back_copy, k)

        def finish_back(self):
            for k in range(1, depth):
                other, device = deep_peer(k)
                remote(
                    self.r4.at[other],
                    self.r4.at[other],
                    self.sems.at[6, k],
                    self.sems.at[7, other],
                    device,
                ).wait_recv()

    red_two = Reduce(
        wide, two_r1.at[pl.ds(0, n * z.piece_two)], two_r2, two_s, two_r3, two_r4, ar_two, z.piece_two, z.sub_two
    )
    red_one = Reduce(
        g_one, two_r1.at[pl.ds(0, n * z.piece_one)], one_r2, one_s, one_r3, one_r4, ar_one, z.piece_one, z.sub_one
    )

    def second_part(hid, k2, p2, z3b, dz3, dz1, wide_cot):
        rims = send_rims(hid, hid_sem)

        def make_hidden(t, carry):
            here = images_at(t)
            b = t // per_batch
            total = first_sum(here, b)
            keep = pixels_at()
            put_three(hid, here, 1, rows, keep * (total * sigmoid(total)))
            return carry

        for b in range(MICRO):
            lax.fori_loop(b * per_batch, (b + 1) * per_batch, make_hidden, 0)
            start_rims(rims, b)

        if pair == 2:
            for k in range(1, n):
                part = plane(k)
                piece = wide_rows(1 - core, part, 0, ag_length)
                remote(
                    piece, piece, ag_pair_sem.at[0, k], ag_pair_sem.at[1, part], sibling
                ).wait_recv()
        gather.finish()
        for t in range(10):
            for part in range(n):
                start = (t // z.half * n + part) * z.piece_two + t % z.half * z.c_pad
                value = wide[start : start + z.c_local]
                if t < 9:
                    base = t % 3 * c_mid + part * z.c_local
                    k2[t // 3, base : base + z.c_local] = value
                else:
                    p2[part * z.c_local : (part + 1) * z.c_local] = value

        acc[...] = jnp.zeros_like(acc)

        def forward_two(t, carry):
            here = images_at(t)
            b = t // per_batch
            spread_halo(hid, t)
            three_branch = dot(flat(hid[here, 0:rows]), k2[0])
            three_branch = three_branch + dot(flat(hid[here, 1 : rows + 1]), k2[1])
            three_branch = three_branch + dot(flat(hid[here, 2 : rows + 2]), k2[2])
            center = flat(hid[here, 1 : rows + 1, :, c_mid : 2 * c_mid])
            point_branch = dot(center, p2[...])
            z3b[here] = shaped(three_branch)
            m = mask_at(t)
            masked = three_branch * m
            add_to(b, 0, masked)
            add_to(b, 1, masked * three_branch)
            masked = point_branch * m
            add_to(b, 2, masked)
            add_to(b, 3, masked * point_branch)
            center = center.astype(F32)
            masked = center * m
            add_to(b, 4, masked)
            add_to(b, 5, masked * center)
            return carry

        for b in range(MICRO):
            take_rims(rims, b)
            lax.fori_loop(b * per_batch, (b + 1) * per_batch, forward_two, 0)

        exchange(1)
        close_rims(rims)

        for b in range(MICRO):
            pixels = par[0, b, 7:8]
            offset = 0.0
            for i in range(3):
                center, rstd = moments(1, b * 8, 2 * i, pixels)
                scale = totals[0, 16 + i : 17 + i] * rstd
                par[1, b, i : i + 1] = scale
                par[1, b, 4 + i : 5 + i] = center
                par[1, b, 7 + i : 8 + i] = rstd
                offset = offset + (totals[0, 19 + i : 20 + i] - center * scale)
            par[1, b, 3:4] = offset

        cot_own.wait()
        for k in range(1, n):
            part = plane(k)
            remote(
                cut.at[part], cut.at[part], cot_sem.at[0, k], cot_sem.at[1, part], (dp, part)
            ).wait_recv()
        acc[...] = jnp.zeros_like(acc)
        wide_cot[...] = jnp.zeros_like(wide_cot)

        def slope_two(t, carry):
            here = images_at(t)
            b = t // per_batch
            for part in range(n):
                lanes = slice(part * z.c_local, (part + 1) * z.c_local)
                wide_cot[:, :, 0 : z.cols, lanes] = cut[part, here].astype(F32)
            v3 = flat(z3b[here])
            vi = flat(hid[here, 1 : rows + 1, :, c_mid : 2 * c_mid])
            v1 = dot(vi, p2[...])
            vi = vi.astype(F32)
            total = (
                v3 * par[1, b, 0:1] + v1 * par[1, b, 1:2] + vi * par[1, b, 2:3] + par[1, b, 3:4]
            )
            m = mask_at(t)
            gate = sigmoid(total)
            down = m * flat(wide_cot[...]) * (gate * (1.0 + total * (1.0 - gate)))
            slope[here] = shaped(down)
            add_to(b, 0, down)
            add_to(b, 1, down * (v3 - par[1, b, 4:5]))
            add_to(b, 2, down * (v1 - par[1, b, 5:6]))
            add_to(b, 3, down * (vi - par[1, b, 6:7]))
            wide_cot[...] = shaped(m * (total * gate))
            for part in range(n):
                lanes = slice(part * z.c_local, (part + 1) * z.c_local)
                cut[part, here] = wide_cot[:, :, 0 : z.cols, lanes].astype(BF16)
            return carry

        lax.fori_loop(0, z.tiles, slope_two, 0)

        def out_copy(k):
            to = plane(k)
            return remote(
                cut.at[to], out_hbm.at[sh], out_sem.at[0, k], out_sem.at[1, sh], (dp, to)
            )

        for k in range(1, n):
            sender.start(out_copy, k)
        out_own = pltpu.make_async_copy(cut.at[sh], out_hbm.at[sh], out_sem.at[1, sh])
        out_own.start()

        exchange(2)

        gains = [0.0, 0.0, 0.0]
        shifts = 0.0
        for b in range(MICRO):
            pixels = par[0, b, 7:8]
            slopes = totals[2, b * 8 : b * 8 + 1]
            shifts = shifts + slopes
            for i in range(3):
                rstd = par[1, b, 7 + i : 8 + i]
                cross = totals[2, b * 8 + 1 + i : b * 8 + 2 + i] * rstd
                gains[i] = gains[i] + cross
                scale = par[1, b, i : i + 1]
                tilt = -scale * rstd * cross / pixels
                par[2, b, 3 * i : 3 * i + 1] = scale
                par[2, b, 3 * i + 1 : 3 * i + 2] = tilt
                par[2, b, 3 * i + 2 : 3 * i + 3] = (
                    -scale * slopes / pixels - tilt * par[1, b, 4 + i : 5 + i]
                )
        for i in range(3):
            small[4 + i : 5 + i] = gains[i]
            small[7 + i : 8 + i] = shifts

        rims_back = send_rims(dz3, dz_sem)

        def make_dz(t, carry):
            here = images_at(t)
            b = t // per_batch
            m = mask_at(t)
            down = flat(slope[here])
            value = down * par[2, b, 0:1] + m * (flat(z3b[here]) * par[2, b, 1:2] + par[2, b, 2:3])
            put_three(dz3, here, 1, rows, value)
            v1 = dot(flat(hid[here, 1 : rows + 1, :, c_mid : 2 * c_mid]), p2[...])
            value = down * par[2, b, 3:4] + m * (v1 * par[2, b, 4:5] + par[2, b, 5:6])
            dz1[here] = shaped(value.astype(BF16))
            return carry

        for b in range(MICRO):
            lax.fori_loop(b * per_batch, (b + 1) * per_batch, make_dz, 0)
            start_rims(rims_back, b)

        def put_two(t, value):
            for part in range(n):
                start = (t // z.half * n + part) * z.piece_two + t % z.half * z.c_pad
                wide[start : start + z.c_local] = value[
                    part * z.c_local : (part + 1) * z.c_local
                ].astype(BF16)

        center = pl.ds(c_mid, c_mid)
        for d in range(3):
            value = dot_tn(flat(hid[:, d : d + rows]), flat(dz3[:, 1 : rows + 1, :, center]))
            for c in range(3):
                put_two(3 * d + c, value[c * c_mid : (c + 1) * c_mid])
        put_two(9, dot_tn(flat(hid[:, 1 : rows + 1, :, center]), flat(dz1[...])))
        red_two.start_pair()

        acc[...] = jnp.zeros_like(acc)

        def backward_two(t, carry):
            here = images_at(t)
            b = t // per_batch
            spread_halo(dz3, t)
            total = dot_nt(flat(dz1[here]), p2[...])
            for k in range(3):
                for q in range(3):
                    total = total + dot_nt(
                        flat(dz3[here, k : k + rows, :, q * c_mid : (q + 1) * c_mid]),
                        k2[2 - k, (2 - q) * c_mid : (3 - q) * c_mid],
                    )
            m = mask_at(t)
            vi = flat(hid[here, 1 : rows + 1, :, c_mid : 2 * c_mid]).astype(F32)
            total = total + (
                flat(slope[here]) * par[2, b, 6:7] + m * (vi * par[2, b, 7:8] + par[2, b, 8:9])
            )
            total = total.astype(BF16).astype(F32)
            summed = first_sum(here, b)
            gate = sigmoid(summed)
            down = m * total * (gate * (1.0 + summed * (1.0 - gate)))
            slope[here] = shaped(down)
            add_to(b, 0, down)
            add_to(b, 1, down * (flat(z3a[here]) - par[0, b, 3:4]))
            add_to(b, 2, down * (flat(z1a[here]) - par[0, b, 4:5]))
            return carry

        for b in range(MICRO):
            take_rims(rims_back, b)
            lax.fori_loop(b * per_batch, (b + 1) * per_batch, backward_two, 0)
        red_two.start_plane()
        exchange(3)
        close_rims(rims_back)
        for k in range(1, n):
            part = plane(k)
            remote(
                cut.at[part], out_hbm.at[part], out_sem.at[0, k], out_sem.at[1, part], (dp, part)
            ).wait_recv()
        out_own.wait()

    pl.run_scoped(
        second_part,
        pltpu.VMEM((images, rows + 2, KEPT, 3 * c_mid), BF16),
        pltpu.VMEM((3, 3 * c_mid, c_mid), BF16),
        pltpu.VMEM((c_mid, c_mid), BF16),
        pltpu.VMEM((images, rows, KEPT, c_mid), F32),
        pltpu.VMEM((images, rows + 2, KEPT, 3 * c_mid), BF16),
        pltpu.VMEM((images, rows, KEPT, c_mid), BF16),
        pltpu.VMEM((tile, rows, KEPT, c_mid), F32),
    )

    def third_part(dz3, dz1, paired, staged):
        gains = [0.0, 0.0]
        shifts = 0.0
        for b in range(MICRO):
            pixels = par[0, b, 7:8]
            slopes = totals[3, b * 8 : b * 8 + 1]
            shifts = shifts + slopes
            for i in range(2):
                rstd = par[0, b, 5 + i : 6 + i]
                cross = totals[3, b * 8 + 1 + i : b * 8 + 2 + i] * rstd
                gains[i] = gains[i] + cross
                scale = par[0, b, i : i + 1]
                tilt = -scale * rstd * cross / pixels
                par[3, b, 3 * i : 3 * i + 1] = scale
                par[3, b, 3 * i + 1 : 3 * i + 2] = tilt
                par[3, b, 3 * i + 2 : 3 * i + 3] = (
                    -scale * slopes / pixels - tilt * par[0, b, 3 + i : 4 + i]
                )
        for i in range(2):
            small[i : i + 1] = gains[i]
            small[2 + i : 3 + i] = shifts
        small[10:16] = jnp.zeros((6, c_mid), F32)

        def make_dz(t, carry):
            here = images_at(t)
            b = t // per_batch
            m = mask_at(t)
            down = flat(slope[here])
            value = down * par[3, b, 0:1] + m * (flat(z3a[here]) * par[3, b, 1:2] + par[3, b, 2:3])
            after = pltpu.roll(value, value.shape[0] - 1, 0)
            dz3[here, 0:rows, :, 0:c_mid] = shaped(value.astype(BF16))
            dz3[here, 0:rows, :, c_mid : 2 * c_mid] = shaped(after.astype(BF16))
            value = down * par[3, b, 3:4] + m * (flat(z1a[here]) * par[3, b, 4:5] + par[3, b, 5:6])
            dz1[here] = shaped(value.astype(BF16))
            return carry

        lax.fori_loop(0, z.tiles, make_dz, 0)
        rim = remote(
            dz3.at[:, 0, :, pl.ds(0, c_mid)], halo.at[1], e_sem.at[0], e_sem.at[1], above
        )
        pl.when(has_above)(rim.start)

        def put_one(base, value):
            g_one[base : base + value.shape[0]] = value.astype(BF16)

        own = flat(dz3[:, 0:rows, :, 0:c_mid])
        for d in range(3):
            if d == 1:
                side = flat(even_win[...])
            else:
                side = flat(odd_win[:, d // 2 : d // 2 + rows])
            value = dot_tn(side, own)
            base = 3 * d * c_in
            put_one(base + c_in, value[0:192])
            put_one(base + 128, value[192:256])
            put_one(base, value[256:384])
            put_one(base + 2 * c_in, value[384:576])
        put_one(9 * c_in, dot_tn(flat(even_win[:, :, :, 0:256]), flat(dz1[...]))[0:192])
        if g_one.shape[0] > 10 * c_in:
            g_one[10 * c_in :] = jnp.zeros((g_one.shape[0] - 10 * c_in, c_mid), BF16)
        red_one.start_pair()
        red_two.start_deep()
        pl.when(has_below)(rim.wait_recv)

        def spread(t, carry):
            here = images_at(t)
            value = flat(halo[1, here]).astype(F32)
            after = pltpu.roll(value, value.shape[0] - 1, 0)
            dz3[here, rows, :, 0:c_mid] = value.astype(BF16).reshape(tile, KEPT, c_mid)
            dz3[here, rows, :, c_mid : 2 * c_mid] = after.astype(BF16).reshape(tile, KEPT, c_mid)
            return carry

        lax.fori_loop(0, z.tiles, spread, 0)
        red_one.start_plane()

        some = staged.shape[1]
        steps = images // some

        def staged_copy(i, slot):
            return pltpu.make_async_copy(
                staged.at[slot],
                grad_in_hbm.at[pl.ds(i * some, some)],
                gi_sem.at[slot],
            )

        def input_grad(i, carry):
            here = pl.ds(i * some, some)
            slot = lax.rem(i, 2)
            lane = (slice(0, c_mid), slice(c_mid, 2 * c_mid))
            here_c = flat(dz3[here, 0:rows, :, lane[0]])
            here_next = flat(dz3[here, 0:rows, :, lane[1]])
            next_c = flat(dz3[here, 1 : rows + 1, :, lane[0]])
            next_next = flat(dz3[here, 1 : rows + 1, :, lane[1]])
            value = [
                [
                    dot_nt(here_c, k1_own[1, 1]) + dot_nt(flat(dz1[here]), p1_win[0:192]),
                    dot_nt(here_c, k1_own[1, 2]) + dot_nt(here_next, k1_own[1, 0]),
                ],
                [
                    dot_nt(here_c, k1_own[2, 1]) + dot_nt(next_c, k1_own[0, 1]),
                    dot_nt(here_c, k1_own[2, 2])
                    + dot_nt(here_next, k1_own[2, 0])
                    + dot_nt(next_c, k1_own[0, 2])
                    + dot_nt(next_next, k1_own[0, 0]),
                ],
            ]

            @pl.when(i >= 2)
            def _():
                staged_copy(i, slot).wait()

            for r in range(2):
                for c in range(2):
                    both = value[r][c]
                    paired[0, :, pl.ds(c, KEPT, stride=2), :] = both[:, 0:128].reshape(
                        some * rows, KEPT, 128
                    )
                    paired[1, :, pl.ds(c, KEPT, stride=2), 0:64] = both[:, 128:192].reshape(
                        some * rows, KEPT, 64
                    )
                shape = (some, rows, z.in_cols, -1)
                staged[slot, :, :, r, :, 0:128] = paired[0, :, 0 : z.in_cols, :].reshape(shape)
                staged[slot, :, :, r, :, 128:192] = paired[1, :, 0 : z.in_cols, 0:64].reshape(shape)
            staged_copy(i, slot).start()
            return carry

        lax.fori_loop(0, steps // 2, input_grad, 0)
        red_two.start_back()
        red_one.start_deep()
        lax.fori_loop(steps // 2, steps, input_grad, 0)
        for i in range(max(0, steps - 2), steps):
            staged_copy(i, i % 2).wait()
        pl.when(has_above)(rim.wait_send)

    some = max(1, min(images // 2, 256 // (rows * KEPT)))
    pl.run_scoped(
        third_part,
        pltpu.VMEM((images, rows + 1, KEPT, 2 * c_mid), BF16),
        pltpu.VMEM((images, rows, KEPT, c_mid), BF16),
        pltpu.VMEM((2, some * rows, 32, 128), F32),
        pltpu.VMEM((2, some, rows, 2, z.in_cols, c_in), F32),
    )

    red_two.finish_back()
    two_at = grad_two_hbm.at[core]
    two_own = pltpu.make_async_copy(red_two.r4, two_at, ar_two.at[8, 0])
    two_own.start()
    two_pair = remote(red_two.r4, two_at, ar_two.at[9, 0], ar_two.at[10, 0], sibling)
    if pair == 2:
        two_pair.start()
    red_one.start_back()
    red_one.finish_back()

    def one_at(half, part):
        return grad_one_hbm.at[half, part]

    one_own = pltpu.make_async_copy(red_one.r4, one_at(core, sh), ar_one.at[8, 0])
    one_own.start()

    def one_pair_copy():
        return remote(
            red_one.r4, one_at(core, sh), ar_one.at[12, 0], ar_one.at[13, sh], sibling
        )

    def one_plane_copy(k):
        return remote(
            red_one.r4, one_at(core, sh), ar_one.at[9, k], ar_one.at[10, sh], (dp, plane(k))
        )

    def one_pass_copy(k):
        part = plane(k)
        at = one_at(core, part)
        return remote(at, at, ar_one.at[11, k], ar_one.at[13, part], sibling)

    if pair == 2:
        sender.start(one_pair_copy)
    for k in range(1, n):
        sender.start(one_plane_copy, k)
    for k in range(1, n):
        part = plane(k)
        at = one_at(core, part)
        remote(at, at, ar_one.at[9, k], ar_one.at[10, part], (dp, part)).wait_recv()
        if pair == 2:
            sender.start(one_pass_copy, k)
    if pair == 2:
        for k in range(n):
            part = plane(k)
            at = one_at(1 - core, part)
            remote(at, at, ar_one.at[11, k], ar_one.at[13, part], sibling).wait_recv()
        two_pair.wait_send()
        remote(
            red_two.r4, grad_two_hbm.at[1 - core], ar_two.at[9, 0], ar_two.at[10, 0], sibling
        ).wait_recv()
    two_own.wait()
    one_own.wait()
    sender.finish()


def build(mesh):
    def shards(
        x_input,
        image_counts,
        kernel_one,
        point_one,
        block_one_norm_gains,
        block_one_norm_shifts,
        kernel_two,
        point_two,
        block_two_norm_gains,
        shifts_two,
        cotangent,
    ):
        z = Sizes.__new__(Sizes)
        whole_x = jax.ShapeDtypeStruct(
            (
                x_input.shape[0] * mesh.shape["dp"],
                x_input.shape[1] * mesh.shape["shard"],
                *x_input.shape[2:],
            ),
            x_input.dtype,
        )
        z.__init__(mesh, whole_x, cotangent, point_one)
        n, pair, depth = z.parts, z.pair, z.depth
        dp, sh = lax.axis_index("dp"), lax.axis_index("shard")
        norm_one = jnp.concatenate(
            [block_one_norm_gains, block_one_norm_shifts, jnp.zeros((4, z.c_mid), F32)]
        )
        norm_two = jnp.concatenate(
            [block_two_norm_gains, shifts_two, jnp.zeros((2, z.c_local), F32)]
        )
        lane = jnp.arange(z.c_mid) // z.c_local
        norm_two = jnp.where((lane == sh) & (dp == 0), jnp.tile(norm_two, (1, n)), 0.0)
        if z.c_pad != z.c_local:
            more = z.c_pad - z.c_local
            kernel_two = jnp.pad(kernel_two, ((0, 0), (0, 0), (0, more), (0, 0)))
            point_two = jnp.pad(point_two, ((0, more), (0, 0)))

        vmem = pl.BlockSpec(memory_space=pltpu.VMEM)
        anywhere = pl.BlockSpec(memory_space=pl.ANY)
        image_rows = (z.images, z.rows, KEPT)
        dma = pltpu.SemaphoreType.DMA
        outs = pl.pallas_call(
            functools.partial(kernel, z),
            out_shape=(
                jax.ShapeDtypeStruct((n, z.images, z.rows, z.cols, z.c_local), BF16),
                jax.ShapeDtypeStruct((z.images, z.rows, 2, z.in_cols, z.c_in), F32),
                jax.ShapeDtypeStruct((pair, n, depth, z.sub_one, z.c_mid), BF16),
                jax.ShapeDtypeStruct((pair, depth, z.sub_two, z.c_mid), BF16),
                jax.ShapeDtypeStruct((16, z.c_mid), F32),
            ),
            in_specs=[
                pl.BlockSpec(memory_space=pltpu.SMEM),
                anywhere,
                anywhere,
                anywhere,
                vmem,
                anywhere,
                anywhere,
                vmem,
                anywhere,
            ],
            out_specs=(anywhere, anywhere, anywhere, anywhere, vmem),
            scratch_shapes=[
                pltpu.VMEM((z.images, z.rows + 1, KEPT, 640), BF16),
                pltpu.VMEM((*image_rows, 640), BF16),
                pltpu.VMEM((3, 640, z.c_mid), BF16),
                pltpu.VMEM((3, 3, z.c_in, z.c_mid), BF16),
                pltpu.VMEM((256, z.c_mid), BF16),
                pltpu.VMEM((*image_rows, z.c_mid), F32),
                pltpu.VMEM((*image_rows, z.c_mid), F32),
                pltpu.VMEM((z.images, z.in_cols, z.c_in), BF16),
                pltpu.VMEM((2, z.images, KEPT, z.c_mid), BF16),
                pltpu.VMEM((pair * n * z.piece_two, z.c_mid), BF16),
                pltpu.VMEM((n, z.images, z.rows, z.cols, z.c_local), BF16),
                pltpu.VMEM((*image_rows, z.c_mid), F32),
                pltpu.VMEM((z.rows, KEPT, 128), F32),
                pltpu.VMEM((MICRO, 8, 8, z.c_mid), F32),
                pltpu.VMEM((4, MICRO, 16, z.c_mid), F32),
                pltpu.VMEM((4, PAYLOAD, z.c_mid), F32),
                pltpu.VMEM((4, pair * n, PAYLOAD, z.c_mid), F32),
                pltpu.VMEM((4, depth, PAYLOAD, z.c_mid), F32),
                pltpu.VMEM((4, PAYLOAD, z.c_mid), F32),
                pltpu.VMEM((pair * n * z.piece_one, z.c_mid), BF16),
                pltpu.VMEM((n, z.piece_one, z.c_mid), BF16),
                pltpu.VMEM((depth, z.sub_one, z.c_mid), BF16),
                pltpu.VMEM((depth, z.sub_one, z.c_mid), BF16),
                pltpu.VMEM((depth, z.sub_one, z.c_mid), BF16),
                pltpu.VMEM((n * max(z.piece_one, z.piece_two), z.c_mid), BF16),
                pltpu.VMEM((n, z.piece_two, z.c_mid), BF16),
                pltpu.VMEM((depth, z.sub_two, z.c_mid), BF16),
                pltpu.VMEM((depth, z.sub_two, z.c_mid), BF16),
                pltpu.VMEM((depth, z.sub_two, z.c_mid), BF16),
                dma((24,)),
                dma((2,)),
                dma((4, MICRO)),
                dma((4, MICRO)),
                dma((2,)),
                dma((2, n)),
                dma((2, n)),
                dma((2, n)),
                dma((2, n)),
                dma((4, pair * n)),
                dma((4, pair * n)),
                dma((4, depth)),
                dma((4, depth)),
                dma((14, max(n, depth))),
                dma((14, max(n, depth))),
                dma((max(4, z.images // 8),)),
            ],
            compiler_params=pltpu.CompilerParams(
                collective_id=0, has_side_effects=True, vmem_limit_bytes=63 * 2**20
            ),
        )(
            image_counts,
            x_input,
            kernel_one,
            point_one,
            norm_one,
            kernel_two,
            point_two,
            norm_two,
            cotangent,
        )
        block_out, grad_input, grad_one, grad_two, small = outs
        block_out = (
            block_out.transpose(1, 0, 2, 3, 4)
            .reshape(z.images, n * z.rows, z.cols, z.c_local)
            .astype(F32)
        )
        grad_input = grad_input.reshape(x_input.shape)
        grad_one = grad_one.reshape(-1, z.c_mid)
        grad_kernel_one = grad_one[: 9 * z.c_in].astype(F32).reshape(3, 3, z.c_in, z.c_mid)
        grad_point_one = grad_one[9 * z.c_in : 10 * z.c_in].astype(F32)
        grad_two = grad_two.reshape(pair, -1, z.c_mid)[:, : z.half * z.c_pad]
        grad_two = grad_two.reshape(pair * z.half, z.c_pad, z.c_mid)[:, : z.c_local].astype(F32)
        grad_kernel_two = grad_two[:9].reshape(3, 3, z.c_local, z.c_mid)
        mine = lax.dynamic_slice(small, (0, sh * z.c_local), (16, z.c_local))
        return (
            block_out,
            grad_input,
            grad_kernel_one,
            grad_point_one,
            small[0:2],
            small[2:4],
            grad_kernel_two,
            grad_two[9],
            mine[4:7],
            mine[7:10],
        )

    return shards


def solution(mesh):
    placed = (
        P("dp", "shard", None, None),
        P("dp"),
        P(),
        P(),
        P(),
        P(),
        P(None, None, "shard", None),
        P("shard", None),
        P(None, "shard"),
        P(None, "shard"),
        P("dp", None, None, "shard"),
    )
    return jax.shard_map(
        build(mesh),
        mesh=mesh,
        in_specs=placed,
        out_specs=(
            P("dp", None, None, "shard"),
            P("dp", "shard", None, None),
            P(),
            P(),
            P(),
            P(),
            P(None, None, "shard", None),
            P("shard", None),
            P(None, "shard"),
            P(None, "shard"),
        ),
        check_vma=False,
    )
```

```python
import functools

import jax
import jax.numpy as jnp
from jax import lax
from jax.experimental import pallas as pl
from jax.experimental.pallas import tpu as pltpu
from jax.sharding import PartitionSpec as P

MICRO = 2
EPSILON = 1e-05
KEPT = 16
PAYLOAD = 16
MESH = pl.DeviceIdType.MESH
BF16 = jnp.bfloat16
F32 = jnp.float32


def up_to(value, step):
    return (value + step - 1) // step * step


def flat(value):
    return value.reshape(-1, value.shape[-1])


def dot(a, b):
    return jnp.dot(a, b, preferred_element_type=F32)


def dot_nt(a, b):
    return lax.dot_general(a, b, (((1,), (1,)), ((), ())), preferred_element_type=F32)


def dot_tn(a, b):
    return lax.dot_general(a, b, (((0,), (0,)), ((), ())), preferred_element_type=F32)


def eight(value):
    rows, lanes = value.shape
    return jnp.sum(value.reshape(rows // 8, 8, lanes), axis=0)


def sigmoid(value):
    return 0.5 * jnp.tanh(0.5 * value) + 0.5


class Sizes:
    def __init__(self, mesh, x_input, cotangent, point_one):
        self.groups, self.parts = mesh.shape["dp"], mesh.shape["shard"]
        self.images = x_input.shape[0] // self.groups
        self.in_rows = x_input.shape[1] // self.parts
        self.in_cols, self.c_in = x_input.shape[2:]
        self.rows = self.in_rows // 2
        self.cols = self.in_cols // 2
        self.c_mid = point_one.shape[1]
        self.c_local = self.c_mid // self.parts
        self.c_pad = up_to(self.c_local, 16)
        self.held_rows = up_to(self.in_rows, 8)
        self.out_rows = self.rows * self.parts
        self.batch = self.images // MICRO
        self.tile = max(1, min(self.batch, 512 // (self.rows * KEPT)))
        self.tiles = self.images // self.tile
        self.pair = 2 if self.groups % 2 == 0 else 1
        self.depth = self.groups // self.pair
        self.half = -(-10 // self.pair)
        self.sub_two = up_to(self.half * self.c_pad, 16 * self.depth) // self.depth
        self.piece_two = self.sub_two * self.depth
        real = 10 * self.c_in
        self.sub_one = up_to(real, 16 * self.depth * self.parts * self.pair) // (
            self.depth * self.parts * self.pair
        )
        self.piece_one = self.sub_one * self.depth


class Sender:
    def __init__(self):
        self.open = []

    def start(self, make, *given, when=None):
        if when is None:
            make(*given).start()
        else:
            pl.when(when)(make(*given).start)
        self.open.append((make, given, when))

    def finish(self):
        for make, given, when in self.open:
            if when is None:
                make(*given).wait_send()
            else:
                pl.when(when)(make(*given).wait_send)
        self.open = []


def kernel(
    z,
    count,
    x_hbm,
    k1_hbm,
    p1_hbm,
    gains_one,
    shifts_one,
    k2_hbm,
    p2_hbm,
    gains_two,
    shifts_two,
    cot_hbm,
    out_hbm,
    grad_in_hbm,
    grad_one_hbm,
    grad_two_hbm,
    grad_gains_one,
    grad_shifts_one,
    grad_gains_two,
    grad_shifts_two,
    odd_win,
    even_win,
    k1_win,
    p1_win,
    z3a,
    z1a,
    x_rim,
    halo,
    wide,
    far,
    near,
    slope,
    mask,
    acc,
    par,
    pay,
    slots_a,
    slots_z,
    totals,
    g_one,
    one_r2,
    one_s,
    one_r3,
    one_r4,
    two_r1,
    two_r2,
    two_s,
    two_r3,
    two_r4,
    local_sem,
    x_sem,
    hid_sem,
    dz_sem,
    e_sem,
    ag_sem,
    ag_pair_sem,
    cot_sem,
    out_sem,
    ea_send,
    ea_recv,
    ez_send,
    ez_recv,
    ar_one,
    ar_two,
    gi_sem,
):
    n, pair, depth = z.parts, z.pair, z.depth
    rows, c_mid, c_in, tile = z.rows, z.c_mid, z.c_in, z.tile
    batch, images = z.batch, z.images
    dp = lax.axis_index("dp")
    sh = lax.axis_index("shard")
    core = lax.rem(dp, pair)
    deep = lax.div(dp, pair)
    sibling = (dp + 1 - 2 * core, sh)
    me = core * n + sh
    has_above = sh > 0
    has_below = sh < n - 1
    above, below = (dp, sh - 1), (dp, sh + 1)
    per_batch = batch // tile

    def plane(k):
        return lax.rem(sh + k, n)

    def group_peer(k):
        slot = lax.rem(me + k, pair * n)
        return slot, (dp - core + lax.div(slot, n), lax.rem(slot, n))

    def deep_peer(k):
        other = lax.rem(deep + k, depth)
        return other, (other * pair + core, sh)

    def remote(src, dst, send, recv, device):
        return pltpu.make_async_remote_copy(
            src_ref=src,
            dst_ref=dst,
            send_sem=send,
            recv_sem=recv,
            device_id=device,
            device_id_type=MESH,
        )

    barrier = pltpu.get_barrier_semaphore()
    for k in range(1, pair * n):
        pl.semaphore_signal(barrier, 1, device_id=group_peer(k)[1], device_id_type=MESH)
    for k in range(1, depth):
        pl.semaphore_signal(barrier, 1, device_id=deep_peer(k)[1], device_id_type=MESH)

    own_loads = []

    def load(src, dst):
        copy = pltpu.make_async_copy(src, dst, local_sem.at[len(own_loads)])
        copy.start()
        own_loads.append(copy)

    def wide_rows(half, part, offset, length):
        start = (half * n + part) * z.piece_two + offset
        if not isinstance(start, int):
            start = pl.multiple_of(start, 16)
        return wide.at[pl.ds(start, length)]

    taps = [k2_hbm.at[t // 3, t % 3] for t in range(9)] + [p2_hbm]
    for t in range(10):
        load(taps[t], wide_rows(t // z.half, sh, t % z.half * z.c_pad, z.c_pad))
    n_wide = len(own_loads)
    for d in range(3):
        load(k1_hbm.at[d, 1], k1_win.at[d, pl.ds(0, 192)])
        load(k1_hbm.at[d, 0, pl.ds(128, 64)], k1_win.at[d, pl.ds(192, 64)])
        load(k1_hbm.at[d, 0, pl.ds(0, 128)], k1_win.at[d, pl.ds(256, 128)])
        load(k1_hbm.at[d, 2], k1_win.at[d, pl.ds(384, 192)])
    load(p1_hbm, p1_win.at[pl.ds(0, 192)])

    pl.semaphore_wait(barrier, pair * n - 1 + depth - 1)

    sender = Sender()
    gather = Sender()

    def x_copy(b):
        some = pl.ds(b * batch, batch)
        return remote(
            x_rim.at[some], halo.at[0, some], x_sem.at[0, b], x_sem.at[1, b], below
        )

    row_at = lax.broadcasted_iota(jnp.int32, mask.shape, 0) + sh * rows
    col_at = lax.broadcasted_iota(jnp.int32, mask.shape, 1)
    mask[...] = jnp.where((row_at < z.cols) & (col_at < z.cols), 1.0, 0.0)

    @pl.when(jnp.logical_not(has_above))
    def _():
        halo[0] = jnp.zeros(halo.shape[1:], BF16)

    @pl.when(jnp.logical_not(has_below))
    def _():
        halo[1] = jnp.zeros(halo.shape[1:], BF16)

    for d in range(3):
        k1_win[d, 576:640] = jnp.zeros((64, c_mid), BF16)
    p1_win[192:256] = jnp.zeros((64, c_mid), BF16)

    ag_length = z.half * z.c_pad

    def gather_copy(k):
        own = wide_rows(core, sh, 0, ag_length)
        return remote(own, own, ag_sem.at[0, k], ag_sem.at[1, sh], (dp, plane(k)))

    def three(value):
        return jnp.concatenate([value] * (c_mid // 128), axis=-1)

    def images_at(t):
        return pl.ds(pl.multiple_of(t * tile, tile), tile)

    def kept(first, count_):
        return mask[first : first + count_][None]

    def mask_of(start, size, first=0, count_=rows):
        shape = (size, count_, KEPT, 128)
        image_at = lax.broadcasted_iota(jnp.int32, shape, 0) + start
        return three(flat(jnp.where(image_at < count[0], kept(first, count_), 0.0)))

    def mask_at(t):
        return mask_of(t * tile, tile)

    def pixels_at():
        return three(flat(jnp.broadcast_to(kept(0, rows), (tile, rows, KEPT, 128))))

    def shaped(value, count_=rows):
        return value.reshape(-1, count_, KEPT, value.shape[-1])

    def add_to(batch_at, at, value):
        acc[batch_at, at] = acc[batch_at, at] + eight(value)

    def group_copy(e, b, k):
        slot, device = group_peer(k)
        some = pl.ds(0, PAYLOAD if e + b == 0 else 8)
        return remote(
            pay.at[e, b, some],
            slots_a.at[e, b, me, some],
            ea_send.at[e * MICRO + b, k],
            ea_recv.at[e * MICRO + b, me],
            device,
        )

    def deep_sum(e, b, k):
        other, device = deep_peer(k)
        some = pl.ds(0, PAYLOAD if e + b == 0 else 8)
        own = slots_z.at[e, b, deep, some]
        return remote(
            own, own, ez_send.at[e * MICRO + b, k], ez_recv.at[e * MICRO + b, deep], device
        )

    def exchange_start(e, b):
        pay[e, b, 0:8] = jnp.sum(acc[b], axis=1)
        length = 8
        if e + b == 0:
            length = PAYLOAD
            lane = lax.broadcasted_iota(jnp.int32, (3, c_mid), 1)
            first = sh * z.c_local
            owned = (lane >= first) & (lane < first + z.c_local) & (dp == 0)
            for at, given in ((8, gains_two), (11, shifts_two)):
                spread_out = jnp.concatenate([given[...]] * n, axis=1)
                pay[e, b, at : at + 3] = jnp.where(owned, spread_out, 0.0)
            pay[e, b, 14:16] = jnp.zeros((2, c_mid), F32)
        slots_a[e, b, me, 0:length] = pay[e, b, 0:length]
        for k in range(1, pair * n):
            group_copy(e, b, k).start()
        acc[b] = jnp.zeros(acc.shape[1:], F32)

    def exchange_pass(e, b):
        at = e * MICRO + b
        length = PAYLOAD if e + b == 0 else 8
        some = pl.ds(0, length)
        for k in range(1, pair * n):
            slot, device = group_peer(k)
            remote(
                pay.at[e, b, some],
                slots_a.at[e, b, slot, some],
                ea_send.at[at, k],
                ea_recv.at[at, slot],
                device,
            ).wait_recv()
        total = slots_a[e, b, 0, 0:length]
        for slot in range(1, pair * n):
            total = total + slots_a[e, b, slot, 0:length]
        slots_z[e, b, deep, 0:length] = total
        for k in range(1, depth):
            deep_sum(e, b, k).start()

    def exchange_end(e, b):
        at = e * MICRO + b
        length = PAYLOAD if e + b == 0 else 8
        some = pl.ds(0, length)
        for k in range(1, depth):
            other, device = deep_peer(k)
            there = slots_z.at[e, b, other, some]
            remote(there, there, ez_send.at[at, k], ez_recv.at[at, other], device).wait_recv()
        total = slots_z[e, b, 0, 0:length]
        for other in range(1, depth):
            total = total + slots_z[e, b, other, 0:length]
        totals[e, b, 0:length] = total
        for k in range(1, pair * n):
            group_copy(e, b, k).wait_send()
        for k in range(1, depth):
            deep_sum(e, b, k).wait_send()

    def moments(e, b, at, pixels):
        center = totals[e, b, at : at + 1] / pixels
        square = totals[e, b, at + 1 : at + 2] / pixels
        return center, lax.rsqrt(square - center * center + EPSILON)

    held = z.held_rows
    spread_rows = z.in_cols * held
    wide_rows_x = 4 * KEPT * held // 2
    group = 4

    def windows(even0, even1, odd0, odd1):
        before0, before1 = pltpu.roll(odd0, 1, 0), pltpu.roll(odd1, 1, 0)
        parts = [even0, even1 + pltpu.roll(before1, 64, 1), before0, odd0, odd1]
        return jnp.concatenate([v.astype(BF16) for v in parts], axis=1)

    def cot_copy(k):
        to = plane(k)
        return remote(far.at[to], near.at[sh], cot_sem.at[0, k], cot_sem.at[1, sh], (dp, to))

    def first_part(x_own, cot_own, x_wide):
        loads = []
        step = 8
        for at in range(0, images, step):
            copy = pltpu.make_async_copy(
                x_hbm.at[pl.ds(at, step)], x_own.at[pl.ds(at, step)], gi_sem.at[at // step]
            )
            copy.start()
            loads.append(copy)
        cot_load = pltpu.make_async_copy(cot_hbm, cot_own, gi_sem.at[images // step])
        cot_load.start()
        x_wide[...] = jnp.zeros_like(x_wide)

        def extract(i, carry):
            here = pl.ds(i * group, group)
            for g in range(group):
                value = x_own[i * group + g].astype(F32).reshape(spread_rows, c_in)
                x_wide[0, g, 0:spread_rows] = value[:, 0:128]
                x_wide[1, g, 0:spread_rows, 0:64] = value[:, 128:192]

            def columns(half, odd):
                return flat(
                    jnp.stack(
                        [
                            x_wide[half, g, pl.ds(odd * held + r, KEPT, stride=2 * held), :]
                            for g in range(group)
                            for r in range(z.in_rows)
                        ]
                    )
                )

            even0, even1, odd0, odd1 = columns(0, 0), columns(1, 0), columns(0, 1), columns(1, 1)
            value = windows(even0, even1, odd0, odd1).reshape(group, rows, 2, KEPT, 640)
            even_win[here] = value[:, :, 0]
            odd_win[here, 1 : rows + 1] = value[:, :, 1]
            rim = jnp.concatenate([even0, odd0, even1 + pltpu.roll(odd1, 64, 1)], axis=1)
            rim = rim.reshape(group, z.in_rows, KEPT, 384)[:, z.in_rows - 1]
            x_rim[here] = rim.astype(BF16)
            return carry

        for at in range(0, images, step):
            loads[at // step].wait()
            lax.fori_loop(at // group, (at + step) // group, extract, 0)
            if (at + step) % batch == 0:
                sender.start(x_copy, at // batch, when=has_below)

        for copy in own_loads[:n_wide]:
            copy.wait()
        for k in range(1, n):
            gather.start(gather_copy, k)

        cot_load.wait()
        out_rows = z.out_rows

        def repack(i, carry):
            value = cot_own[i].astype(F32).reshape(z.cols * out_rows, z.c_local)
            x_wide[0, 0, 0 : z.cols * out_rows, 0 : z.c_local] = value
            for to in range(n):
                pieces = [
                    x_wide[0, 0, pl.ds(to * rows + r, KEPT, stride=out_rows), :][:, 0 : z.c_local]
                    for r in range(rows)
                ]
                far[to, i] = jnp.concatenate(pieces, axis=1).astype(BF16)
            return carry

        lax.fori_loop(0, images, repack, 0)

    pl.run_scoped(
        first_part,
        pltpu.VMEM((images, z.in_cols, held, c_in), BF16),
        pltpu.VMEM((images, z.cols, z.out_rows, z.c_local), BF16),
        pltpu.VMEM((2, group, max(wide_rows_x, KEPT * z.out_rows), 128), F32),
    )

    for copy in own_loads[n_wide:]:
        copy.wait()
    acc[...] = jnp.zeros_like(acc)

    def extract_above(i, carry):
        here = pl.ds(i * 8, 8)
        value = flat(halo[0, here]).astype(F32)
        low = lax.broadcasted_iota(jnp.int32, (8 * KEPT, 128), 1) < 64
        mixed = value[:, 256:384]
        even1 = jnp.where(low, mixed, 0.0)
        odd1 = jnp.where(low, pltpu.roll(mixed, 64, 1), 0.0)
        value = windows(value[:, 0:128], even1, value[:, 128:256], odd1)
        odd_win[here, 0] = value.reshape(8, KEPT, 640)
        return carry

    def forward_one(t, carry):
        here = images_at(t)
        b = t // per_batch
        side = flat(even_win[here])
        three_branch = dot(flat(odd_win[here, 0:rows]), k1_win[0])
        three_branch = three_branch + dot(side, k1_win[1])
        three_branch = three_branch + dot(flat(odd_win[here, 1 : rows + 1]), k1_win[2])
        point_branch = dot(side[:, 0:256], p1_win[...])
        z3a[here] = shaped(three_branch)
        z1a[here] = shaped(point_branch)
        m = mask_at(t)
        masked = three_branch * m
        add_to(b, 0, masked)
        add_to(b, 1, masked * three_branch)
        masked = point_branch * m
        add_to(b, 2, masked)
        add_to(b, 3, masked * point_branch)
        add_to(b, 4, m)
        return carry

    near[sh] = far[sh]
    for b in range(MICRO):
        pl.when(has_above)(x_copy(b).wait_recv)
        lax.fori_loop(b * batch // 8, (b + 1) * batch // 8, extract_above, 0)
        for t in range(per_batch):
            forward_one(b * per_batch + t, 0)
            if b and t == 0:
                exchange_pass(0, 0)
        exchange_start(0, b)
        if b == 0:
            for k in range(1, n):
                cot_copy(k).start()

    def pass_copy(k):
        part = plane(k)
        piece = wide_rows(core, part, 0, ag_length)
        return remote(piece, piece, ag_pair_sem.at[0, k], ag_pair_sem.at[1, part], sibling)

    for k in range(1, n):
        part = plane(k)
        piece = wide_rows(core, part, 0, ag_length)
        remote(piece, piece, ag_sem.at[0, k], ag_sem.at[1, part], (dp, part)).wait_recv()
        if pair == 2:
            gather.start(pass_copy, k)

    def norm_one(b):
        pixels = totals[0, b, 4:5]
        center_three, rstd_three = moments(0, b, 0, pixels)
        center_point, rstd_point = moments(0, b, 2, pixels)
        scale_three = gains_one[0:1] * rstd_three
        scale_point = gains_one[1:2] * rstd_point
        par[0, b, 0:1] = scale_three
        par[0, b, 1:2] = scale_point
        par[0, b, 2:3] = (shifts_one[0:1] - center_three * scale_three) + (
            shifts_one[1:2] - center_point * scale_point
        )
        par[0, b, 3:4] = center_three
        par[0, b, 4:5] = center_point
        par[0, b, 5:6] = rstd_three
        par[0, b, 6:7] = rstd_point
        par[0, b, 7:8] = pixels

    def first_sum(here, b, first=0, count_=rows):
        some = slice(first, first + count_)
        return (
            flat(z3a[here, some]) * par[0, b, 0:1]
            + flat(z1a[here, some]) * par[0, b, 1:2]
            + par[0, b, 2:3]
        )

    def put_three(target, here, at, count_, value):
        length = value.shape[0]
        shape = (-1, count_, KEPT, c_mid)
        before = pltpu.roll(value, 1, 0)
        after = pltpu.roll(value, length - 1, 0)
        target[here, at : at + count_, :, 0:c_mid] = before.astype(BF16).reshape(shape)
        target[here, at : at + count_, :, c_mid : 2 * c_mid] = value.astype(BF16).reshape(shape)
        target[here, at : at + count_, :, 2 * c_mid : 3 * c_mid] = after.astype(BF16).reshape(shape)

    def send_rims(source, sems):
        copies = []
        center = pl.ds(c_mid, c_mid)
        for b in range(MICRO):
            some = pl.ds(b * batch, batch)
            copies.append(
                (
                    remote(
                        source.at[some, 1, :, center],
                        halo.at[1, some],
                        sems.at[0, b],
                        sems.at[1, b],
                        above,
                    ),
                    remote(
                        source.at[some, rows, :, center],
                        halo.at[0, some],
                        sems.at[2, b],
                        sems.at[3, b],
                        below,
                    ),
                )
            )
        return copies

    def spread_halo(target, side, b):
        def one(i, carry):
            here = pl.ds(b * batch + i * 8, 8)
            value = flat(halo[side, here]).astype(F32)
            put_three(target, here, 0 if side == 0 else rows + 1, 1, value)
            return carry

        lax.fori_loop(0, batch // 8, one, 0)

    def start_rims(copies, b):
        pl.when(has_above)(copies[b][0].start)
        pl.when(has_below)(copies[b][1].start)

    def take_rims(copies, b):
        pl.when(has_below)(copies[b][0].wait_recv)
        pl.when(has_above)(copies[b][1].wait_recv)

    def close_rims(copies):
        for b in range(MICRO):
            pl.when(has_above)(copies[b][0].wait_send)
            pl.when(has_below)(copies[b][1].wait_send)

    inner = (1, rows - 2) if rows > 2 else None
    outer = sorted({0, rows - 1})

    class Reduce:
        def __init__(self, g, r1, r2, s, r3, r4, sems, piece, sub):
            self.g, self.r1, self.r2, self.s, self.r3, self.r4 = g, r1, r2, s, r3, r4
            self.sems, self.piece, self.sub = sems, piece, sub

        def at(self, half, part):
            return pl.ds(pl.multiple_of((half * n + part) * self.piece, 16), self.piece)

        def pair_copy(self):
            start = pl.multiple_of((1 - core) * n * self.piece, 16)
            return remote(
                self.g.at[pl.ds(start, n * self.piece)],
                self.r1,
                self.sems.at[0, 0],
                self.sems.at[1, 0],
                sibling,
            )

        def start_pair(self):
            if pair == 2:
                sender.start(self.pair_copy)

        def start_plane(self):
            if pair == 2:
                self.pair_copy().wait_recv()

                def join(part, carry):
                    at = self.at(core, part)
                    arrived = self.r1[
                        pl.ds(pl.multiple_of(part * self.piece, 16), self.piece)
                    ]
                    self.g[at] = (self.g[at].astype(F32) + arrived.astype(F32)).astype(BF16)
                    return carry

                lax.fori_loop(0, n, join, 0)
            self.r2[sh] = self.g[self.at(core, sh)]

            def plane_copy(k):
                to = plane(k)
                return remote(
                    self.g.at[self.at(core, to)],
                    self.r2.at[sh],
                    self.sems.at[2, k],
                    self.sems.at[3, sh],
                    (dp, to),
                )

            for k in range(1, n):
                sender.start(plane_copy, k)

        def start_deep(self):
            for k in range(1, n):
                part = plane(k)
                remote(
                    self.r2.at[part],
                    self.r2.at[part],
                    self.sems.at[2, k],
                    self.sems.at[3, part],
                    (dp, part),
                ).wait_recv()
            total = self.r2[0].astype(F32)
            for part in range(1, n):
                total = total + self.r2[part].astype(F32)
            self.s[...] = total.astype(BF16).reshape(self.s.shape)
            self.r3[deep] = self.s[deep]

            def deep_copy(k):
                other, device = deep_peer(k)
                return remote(
                    self.s.at[other],
                    self.r3.at[deep],
                    self.sems.at[4, k],
                    self.sems.at[5, deep],
                    device,
                )

            for k in range(1, depth):
                sender.start(deep_copy, k)

        def start_back(self):
            for k in range(1, depth):
                other, device = deep_peer(k)
                remote(
                    self.r3.at[other],
                    self.r3.at[other],
                    self.sems.at[4, k],
                    self.sems.at[5, other],
                    device,
                ).wait_recv()
            total = self.r3[0].astype(F32)
            for other in range(1, depth):
                total = total + self.r3[other].astype(F32)
            self.r4[deep] = total.astype(BF16)

            def back_copy(k):
                own = self.r4.at[deep]
                return remote(
                    own, own, self.sems.at[6, k], self.sems.at[7, deep], deep_peer(k)[1]
                )

            for k in range(1, depth):
                sender.start(back_copy, k)

        def finish_back(self):
            for k in range(1, depth):
                other, device = deep_peer(k)
                remote(
                    self.r4.at[other],
                    self.r4.at[other],
                    self.sems.at[6, k],
                    self.sems.at[7, other],
                    device,
                ).wait_recv()

    red_two = Reduce(
        wide, two_r1.at[pl.ds(0, n * z.piece_two)], two_r2, two_s, two_r3, two_r4, ar_two, z.piece_two, z.sub_two
    )
    red_one = Reduce(
        g_one, two_r1.at[pl.ds(0, n * z.piece_one)], one_r2, one_s, one_r3, one_r4, ar_one, z.piece_one, z.sub_one
    )

    def out_copy(b, k):
        to = plane(k)
        some = pl.ds(b * batch, batch)
        return remote(
            near.at[to, some],
            far.at[sh, some],
            out_sem.at[0, b * n + k],
            out_sem.at[1, b * n + sh],
            (dp, to),
        )

    def second_part(hid, k2, p2, z3b, dz3, dz1):
        rims = send_rims(hid, hid_sem)

        def make_hidden(t, carry):
            here = images_at(t)
            b = t // per_batch
            total = first_sum(here, b)
            put_three(hid, here, 1, rows, pixels_at() * (total * sigmoid(total)))
            return carry

        exchange_end(0, 0)
        norm_one(0)
        lax.fori_loop(0, per_batch, make_hidden, 0)
        start_rims(rims, 0)
        exchange_pass(0, 1)

        if pair == 2:
            for k in range(1, n):
                part = plane(k)
                piece = wide_rows(1 - core, part, 0, ag_length)
                remote(
                    piece, piece, ag_pair_sem.at[0, k], ag_pair_sem.at[1, part], sibling
                ).wait_recv()
        gather.finish()
        for t in range(10):
            for part in range(n):
                start = (t // z.half * n + part) * z.piece_two + t % z.half * z.c_pad
                value = wide[start : start + z.c_local]
                if t < 9:
                    base = t % 3 * c_mid + part * z.c_local
                    k2[t // 3, base : base + z.c_local] = value
                else:
                    p2[part * z.c_local : (part + 1) * z.c_local] = value

        exchange_end(0, 1)
        norm_one(1)
        lax.fori_loop(per_batch, 2 * per_batch, make_hidden, 0)
        start_rims(rims, 1)

        def forward_two(b, first, count_):
            start = b * batch
            here = pl.ds(start, batch)
            three_branch = dot(flat(hid[here, first : first + count_]), k2[0])
            for d in (1, 2):
                three_branch = three_branch + dot(
                    flat(hid[here, first + d : first + d + count_]), k2[d]
                )
            center = flat(hid[here, first + 1 : first + 1 + count_, :, c_mid : 2 * c_mid])
            point_branch = dot(center, p2[...])
            z3b[here, first : first + count_] = shaped(three_branch, count_)
            m = mask_of(start, batch, first, count_)
            masked = three_branch * m
            add_to(b, 0, masked)
            add_to(b, 1, masked * three_branch)
            masked = point_branch * m
            add_to(b, 2, masked)
            add_to(b, 3, masked * point_branch)
            center = center.astype(F32)
            masked = center * m
            add_to(b, 4, masked)
            add_to(b, 5, masked * center)

        if inner:
            for b in range(MICRO):
                forward_two(b, *inner)
        for b in range(MICRO):
            take_rims(rims, b)
            spread_halo(hid, 0, b)
            spread_halo(hid, 1, b)
            for at in outer:
                forward_two(b, at, 1)
                if b and at == 0:
                    exchange_pass(1, 0)
            if b == 0:
                for k in range(1, n):
                    cot_copy(k).wait_send()
            exchange_start(1, b)

        def norm_two(b):
            pixels = par[0, b, 7:8]
            offset = 0.0
            for i in range(3):
                center, rstd = moments(1, b, 2 * i, pixels)
                scale = totals[0, 0, 8 + i : 9 + i] * rstd
                par[1, b, i : i + 1] = scale
                par[1, b, 4 + i : 5 + i] = center
                par[1, b, 7 + i : 8 + i] = rstd
                offset = offset + (totals[0, 0, 11 + i : 12 + i] - center * scale)
            par[1, b, 3:4] = offset

        def slope_two(t, carry):
            here = images_at(t)
            b = t // per_batch
            taken = [near[part, here] for part in range(n)]
            cot = jnp.stack(
                [
                    jnp.concatenate(
                        [v[:, :, r * z.c_local : (r + 1) * z.c_local] for v in taken], axis=2
                    )
                    for r in range(rows)
                ],
                axis=1,
            )
            v3 = flat(z3b[here])
            vi = flat(hid[here, 1 : rows + 1, :, c_mid : 2 * c_mid])
            v1 = dot(vi, p2[...])
            vi = vi.astype(F32)
            total = (
                v3 * par[1, b, 0:1] + v1 * par[1, b, 1:2] + vi * par[1, b, 2:3] + par[1, b, 3:4]
            )
            m = mask_at(t)
            gate = sigmoid(total)
            down = m * flat(cot).astype(F32) * (gate * (1.0 + total * (1.0 - gate)))
            slope[here] = shaped(down)
            add_to(b, 0, down)
            add_to(b, 1, down * (v3 - par[1, b, 4:5]))
            add_to(b, 2, down * (v1 - par[1, b, 5:6]))
            add_to(b, 3, down * (vi - par[1, b, 6:7]))
            out = shaped((m * (total * gate)).astype(BF16))
            for part in range(n):
                lanes = slice(part * z.c_local, (part + 1) * z.c_local)
                near[part, here] = jnp.concatenate(
                    [out[:, r, :, lanes] for r in range(rows)], axis=2
                )
            return carry

        for k in range(1, n):
            part = plane(k)
            remote(
                near.at[part], near.at[part], cot_sem.at[0, k], cot_sem.at[1, part], (dp, part)
            ).wait_recv()
        exchange_pass(1, 1)
        for b in range(MICRO):
            exchange_end(1, b)
            norm_two(b)
            for t in range(per_batch):
                slope_two(b * per_batch + t, 0)
                if b and t == 0:
                    exchange_pass(2, 0)
            exchange_start(2, b)
            for k in range(1, n):
                sender.start(out_copy, b, k)
        far[sh] = near[sh]

        def turn_two(b):
            pixels = par[0, b, 7:8]
            slopes = totals[2, b, 0:1]
            for i in range(3):
                rstd = par[1, b, 7 + i : 8 + i]
                cross = totals[2, b, 1 + i : 2 + i] * rstd
                scale = par[1, b, i : i + 1]
                tilt = -scale * rstd * cross / pixels
                par[2, b, 3 * i : 3 * i + 1] = scale
                par[2, b, 3 * i + 1 : 3 * i + 2] = tilt
                par[2, b, 3 * i + 2 : 3 * i + 3] = (
                    -scale * slopes / pixels - tilt * par[1, b, 4 + i : 5 + i]
                )

        rims_back = send_rims(dz3, dz_sem)

        def make_dz(t, carry):
            here = images_at(t)
            b = t // per_batch
            m = mask_at(t)
            down = flat(slope[here])
            value = down * par[2, b, 0:1] + m * (flat(z3b[here]) * par[2, b, 1:2] + par[2, b, 2:3])
            put_three(dz3, here, 1, rows, value)
            v1 = dot(flat(hid[here, 1 : rows + 1, :, c_mid : 2 * c_mid]), p2[...])
            value = down * par[2, b, 3:4] + m * (v1 * par[2, b, 4:5] + par[2, b, 5:6])
            dz1[here] = shaped(value.astype(BF16))
            return carry

        exchange_end(2, 0)
        turn_two(0)
        lax.fori_loop(0, per_batch, make_dz, 0)
        start_rims(rims_back, 0)
        exchange_pass(2, 1)
        exchange_end(2, 1)
        turn_two(1)
        lax.fori_loop(per_batch, 2 * per_batch, make_dz, 0)
        start_rims(rims_back, 1)

        def mine(value):
            result = jnp.zeros((1, z.c_local), F32)
            for part in range(n):
                here = value[:, part * z.c_local : (part + 1) * z.c_local]
                result = result + jnp.where(sh == part, here, 0.0)
            return result

        shifts = mine(totals[2, 0, 0:1] + totals[2, 1, 0:1])
        for i in range(3):
            cross = [
                totals[2, b, 1 + i : 2 + i] * par[1, b, 7 + i : 8 + i] for b in range(MICRO)
            ]
            grad_gains_two[i : i + 1] = mine(cross[0] + cross[1])
            grad_shifts_two[i : i + 1] = shifts

        def put_two(t, value):
            for part in range(n):
                start = (t // z.half * n + part) * z.piece_two + t % z.half * z.c_pad
                wide[start : start + z.c_local] = value[
                    part * z.c_local : (part + 1) * z.c_local
                ].astype(BF16)

        center = pl.ds(c_mid, c_mid)
        for d in range(3):
            value = dot_tn(flat(hid[:, d : d + rows]), flat(dz3[:, 1 : rows + 1, :, center]))
            for c in range(3):
                put_two(3 * d + c, value[c * c_mid : (c + 1) * c_mid])
        put_two(9, dot_tn(flat(hid[:, 1 : rows + 1, :, center]), flat(dz1[...])))
        red_two.start_pair()

        def backward_two(b, first, count_):
            start = b * batch
            here = pl.ds(start, batch)
            some = slice(first, first + count_)
            total = dot_nt(flat(dz1[here, some]), p2[...])
            for k in range(3):
                for q in range(3):
                    total = total + dot_nt(
                        flat(
                            dz3[here, first + k : first + k + count_, :, q * c_mid : (q + 1) * c_mid]
                        ),
                        k2[2 - k, (2 - q) * c_mid : (3 - q) * c_mid],
                    )
            m = mask_of(start, batch, first, count_)
            vi = flat(hid[here, first + 1 : first + 1 + count_, :, c_mid : 2 * c_mid]).astype(F32)
            total = total + (
                flat(slope[here, some]) * par[2, b, 6:7]
                + m * (vi * par[2, b, 7:8] + par[2, b, 8:9])
            )
            total = total.astype(BF16).astype(F32)
            summed = first_sum(here, b, first, count_)
            gate = sigmoid(summed)
            down = m * total * (gate * (1.0 + summed * (1.0 - gate)))
            slope[here, some] = shaped(down, count_)
            add_to(b, 0, down)
            add_to(b, 1, down * (flat(z3a[here, some]) - par[0, b, 3:4]))
            add_to(b, 2, down * (flat(z1a[here, some]) - par[0, b, 4:5]))

        if inner:
            for b in range(MICRO):
                backward_two(b, *inner)
        red_two.start_plane()
        for b in range(MICRO):
            take_rims(rims_back, b)
            spread_halo(dz3, 0, b)
            spread_halo(dz3, 1, b)
            for at in outer:
                backward_two(b, at, 1)
                if b and at == 0:
                    exchange_pass(3, 0)
            exchange_start(3, b)
        close_rims(rims)
        close_rims(rims_back)
        exchange_pass(3, 1)

    pl.run_scoped(
        second_part,
        pltpu.VMEM((images, rows + 2, KEPT, 3 * c_mid), BF16),
        pltpu.VMEM((3, 3 * c_mid, c_mid), BF16),
        pltpu.VMEM((c_mid, c_mid), BF16),
        pltpu.VMEM((images, rows, KEPT, c_mid), F32),
        pltpu.VMEM((images, rows + 2, KEPT, 3 * c_mid), BF16),
        pltpu.VMEM((images, rows, KEPT, c_mid), BF16),
    )

    def third_part(dz3, dz1, paired, staged, out_own):
        def turn_one(b):
            pixels = par[0, b, 7:8]
            slopes = totals[3, b, 0:1]
            for i in range(2):
                rstd = par[0, b, 5 + i : 6 + i]
                cross = totals[3, b, 1 + i : 2 + i] * rstd
                scale = par[0, b, i : i + 1]
                tilt = -scale * rstd * cross / pixels
                par[3, b, 3 * i : 3 * i + 1] = scale
                par[3, b, 3 * i + 1 : 3 * i + 2] = tilt
                par[3, b, 3 * i + 2 : 3 * i + 3] = (
                    -scale * slopes / pixels - tilt * par[0, b, 3 + i : 4 + i]
                )

        rims = [
            remote(
                dz3.at[pl.ds(b * batch, batch), 0, :, pl.ds(0, c_mid)],
                halo.at[1, pl.ds(b * batch, batch)],
                e_sem.at[0, b],
                e_sem.at[1, b],
                above,
            )
            for b in range(MICRO)
        ]

        def make_dz(t, carry):
            here = images_at(t)
            b = t // per_batch
            m = mask_at(t)
            down = flat(slope[here])
            value = down * par[3, b, 0:1] + m * (flat(z3a[here]) * par[3, b, 1:2] + par[3, b, 2:3])
            after = pltpu.roll(value, value.shape[0] - 1, 0)
            dz3[here, 0:rows, :, 0:c_mid] = shaped(value.astype(BF16))
            dz3[here, 0:rows, :, c_mid : 2 * c_mid] = shaped(after.astype(BF16))
            value = down * par[3, b, 3:4] + m * (flat(z1a[here]) * par[3, b, 4:5] + par[3, b, 5:6])
            dz1[here] = shaped(value.astype(BF16))
            return carry

        for b in range(MICRO):
            exchange_end(3, b)
            turn_one(b)
            lax.fori_loop(b * per_batch, (b + 1) * per_batch, make_dz, 0)
            pl.when(has_above)(rims[b].start)
        shifts = totals[3, 0, 0:1] + totals[3, 1, 0:1]
        for i in range(2):
            cross = [
                totals[3, b, 1 + i : 2 + i] * par[0, b, 5 + i : 6 + i] for b in range(MICRO)
            ]
            grad_gains_one[i : i + 1] = cross[0] + cross[1]
            grad_shifts_one[i : i + 1] = shifts

        def put_one(base, value):
            g_one[base : base + value.shape[0]] = value.astype(BF16)

        own = flat(dz3[:, 0:rows, :, 0:c_mid])
        for d in range(3):
            if d == 1:
                side = flat(even_win[...])
            else:
                side = flat(odd_win[:, d // 2 : d // 2 + rows])
            value = dot_tn(side, own)
            base = 3 * d * c_in
            put_one(base + c_in, value[0:192])
            put_one(base + 128, value[192:256])
            put_one(base, value[256:384])
            put_one(base + 2 * c_in, value[384:576])
        put_one(9 * c_in, dot_tn(flat(even_win[:, :, :, 0:256]), flat(dz1[...]))[0:192])
        if g_one.shape[0] > 10 * c_in:
            g_one[10 * c_in :] = jnp.zeros((g_one.shape[0] - 10 * c_in, c_mid), BF16)
        red_one.start_pair()
        red_two.start_deep()
        for b in range(MICRO):
            pl.when(has_below)(rims[b].wait_recv)

        def spread(t, carry):
            here = images_at(t)
            value = flat(halo[1, here]).astype(F32)
            after = pltpu.roll(value, value.shape[0] - 1, 0)
            dz3[here, rows, :, 0:c_mid] = value.astype(BF16).reshape(tile, KEPT, c_mid)
            dz3[here, rows, :, c_mid : 2 * c_mid] = after.astype(BF16).reshape(tile, KEPT, c_mid)
            return carry

        lax.fori_loop(0, z.tiles, spread, 0)
        red_one.start_plane()

        some = staged.shape[1]
        steps = images // some

        def staged_copy(i, slot):
            return pltpu.make_async_copy(
                staged.at[slot],
                grad_in_hbm.at[pl.ds(i * some, some)],
                gi_sem.at[slot],
            )

        def tap(d, c):
            if c == 0:
                return jnp.concatenate([k1_win[d, 256:384], k1_win[d, 192:256]], axis=0)
            return k1_win[d, 0:192] if c == 1 else k1_win[d, 384:576]

        def input_grad(i, carry):
            here = pl.ds(i * some, some)
            slot = lax.rem(i, 2)
            lane = (slice(0, c_mid), slice(c_mid, 2 * c_mid))
            here_c = flat(dz3[here, 0:rows, :, lane[0]])
            here_next = flat(dz3[here, 0:rows, :, lane[1]])
            next_c = flat(dz3[here, 1 : rows + 1, :, lane[0]])
            next_next = flat(dz3[here, 1 : rows + 1, :, lane[1]])
            value = [
                [
                    dot_nt(here_c, tap(1, 1)) + dot_nt(flat(dz1[here]), p1_win[0:192]),
                    dot_nt(here_c, tap(1, 2)) + dot_nt(here_next, tap(1, 0)),
                ],
                [
                    dot_nt(here_c, tap(2, 1)) + dot_nt(next_c, tap(0, 1)),
                    dot_nt(here_c, tap(2, 2))
                    + dot_nt(here_next, tap(2, 0))
                    + dot_nt(next_c, tap(0, 2))
                    + dot_nt(next_next, tap(0, 0)),
                ],
            ]

            @pl.when(i >= 2)
            def _():
                staged_copy(i, slot).wait()

            for r in range(2):
                for c in range(2):
                    both = value[r][c].reshape(some, rows, KEPT, c_in)
                    for g in range(some):
                        for at in range(rows):
                            place = pl.ds(c * held + 2 * at + r, KEPT, stride=2 * held)
                            paired[0, g, place, :] = both[g, at, :, 0:128]
                            paired[1, g, place, 0:64] = both[g, at, :, 128:192]
            staged[slot, :, :, :, 0:128] = paired[0, :, 0:spread_rows].reshape(
                some, z.in_cols, held, 128
            )
            staged[slot, :, :, :, 128:192] = paired[1, :, 0:spread_rows, 0:64].reshape(
                some, z.in_cols, held, 64
            )
            staged_copy(i, slot).start()
            return carry

        lax.fori_loop(0, steps // 2, input_grad, 0)
        red_two.start_back()
        red_one.start_deep()
        lax.fori_loop(steps // 2, steps, input_grad, 0)
        for b in range(MICRO):
            for k in range(1, n):
                part = plane(k)
                there = far.at[part, pl.ds(b * batch, batch)]
                remote(
                    there, there, out_sem.at[0, b * n + k], out_sem.at[1, b * n + part], (dp, part)
                ).wait_recv()

        def place_out(i, carry):
            for part in range(n):
                value = far[part, i].astype(F32)
                for r in range(rows):
                    place = pl.ds(part * rows + r, KEPT, stride=z.out_rows)
                    paired[0, 0, place, 0 : z.c_local] = value[
                        :, r * z.c_local : (r + 1) * z.c_local
                    ]
            value = paired[0, 0, 0 : z.cols * z.out_rows, 0 : z.c_local]
            out_own[i] = value.reshape(z.cols, z.out_rows, z.c_local).astype(BF16)
            return carry

        lax.fori_loop(0, images, place_out, 0)
        out_write = pltpu.make_async_copy(out_own, out_hbm, gi_sem.at[2])
        out_write.start()
        for i in range(max(0, steps - 2), steps):
            staged_copy(i, i % 2).wait()
        out_write.wait()
        for b in range(MICRO):
            pl.when(has_above)(rims[b].wait_send)

    some = max(1, min(images // 2, 256 // (rows * KEPT)))
    pl.run_scoped(
        third_part,
        pltpu.VMEM((images, rows + 1, KEPT, 2 * c_mid), BF16),
        pltpu.VMEM((images, rows, KEPT, c_mid), BF16),
        pltpu.VMEM((2, some, max(wide_rows_x, KEPT * z.out_rows), 128), F32),
        pltpu.VMEM((2, some, z.in_cols, held, c_in), F32),
        pltpu.VMEM((images, z.cols, z.out_rows, z.c_local), BF16),
    )

    red_two.finish_back()
    two_at = grad_two_hbm.at[core]
    two_own = pltpu.make_async_copy(red_two.r4, two_at, ar_two.at[8, 0])
    two_own.start()
    two_pair = remote(red_two.r4, two_at, ar_two.at[9, 0], ar_two.at[10, 0], sibling)
    if pair == 2:
        two_pair.start()
    red_one.start_back()
    red_one.finish_back()

    def one_at(half, part):
        return grad_one_hbm.at[half, part]

    one_own = pltpu.make_async_copy(red_one.r4, one_at(core, sh), ar_one.at[8, 0])
    one_own.start()

    def one_pair_copy():
        return remote(
            red_one.r4, one_at(core, sh), ar_one.at[12, 0], ar_one.at[13, sh], sibling
        )

    def one_plane_copy(k):
        return remote(
            red_one.r4, one_at(core, sh), ar_one.at[9, k], ar_one.at[10, sh], (dp, plane(k))
        )

    def one_pass_copy(k):
        part = plane(k)
        at = one_at(core, part)
        return remote(at, at, ar_one.at[11, k], ar_one.at[13, part], sibling)

    if pair == 2:
        sender.start(one_pair_copy)
    for k in range(1, n):
        sender.start(one_plane_copy, k)
    for k in range(1, n):
        part = plane(k)
        at = one_at(core, part)
        remote(at, at, ar_one.at[9, k], ar_one.at[10, part], (dp, part)).wait_recv()
        if pair == 2:
            sender.start(one_pass_copy, k)
    if pair == 2:
        for k in range(n):
            part = plane(k)
            at = one_at(1 - core, part)
            remote(at, at, ar_one.at[11, k], ar_one.at[13, part], sibling).wait_recv()
        two_pair.wait_send()
        remote(
            red_two.r4, grad_two_hbm.at[1 - core], ar_two.at[9, 0], ar_two.at[10, 0], sibling
        ).wait_recv()
    two_own.wait()
    one_own.wait()
    sender.finish()


def build(mesh):
    def shards(
        x_input,
        image_counts,
        kernel_one,
        point_one,
        block_one_norm_gains,
        block_one_norm_shifts,
        kernel_two,
        point_two,
        block_two_norm_gains,
        shifts_two,
        cotangent,
    ):
        z = Sizes.__new__(Sizes)
        whole_x = jax.ShapeDtypeStruct(
            (
                x_input.shape[0] * mesh.shape["dp"],
                x_input.shape[1] * mesh.shape["shard"],
                *x_input.shape[2:],
            ),
            x_input.dtype,
        )
        z.__init__(mesh, whole_x, cotangent, point_one)
        n, pair, depth = z.parts, z.pair, z.depth
        x_turned = x_input.transpose(0, 2, 1, 3)
        if z.held_rows != z.in_rows:
            more = z.held_rows - z.in_rows
            x_turned = jnp.pad(x_turned, ((0, 0), (0, 0), (0, more), (0, 0)))
        if z.c_pad != z.c_local:
            more = z.c_pad - z.c_local
            kernel_two = jnp.pad(kernel_two, ((0, 0), (0, 0), (0, more), (0, 0)))
            point_two = jnp.pad(point_two, ((0, more), (0, 0)))

        vmem = pl.BlockSpec(memory_space=pltpu.VMEM)
        anywhere = pl.BlockSpec(memory_space=pl.ANY)
        image_rows = (z.images, z.rows, KEPT)
        dma = pltpu.SemaphoreType.DMA
        outs = pl.pallas_call(
            functools.partial(kernel, z),
            out_shape=(
                jax.ShapeDtypeStruct((z.images, z.cols, z.out_rows, z.c_local), BF16),
                jax.ShapeDtypeStruct((z.images, z.in_cols, z.held_rows, z.c_in), F32),
                jax.ShapeDtypeStruct((pair, n, depth, z.sub_one, z.c_mid), BF16),
                jax.ShapeDtypeStruct((pair, depth, z.sub_two, z.c_mid), BF16),
                jax.ShapeDtypeStruct((2, z.c_mid), F32),
                jax.ShapeDtypeStruct((2, z.c_mid), F32),
                jax.ShapeDtypeStruct((3, z.c_local), F32),
                jax.ShapeDtypeStruct((3, z.c_local), F32),
            ),
            in_specs=[
                pl.BlockSpec(memory_space=pltpu.SMEM),
                anywhere,
                anywhere,
                anywhere,
                vmem,
                vmem,
                anywhere,
                anywhere,
                vmem,
                vmem,
                anywhere,
            ],
            out_specs=(anywhere, anywhere, anywhere, anywhere, vmem, vmem, vmem, vmem),
            scratch_shapes=[
                pltpu.VMEM((z.images, z.rows + 1, KEPT, 640), BF16),
                pltpu.VMEM((*image_rows, 640), BF16),
                pltpu.VMEM((3, 640, z.c_mid), BF16),
                pltpu.VMEM((256, z.c_mid), BF16),
                pltpu.VMEM((*image_rows, z.c_mid), F32),
                pltpu.VMEM((*image_rows, z.c_mid), F32),
                pltpu.VMEM((z.images, KEPT, z.c_mid), BF16),
                pltpu.VMEM((2, z.images, KEPT, z.c_mid), BF16),
                pltpu.VMEM((pair * n * z.piece_two, z.c_mid), BF16),
                pltpu.VMEM((n, z.images, KEPT, z.rows * z.c_local), BF16),
                pltpu.VMEM((n, z.images, KEPT, z.rows * z.c_local), BF16),
                pltpu.VMEM((*image_rows, z.c_mid), F32),
                pltpu.VMEM((z.rows, KEPT, 128), F32),
                pltpu.VMEM((MICRO, 8, 8, z.c_mid), F32),
                pltpu.VMEM((4, MICRO, 16, z.c_mid), F32),
                pltpu.VMEM((4, MICRO, PAYLOAD, z.c_mid), F32),
                pltpu.VMEM((4, MICRO, pair * n, PAYLOAD, z.c_mid), F32),
                pltpu.VMEM((4, MICRO, depth, PAYLOAD, z.c_mid), F32),
                pltpu.VMEM((4, MICRO, PAYLOAD, z.c_mid), F32),
                pltpu.VMEM((pair * n * z.piece_one, z.c_mid), BF16),
                pltpu.VMEM((n, z.piece_one, z.c_mid), BF16),
                pltpu.VMEM((depth, z.sub_one, z.c_mid), BF16),
                pltpu.VMEM((depth, z.sub_one, z.c_mid), BF16),
                pltpu.VMEM((depth, z.sub_one, z.c_mid), BF16),
                pltpu.VMEM((n * max(z.piece_one, z.piece_two), z.c_mid), BF16),
                pltpu.VMEM((n, z.piece_two, z.c_mid), BF16),
                pltpu.VMEM((depth, z.sub_two, z.c_mid), BF16),
                pltpu.VMEM((depth, z.sub_two, z.c_mid), BF16),
                pltpu.VMEM((depth, z.sub_two, z.c_mid), BF16),
                dma((24,)),
                dma((2, MICRO)),
                dma((4, MICRO)),
                dma((4, MICRO)),
                dma((2, MICRO)),
                dma((2, n)),
                dma((2, n)),
                dma((2, n)),
                dma((2, MICRO * n)),
                dma((4 * MICRO, pair * n)),
                dma((4 * MICRO, pair * n)),
                dma((4 * MICRO, depth)),
                dma((4 * MICRO, depth)),
                dma((14, max(n, depth))),
                dma((14, max(n, depth))),
                dma((max(4, z.images // 8 + 1),)),
            ],
            compiler_params=pltpu.CompilerParams(
                collective_id=0, has_side_effects=True, vmem_limit_bytes=63 * 2**20
            ),
        )(
            image_counts,
            x_turned,
            kernel_one,
            point_one,
            block_one_norm_gains,
            block_one_norm_shifts,
            kernel_two,
            point_two,
            block_two_norm_gains,
            shifts_two,
            cotangent.transpose(0, 2, 1, 3),
        )
        block_out, grad_input, grad_one, grad_two, *small = outs
        block_out = block_out.transpose(0, 2, 1, 3).astype(F32)
        grad_input = grad_input[:, :, : z.in_rows].transpose(0, 2, 1, 3)
        grad_one = grad_one.reshape(-1, z.c_mid)
        grad_kernel_one = grad_one[: 9 * z.c_in].astype(F32).reshape(3, 3, z.c_in, z.c_mid)
        grad_point_one = grad_one[9 * z.c_in : 10 * z.c_in].astype(F32)
        grad_two = grad_two.reshape(pair, -1, z.c_mid)[:, : z.half * z.c_pad]
        grad_two = grad_two.reshape(pair * z.half, z.c_pad, z.c_mid)[:, : z.c_local].astype(F32)
        grad_kernel_two = grad_two[:9].reshape(3, 3, z.c_local, z.c_mid)
        return (
            block_out,
            grad_input,
            grad_kernel_one,
            grad_point_one,
            small[0],
            small[1],
            grad_kernel_two,
            grad_two[9],
            small[2],
            small[3],
        )

    return shards


def solution(mesh):
    placed = (
        P("dp", "shard", None, None),
        P("dp"),
        P(),
        P(),
        P(),
        P(),
        P(None, None, "shard", None),
        P("shard", None),
        P(None, "shard"),
        P(None, "shard"),
        P("dp", None, None, "shard"),
    )
    return jax.shard_map(
        build(mesh),
        mesh=mesh,
        in_specs=placed,
        out_specs=(
            P("dp", None, None, "shard"),
            P("dp", "shard", None, None),
            P(),
            P(),
            P(),
            P(),
            P(None, None, "shard", None),
            P("shard", None),
            P(None, "shard"),
            P(None, "shard"),
        ),
        check_vma=False,
    )
```

```python
import functools

import jax
import jax.numpy as jnp
from jax import lax
from jax.experimental import pallas as pl
from jax.experimental.pallas import tpu as pltpu
from jax.sharding import PartitionSpec as P

MICRO = 2
EPSILON = 1e-05
KEPT = 16
PAYLOAD = 16
MESH = pl.DeviceIdType.MESH
BF16 = jnp.bfloat16
F32 = jnp.float32


def up_to(value, step):
    return (value + step - 1) // step * step


def flat(value):
    return value.reshape(-1, value.shape[-1])


def dot(a, b):
    return jnp.dot(a, b, preferred_element_type=F32)


def dot_nt(a, b):
    return lax.dot_general(a, b, (((1,), (1,)), ((), ())), preferred_element_type=F32)


def dot_tn(a, b):
    return lax.dot_general(a, b, (((0,), (0,)), ((), ())), preferred_element_type=F32)


def eight(value):
    rows, lanes = value.shape
    return jnp.sum(value.reshape(rows // 8, 8, lanes), axis=0)


def sigmoid(value):
    return 0.5 * jnp.tanh(0.5 * value) + 0.5


class Sizes:
    def __init__(self, mesh, x_input, cotangent, point_one):
        self.groups, self.parts = mesh.shape["dp"], mesh.shape["shard"]
        self.images = x_input.shape[0] // self.groups
        self.in_rows = x_input.shape[1] // self.parts
        self.in_cols, self.c_in = x_input.shape[2:]
        self.rows = self.in_rows // 2
        self.cols = self.in_cols // 2
        self.c_mid = point_one.shape[1]
        self.c_local = self.c_mid // self.parts
        self.c_pad = up_to(self.c_local, 16)
        self.held_rows = up_to(self.in_rows, 8)
        self.out_rows = self.rows * self.parts
        self.batch = self.images // MICRO
        self.tile = max(1, min(self.batch, 512 // (self.rows * KEPT)))
        self.tiles = self.images // self.tile
        self.pair = 2 if self.groups % 2 == 0 else 1
        self.depth = self.groups // self.pair
        self.half = -(-10 // self.pair)
        self.sub_two = up_to(self.half * self.c_pad, 16 * self.depth) // self.depth
        self.piece_two = self.sub_two * self.depth
        real = 10 * self.c_in
        self.sub_one = up_to(real, 16 * self.depth * self.parts * self.pair) // (
            self.depth * self.parts * self.pair
        )
        self.piece_one = self.sub_one * self.depth


class Sender:
    def __init__(self):
        self.open = []

    def start(self, make, *given, when=None):
        if when is None:
            make(*given).start()
        else:
            pl.when(when)(make(*given).start)
        self.open.append((make, given, when))

    def finish(self):
        for make, given, when in self.open:
            if when is None:
                make(*given).wait_send()
            else:
                pl.when(when)(make(*given).wait_send)
        self.open = []


def kernel(
    z,
    count,
    x_hbm,
    k1_hbm,
    p1_hbm,
    gains_one,
    shifts_one,
    k2_hbm,
    p2_hbm,
    gains_two,
    shifts_two,
    cot_hbm,
    out_hbm,
    grad_in_hbm,
    grad_one_hbm,
    grad_two_hbm,
    grad_gains_one,
    grad_shifts_one,
    grad_gains_two,
    grad_shifts_two,
    odd_win,
    even_win,
    k1_win,
    p1_win,
    z3a,
    z1a,
    x_rim,
    halo,
    wide,
    far,
    near,
    slope,
    mask,
    acc,
    par,
    pay,
    slots_a,
    slots_z,
    totals,
    g_one,
    one_r2,
    one_s,
    one_r3,
    one_r4,
    two_r1,
    two_r2,
    two_s,
    two_r3,
    two_r4,
    local_sem,
    x_sem,
    hid_sem,
    dz_sem,
    e_sem,
    ag_sem,
    ag_pair_sem,
    cot_sem,
    out_sem,
    ea_send,
    ea_recv,
    ez_send,
    ez_recv,
    ar_one,
    ar_two,
    gi_sem,
):
    n, pair, depth = z.parts, z.pair, z.depth
    rows, c_mid, c_in, tile = z.rows, z.c_mid, z.c_in, z.tile
    batch, images = z.batch, z.images
    dp = lax.axis_index("dp")
    sh = lax.axis_index("shard")
    core = lax.rem(dp, pair)
    deep = lax.div(dp, pair)
    sibling = (dp + 1 - 2 * core, sh)
    me = core * n + sh
    has_above = sh > 0
    has_below = sh < n - 1
    above, below = (dp, sh - 1), (dp, sh + 1)
    per_batch = batch // tile

    def plane(k):
        return lax.rem(sh + k, n)

    def group_peer(k):
        slot = lax.rem(me + k, pair * n)
        return slot, (dp - core + lax.div(slot, n), lax.rem(slot, n))

    def deep_peer(k):
        other = lax.rem(deep + k, depth)
        return other, (other * pair + core, sh)

    def remote(src, dst, send, recv, device):
        return pltpu.make_async_remote_copy(
            src_ref=src,
            dst_ref=dst,
            send_sem=send,
            recv_sem=recv,
            device_id=device,
            device_id_type=MESH,
        )

    barrier = pltpu.get_barrier_semaphore()
    for k in range(1, pair * n):
        pl.semaphore_signal(barrier, 1, device_id=group_peer(k)[1], device_id_type=MESH)
    for k in range(1, depth):
        pl.semaphore_signal(barrier, 1, device_id=deep_peer(k)[1], device_id_type=MESH)

    own_loads = []

    def load(src, dst):
        copy = pltpu.make_async_copy(src, dst, local_sem.at[len(own_loads)])
        copy.start()
        own_loads.append(copy)

    def wide_rows(half, part, offset, length):
        start = (half * n + part) * z.piece_two + offset
        if not isinstance(start, int):
            start = pl.multiple_of(start, 16)
        return wide.at[pl.ds(start, length)]

    taps = [k2_hbm.at[t // 3, t % 3] for t in range(9)] + [p2_hbm]
    for t in range(10):
        load(taps[t], wide_rows(t // z.half, sh, t % z.half * z.c_pad, z.c_pad))
    n_wide = len(own_loads)
    for d in range(3):
        load(k1_hbm.at[d, 1], k1_win.at[d, pl.ds(0, 192)])
        load(k1_hbm.at[d, 0, pl.ds(128, 64)], k1_win.at[d, pl.ds(192, 64)])
        load(k1_hbm.at[d, 0, pl.ds(0, 128)], k1_win.at[d, pl.ds(256, 128)])
        load(k1_hbm.at[d, 2], k1_win.at[d, pl.ds(384, 192)])
    load(p1_hbm, p1_win.at[pl.ds(0, 192)])

    pl.semaphore_wait(barrier, pair * n - 1 + depth - 1)

    sender = Sender()
    gather = Sender()

    def x_copy(b):
        some = pl.ds(b * batch, batch)
        return remote(
            x_rim.at[some], halo.at[0, some], x_sem.at[0, b], x_sem.at[1, b], below
        )

    row_at = lax.broadcasted_iota(jnp.int32, mask.shape, 0) + sh * rows
    col_at = lax.broadcasted_iota(jnp.int32, mask.shape, 1)
    mask[...] = jnp.where((row_at < z.cols) & (col_at < z.cols), 1.0, 0.0)

    @pl.when(jnp.logical_not(has_above))
    def _():
        halo[0] = jnp.zeros(halo.shape[1:], BF16)

    @pl.when(jnp.logical_not(has_below))
    def _():
        halo[1] = jnp.zeros(halo.shape[1:], BF16)

    for d in range(3):
        k1_win[d, 576:640] = jnp.zeros((64, c_mid), BF16)
    p1_win[192:256] = jnp.zeros((64, c_mid), BF16)

    ag_length = z.half * z.c_pad

    def gather_copy(k, first=0, length=ag_length):
        own = wide_rows(core, sh, first, length)
        return remote(own, own, ag_sem.at[0, k], ag_sem.at[1, sh], (dp, plane(k)))

    def gather_taps(first, last):
        for k in range(1, n):
            gather_copy(k, first * z.c_pad, (last - first) * z.c_pad).start()

    def three(value):
        return jnp.concatenate([value] * (c_mid // 128), axis=-1)

    def images_at(t):
        return pl.ds(pl.multiple_of(t * tile, tile), tile)

    def kept(first, count_):
        return mask[first : first + count_][None]

    def mask_of(start, size, first=0, count_=rows):
        shape = (size, count_, KEPT, 128)
        image_at = lax.broadcasted_iota(jnp.int32, shape, 0) + start
        return three(flat(jnp.where(image_at < count[0], kept(first, count_), 0.0)))

    def mask_at(t):
        return mask_of(t * tile, tile)

    def pixels_at():
        return three(flat(jnp.broadcast_to(kept(0, rows), (tile, rows, KEPT, 128))))

    def shaped(value, count_=rows):
        return value.reshape(-1, count_, KEPT, value.shape[-1])

    def add_to(batch_at, at, value):
        acc[batch_at, at] = acc[batch_at, at] + eight(value)

    def group_copy(e, b, k):
        slot, device = group_peer(k)
        some = pl.ds(0, PAYLOAD if e + b == 0 else 8)
        return remote(
            pay.at[e, b, some],
            slots_a.at[e, b, me, some],
            ea_send.at[e * MICRO + b, k],
            ea_recv.at[e * MICRO + b, me],
            device,
        )

    def deep_sum(e, b, k):
        other, device = deep_peer(k)
        some = pl.ds(0, PAYLOAD if e + b == 0 else 8)
        own = slots_z.at[e, b, deep, some]
        return remote(
            own, own, ez_send.at[e * MICRO + b, k], ez_recv.at[e * MICRO + b, deep], device
        )

    def exchange_start(e, b):
        pay[e, b, 0:8] = jnp.sum(acc[b], axis=1)
        length = 8
        if e + b == 0:
            length = PAYLOAD
            lane = lax.broadcasted_iota(jnp.int32, (3, c_mid), 1)
            first = sh * z.c_local
            owned = (lane >= first) & (lane < first + z.c_local) & (dp == 0)
            for at, given in ((8, gains_two), (11, shifts_two)):
                spread_out = jnp.concatenate([given[...]] * n, axis=1)
                pay[e, b, at : at + 3] = jnp.where(owned, spread_out, 0.0)
            pay[e, b, 14:16] = jnp.zeros((2, c_mid), F32)
        slots_a[e, b, me, 0:length] = pay[e, b, 0:length]
        for k in range(1, pair * n):
            group_copy(e, b, k).start()
        acc[b] = jnp.zeros(acc.shape[1:], F32)

    def exchange_pass(e, b):
        at = e * MICRO + b
        length = PAYLOAD if e + b == 0 else 8
        some = pl.ds(0, length)
        for k in range(1, pair * n):
            slot, device = group_peer(k)
            remote(
                pay.at[e, b, some],
                slots_a.at[e, b, slot, some],
                ea_send.at[at, k],
                ea_recv.at[at, slot],
                device,
            ).wait_recv()
        total = slots_a[e, b, 0, 0:length]
        for slot in range(1, pair * n):
            total = total + slots_a[e, b, slot, 0:length]
        slots_z[e, b, deep, 0:length] = total
        for k in range(1, depth):
            deep_sum(e, b, k).start()

    def exchange_end(e, b):
        at = e * MICRO + b
        length = PAYLOAD if e + b == 0 else 8
        some = pl.ds(0, length)
        for k in range(1, depth):
            other, device = deep_peer(k)
            there = slots_z.at[e, b, other, some]
            remote(there, there, ez_send.at[at, k], ez_recv.at[at, other], device).wait_recv()
        total = slots_z[e, b, 0, 0:length]
        for other in range(1, depth):
            total = total + slots_z[e, b, other, 0:length]
        totals[e, b, 0:length] = total
        for k in range(1, pair * n):
            group_copy(e, b, k).wait_send()
        for k in range(1, depth):
            deep_sum(e, b, k).wait_send()

    def moments(e, b, at, pixels):
        center = totals[e, b, at : at + 1] / pixels
        square = totals[e, b, at + 1 : at + 2] / pixels
        return center, lax.rsqrt(square - center * center + EPSILON)

    held = z.held_rows
    spread_rows = z.in_cols * held
    wide_rows_x = 4 * KEPT * held // 2
    group = 4

    def windows(even0, even1, odd0, odd1):
        before0, before1 = pltpu.roll(odd0, 1, 0), pltpu.roll(odd1, 1, 0)
        parts = [even0, even1 + pltpu.roll(before1, 64, 1), before0, odd0, odd1]
        return jnp.concatenate([v.astype(BF16) for v in parts], axis=1)

    def cot_copy(b, k):
        to = plane(k)
        some = pl.ds(b * batch, batch)
        return remote(
            far.at[to, some],
            near.at[sh, some],
            cot_sem.at[0, b * n + k],
            cot_sem.at[1, b * n + sh],
            (dp, to),
        )

    for copy in own_loads[:n_wide]:
        copy.wait()
    gather_taps(0, 1)

    def extract_above(i, carry):
        here = pl.ds(i * 8, 8)
        value = flat(halo[0, here]).astype(F32)
        low = lax.broadcasted_iota(jnp.int32, (8 * KEPT, 128), 1) < 64
        mixed = value[:, 256:384]
        even1 = jnp.where(low, mixed, 0.0)
        odd1 = jnp.where(low, pltpu.roll(mixed, 64, 1), 0.0)
        value = windows(value[:, 0:128], even1, value[:, 128:256], odd1)
        odd_win[here, 0] = value.reshape(8, KEPT, 640)
        return carry

    def forward_one(b, first, count_):
        start = b * batch
        here = pl.ds(start, batch)
        side = flat(even_win[here, first : first + count_])
        three_branch = dot(flat(odd_win[here, first : first + count_]), k1_win[0])
        three_branch = three_branch + dot(side, k1_win[1])
        three_branch = three_branch + dot(
            flat(odd_win[here, first + 1 : first + 1 + count_]), k1_win[2]
        )
        point_branch = dot(side[:, 0:256], p1_win[...])
        z3a[here, first : first + count_] = shaped(three_branch, count_)
        z1a[here, first : first + count_] = shaped(point_branch, count_)
        m = mask_of(start, batch, first, count_)
        masked = three_branch * m
        add_to(b, 0, masked)
        add_to(b, 1, masked * three_branch)
        masked = point_branch * m
        add_to(b, 2, masked)
        add_to(b, 3, masked * point_branch)
        add_to(b, 4, m)

    def first_part(x_own, cot_own, x_wide):
        loads = []
        step = 8
        for at in range(0, images, step):
            copy = pltpu.make_async_copy(
                x_hbm.at[pl.ds(at, step)], x_own.at[pl.ds(at, step)], gi_sem.at[at // step]
            )
            copy.start()
            loads.append(copy)
        cot_load = pltpu.make_async_copy(cot_hbm, cot_own, gi_sem.at[images // step])
        cot_load.start()
        x_wide[...] = jnp.zeros_like(x_wide)

        def extract(i, carry):
            here = pl.ds(i * group, group)
            for g in range(group):
                value = x_own[i * group + g].astype(F32).reshape(spread_rows, c_in)
                x_wide[0, g, 0:spread_rows] = value[:, 0:128]
                x_wide[1, g, 0:spread_rows, 0:64] = value[:, 128:192]

            def columns(half, odd):
                return flat(
                    jnp.stack(
                        [
                            x_wide[half, g, pl.ds(odd * held + r, KEPT, stride=2 * held), :]
                            for g in range(group)
                            for r in range(z.in_rows)
                        ]
                    )
                )

            even0, even1, odd0, odd1 = columns(0, 0), columns(1, 0), columns(0, 1), columns(1, 1)
            value = windows(even0, even1, odd0, odd1).reshape(group, rows, 2, KEPT, 640)
            even_win[here] = value[:, :, 0]
            odd_win[here, 1 : rows + 1] = value[:, :, 1]
            rim = jnp.concatenate([even0, odd0, even1 + pltpu.roll(odd1, 64, 1)], axis=1)
            rim = rim.reshape(group, z.in_rows, KEPT, 384)[:, z.in_rows - 1]
            x_rim[here] = rim.astype(BF16)
            return carry

        for at in range(0, images, step):
            loads[at // step].wait()
            lax.fori_loop(at // group, (at + step) // group, extract, 0)
            if (at + step) % batch == 0:
                sender.start(x_copy, at // batch, when=has_below)

        cot_load.wait()
        out_rows = z.out_rows

        def repack(i, carry):
            value = cot_own[i].astype(F32).reshape(z.cols * out_rows, z.c_local)
            x_wide[0, 0, 0 : z.cols * out_rows, 0 : z.c_local] = value
            for to in range(n):
                pieces = [
                    x_wide[0, 0, pl.ds(to * rows + r, KEPT, stride=out_rows), :][:, 0 : z.c_local]
                    for r in range(rows)
                ]
                far[to, i] = jnp.concatenate(pieces, axis=1).astype(BF16)
            return carry


        for copy in own_loads[n_wide:]:
            copy.wait()
        acc[...] = jnp.zeros_like(acc)
        for b in range(MICRO):
            for at in range(1, rows, 2):
                forward_one(b, at, min(2, rows - at))
        for b in range(MICRO):
            pl.when(has_above)(x_copy(b).wait_recv)
            lax.fori_loop(b * batch // 8, (b + 1) * batch // 8, extract_above, 0)
            forward_one(b, 0, 1)
            exchange_start(0, b)
        gather_taps(1, z.half)
        lax.fori_loop(0, images // 4, repack, 0)
        exchange_pass(0, 0)
        lax.fori_loop(images // 4, images // 2, repack, 0)
        exchange_pass(0, 1)
        lax.fori_loop(images // 2, images, repack, 0)
        near[sh] = far[sh]

    pl.run_scoped(
        first_part,
        pltpu.VMEM((images, z.in_cols, held, c_in), BF16),
        pltpu.VMEM((images, z.cols, z.out_rows, z.c_local), BF16),
        pltpu.VMEM((2, group, max(wide_rows_x, KEPT * z.out_rows), 128), F32),
    )

    def pass_copy(k):
        part = plane(k)
        piece = wide_rows(core, part, 0, ag_length)
        return remote(piece, piece, ag_pair_sem.at[0, k], ag_pair_sem.at[1, part], sibling)

    def norm_one(b):
        pixels = totals[0, b, 4:5]
        center_three, rstd_three = moments(0, b, 0, pixels)
        center_point, rstd_point = moments(0, b, 2, pixels)
        scale_three = gains_one[0:1] * rstd_three
        scale_point = gains_one[1:2] * rstd_point
        par[0, b, 0:1] = scale_three
        par[0, b, 1:2] = scale_point
        par[0, b, 2:3] = (shifts_one[0:1] - center_three * scale_three) + (
            shifts_one[1:2] - center_point * scale_point
        )
        par[0, b, 3:4] = center_three
        par[0, b, 4:5] = center_point
        par[0, b, 5:6] = rstd_three
        par[0, b, 6:7] = rstd_point
        par[0, b, 7:8] = pixels

    def first_sum(here, b, first=0, count_=rows):
        some = slice(first, first + count_)
        return (
            flat(z3a[here, some]) * par[0, b, 0:1]
            + flat(z1a[here, some]) * par[0, b, 1:2]
            + par[0, b, 2:3]
        )

    def put_three(target, here, at, count_, value):
        length = value.shape[0]
        shape = (-1, count_, KEPT, c_mid)
        before = pltpu.roll(value, 1, 0)
        after = pltpu.roll(value, length - 1, 0)
        target[here, at : at + count_, :, 0:c_mid] = before.astype(BF16).reshape(shape)
        target[here, at : at + count_, :, c_mid : 2 * c_mid] = value.astype(BF16).reshape(shape)
        target[here, at : at + count_, :, 2 * c_mid : 3 * c_mid] = after.astype(BF16).reshape(shape)

    def send_rims(source, sems):
        copies = []
        center = pl.ds(c_mid, c_mid)
        for b in range(MICRO):
            some = pl.ds(b * batch, batch)
            copies.append(
                (
                    remote(
                        source.at[some, 1, :, center],
                        halo.at[1, some],
                        sems.at[0, b],
                        sems.at[1, b],
                        above,
                    ),
                    remote(
                        source.at[some, rows, :, center],
                        halo.at[0, some],
                        sems.at[2, b],
                        sems.at[3, b],
                        below,
                    ),
                )
            )
        return copies

    def spread_halo(target, side, b):
        def one(i, carry):
            here = pl.ds(b * batch + i * 8, 8)
            value = flat(halo[side, here]).astype(F32)
            put_three(target, here, 0 if side == 0 else rows + 1, 1, value)
            return carry

        lax.fori_loop(0, batch // 8, one, 0)

    def start_rims(copies, b):
        pl.when(has_above)(copies[b][0].start)
        pl.when(has_below)(copies[b][1].start)

    def take_rims(copies, b):
        pl.when(has_below)(copies[b][0].wait_recv)
        pl.when(has_above)(copies[b][1].wait_recv)

    def close_rims(copies):
        for b in range(MICRO):
            pl.when(has_above)(copies[b][0].wait_send)
            pl.when(has_below)(copies[b][1].wait_send)

    inner = (1, rows - 2) if rows > 2 else None
    outer = sorted({0, rows - 1})

    class Group:
        def __init__(self, size, own, peer):
            self.size, self.own, self.peer = size, own, peer

    by_plane = Group(n, sh, lambda k: (plane(k), (dp, plane(k))))
    by_depth = Group(depth, deep, deep_peer)

    class Reduce:
        def __init__(self, first, second, g, r1, r2, s, r3, r4, sems, sub):
            self.first, self.second = first, second
            self.g, self.r1, self.r2, self.s, self.r3, self.r4 = g, r1, r2, s, r3, r4
            self.sems, self.piece = sems, second.size * sub

        def at(self, half, i):
            start = (half * self.first.size + i) * self.piece
            return pl.ds(pl.multiple_of(start, 16), self.piece)

        def pair_copy(self):
            start = pl.multiple_of((1 - core) * self.first.size * self.piece, 16)
            return remote(
                self.g.at[pl.ds(start, self.first.size * self.piece)],
                self.r1,
                self.sems.at[0, 0],
                self.sems.at[1, 0],
                sibling,
            )

        def start_pair(self):
            if pair == 2:
                sender.start(self.pair_copy)

        def start_first(self):
            if pair == 2:
                self.pair_copy().wait_recv()

                def join(i, carry):
                    at = self.at(core, i)
                    arrived = self.r1[pl.ds(pl.multiple_of(i * self.piece, 16), self.piece)]
                    self.g[at] = (self.g[at].astype(F32) + arrived.astype(F32)).astype(BF16)
                    return carry

                lax.fori_loop(0, self.first.size, join, 0)

            self.r2[self.first.own] = self.g[self.at(core, self.first.own)]

        def first_copy(self, k, part=0, parts=1):
            to, device = self.first.peer(k)
            length = self.piece // parts
            start = (core * self.first.size + to) * self.piece + part * length
            return remote(
                self.g.at[pl.ds(pl.multiple_of(start, 16), length)],
                self.r2.at[self.first.own, pl.ds(part * length, length)],
                self.sems.at[2, k],
                self.sems.at[3, self.first.own],
                device,
            )

        def send_first(self, part, parts):
            for k in range(1, self.first.size):
                self.first_copy(k, part, parts).start()

        def start_second(self):
            for k in range(1, self.first.size):
                other, device = self.first.peer(k)
                there = self.r2.at[other]
                remote(
                    there, there, self.sems.at[2, k], self.sems.at[3, other], device
                ).wait_recv()
                self.first_copy(k).wait_send()
            total = self.r2[0].astype(F32)
            for i in range(1, self.first.size):
                total = total + self.r2[i].astype(F32)
            self.s[...] = total.astype(BF16).reshape(self.s.shape)

            def second_copy(k):
                to, device = self.second.peer(k)
                return remote(
                    self.s.at[to],
                    self.r3.at[self.second.own],
                    self.sems.at[4, k],
                    self.sems.at[5, self.second.own],
                    device,
                )

            for k in range(1, self.second.size):
                sender.start(second_copy, k)
            self.r3[self.second.own] = self.s[self.second.own]

        def start_back(self):
            for k in range(1, self.second.size):
                other, device = self.second.peer(k)
                there = self.r3.at[other]
                remote(
                    there, there, self.sems.at[4, k], self.sems.at[5, other], device
                ).wait_recv()
            total = self.r3[0].astype(F32)
            for i in range(1, self.second.size):
                total = total + self.r3[i].astype(F32)
            self.r4[deep] = total.astype(BF16)

            def back_copy(k):
                own = self.r4.at[deep]
                return remote(
                    own, own, self.sems.at[6, k], self.sems.at[7, deep], deep_peer(k)[1]
                )

            for k in range(1, depth):
                sender.start(back_copy, k)

        def finish_back(self):
            for k in range(1, depth):
                other, device = deep_peer(k)
                there = self.r4.at[other]
                remote(
                    there, there, self.sems.at[6, k], self.sems.at[7, other], device
                ).wait_recv()

    red_two = Reduce(
        by_depth,
        by_plane,
        wide,
        two_r1.at[pl.ds(0, n * z.piece_two)],
        two_r2,
        two_s,
        two_r3,
        two_r4,
        ar_two,
        z.sub_two,
    )
    red_one = Reduce(
        by_plane,
        by_depth,
        g_one,
        two_r1.at[pl.ds(0, n * z.piece_one)],
        one_r2,
        one_s,
        one_r3,
        one_r4,
        ar_one,
        z.sub_one,
    )

    def out_copy(b, k, part=0, parts=1):
        to = plane(k)
        length = batch // parts
        some = pl.ds(b * batch + part * length, length)
        return remote(
            near.at[to, some],
            far.at[sh, some],
            out_sem.at[0, b * n + k],
            out_sem.at[1, b * n + sh],
            (dp, to),
        )

    def send_out(b, part, parts):
        for k in range(1, n):
            out_copy(b, k, part, parts).start()

    def second_part(hid, k2, p2, z3b, dz3, dz1):
        rims = send_rims(hid, hid_sem)

        def make_hidden(t, carry):
            here = images_at(t)
            b = t // per_batch
            total = first_sum(here, b)
            put_three(hid, here, 1, rows, pixels_at() * (total * sigmoid(total)))
            return carry

        for b in range(MICRO):
            exchange_end(0, b)
            norm_one(b)
            lax.fori_loop(b * per_batch, (b + 1) * per_batch, make_hidden, 0)
            start_rims(rims, b)
        for k in range(1, n):
            cot_copy(0, k).start()

        for k in range(1, n):
            part = plane(k)
            piece = wide_rows(core, part, 0, ag_length)
            remote(piece, piece, ag_sem.at[0, k], ag_sem.at[1, part], (dp, part)).wait_recv()
            if pair == 2:
                gather.start(pass_copy, k)
        if pair == 2:
            for k in range(1, n):
                part = plane(k)
                piece = wide_rows(1 - core, part, 0, ag_length)
                remote(
                    piece, piece, ag_pair_sem.at[0, k], ag_pair_sem.at[1, part], sibling
                ).wait_recv()
        gather.finish()
        for k in range(1, n):
            gather_copy(k).wait_send()
        for t in range(10):
            for part in range(n):
                start = (t // z.half * n + part) * z.piece_two + t % z.half * z.c_pad
                value = wide[start : start + z.c_local]
                if t < 9:
                    base = t % 3 * c_mid + part * z.c_local
                    k2[t // 3, base : base + z.c_local] = value
                else:
                    p2[part * z.c_local : (part + 1) * z.c_local] = value

        def forward_two(b, first, count_):
            start = b * batch
            here = pl.ds(start, batch)
            three_branch = dot(flat(hid[here, first : first + count_]), k2[0])
            for d in (1, 2):
                three_branch = three_branch + dot(
                    flat(hid[here, first + d : first + d + count_]), k2[d]
                )
            center = flat(hid[here, first + 1 : first + 1 + count_, :, c_mid : 2 * c_mid])
            point_branch = dot(center, p2[...])
            z3b[here, first : first + count_] = shaped(three_branch, count_)
            m = mask_of(start, batch, first, count_)
            masked = three_branch * m
            add_to(b, 0, masked)
            add_to(b, 1, masked * three_branch)
            masked = point_branch * m
            add_to(b, 2, masked)
            add_to(b, 3, masked * point_branch)
            center = center.astype(F32)
            masked = center * m
            add_to(b, 4, masked)
            add_to(b, 5, masked * center)

        if inner:
            for b in range(MICRO):
                forward_two(b, *inner)
        for b in range(MICRO):
            take_rims(rims, b)
            spread_halo(hid, 0, b)
            spread_halo(hid, 1, b)
            for at in outer:
                forward_two(b, at, 1)
                if b and at == 0:
                    exchange_pass(1, 0)
            if b == 0:
                for k in range(1, n):
                    cot_copy(0, k).wait_send()
            exchange_start(1, b)
        for k in range(1, n):
            cot_copy(1, k).start()

        def norm_two(b):
            pixels = par[0, b, 7:8]
            offset = 0.0
            for i in range(3):
                center, rstd = moments(1, b, 2 * i, pixels)
                scale = totals[0, 0, 8 + i : 9 + i] * rstd
                par[1, b, i : i + 1] = scale
                par[1, b, 4 + i : 5 + i] = center
                par[1, b, 7 + i : 8 + i] = rstd
                offset = offset + (totals[0, 0, 11 + i : 12 + i] - center * scale)
            par[1, b, 3:4] = offset

        def slope_two(t, carry):
            here = images_at(t)
            b = t // per_batch
            taken = [near[part, here] for part in range(n)]
            cot = jnp.stack(
                [
                    jnp.concatenate(
                        [v[:, :, r * z.c_local : (r + 1) * z.c_local] for v in taken], axis=2
                    )
                    for r in range(rows)
                ],
                axis=1,
            )
            v3 = flat(z3b[here])
            vi = flat(hid[here, 1 : rows + 1, :, c_mid : 2 * c_mid])
            v1 = dot(vi, p2[...])
            vi = vi.astype(F32)
            total = (
                v3 * par[1, b, 0:1] + v1 * par[1, b, 1:2] + vi * par[1, b, 2:3] + par[1, b, 3:4]
            )
            m = mask_at(t)
            gate = sigmoid(total)
            down = m * flat(cot).astype(F32) * (gate * (1.0 + total * (1.0 - gate)))
            slope[here] = shaped(down)
            add_to(b, 0, down)
            add_to(b, 1, down * (v3 - par[1, b, 4:5]))
            add_to(b, 2, down * (v1 - par[1, b, 5:6]))
            add_to(b, 3, down * (vi - par[1, b, 6:7]))
            out = shaped((m * (total * gate)).astype(BF16))
            for part in range(n):
                lanes = slice(part * z.c_local, (part + 1) * z.c_local)
                near[part, here] = jnp.concatenate(
                    [out[:, r, :, lanes] for r in range(rows)], axis=2
                )
            return carry

        def block(t):
            return t // 3, slice(t % 3 * c_mid, (t % 3 + 1) * c_mid)

        for t in range(5):
            one, other = k2[block(t)], k2[block(8 - t)]
            k2[block(t)] = other.T
            if t != 4:
                k2[block(8 - t)] = one.T

        for b in range(MICRO):
            exchange_end(1, b)
            norm_two(b)
            for k in range(1, n):
                part = plane(k)
                there = near.at[part, pl.ds(b * batch, batch)]
                remote(
                    there, there, cot_sem.at[0, b * n + k], cot_sem.at[1, b * n + part], (dp, part)
                ).wait_recv()
            for t in range(per_batch):
                slope_two(b * per_batch + t, 0)
                if t == 0:
                    exchange_pass(1, 1) if b == 0 else exchange_pass(2, 0)
            exchange_start(2, b)
            if b == 0:
                for k in range(1, n):
                    cot_copy(1, k).wait_send()
        send_out(0, 0, 2)
        far[sh] = near[sh]

        def turn_two(b):
            pixels = par[0, b, 7:8]
            slopes = totals[2, b, 0:1]
            for i in range(3):
                rstd = par[1, b, 7 + i : 8 + i]
                cross = totals[2, b, 1 + i : 2 + i] * rstd
                scale = par[1, b, i : i + 1]
                tilt = -scale * rstd * cross / pixels
                par[2, b, 3 * i : 3 * i + 1] = scale
                par[2, b, 3 * i + 1 : 3 * i + 2] = tilt
                par[2, b, 3 * i + 2 : 3 * i + 3] = (
                    -scale * slopes / pixels - tilt * par[1, b, 4 + i : 5 + i]
                )

        rims_back = send_rims(dz3, dz_sem)

        def make_dz(t, carry):
            here = images_at(t)
            b = t // per_batch
            m = mask_at(t)
            down = flat(slope[here])
            value = down * par[2, b, 0:1] + m * (flat(z3b[here]) * par[2, b, 1:2] + par[2, b, 2:3])
            put_three(dz3, here, 1, rows, value)
            v1 = dot(flat(hid[here, 1 : rows + 1, :, c_mid : 2 * c_mid]), p2[...])
            value = down * par[2, b, 3:4] + m * (v1 * par[2, b, 4:5] + par[2, b, 5:6])
            dz1[here] = shaped(value.astype(BF16))
            return carry

        def backward_two(b, first, count_):
            start = b * batch
            here = pl.ds(start, batch)
            some = slice(first, first + count_)
            total = dot_nt(flat(dz1[here, some]), p2[...])
            for k in range(3):
                total = total + dot(flat(dz3[here, first + k : first + k + count_]), k2[k])
            m = mask_of(start, batch, first, count_)
            vi = flat(hid[here, first + 1 : first + 1 + count_, :, c_mid : 2 * c_mid]).astype(F32)
            total = total + (
                flat(slope[here, some]) * par[2, b, 6:7]
                + m * (vi * par[2, b, 7:8] + par[2, b, 8:9])
            )
            total = total.astype(BF16).astype(F32)
            summed = first_sum(here, b, first, count_)
            gate = sigmoid(summed)
            down = m * total * (gate * (1.0 + summed * (1.0 - gate)))
            slope[here, some] = shaped(down, count_)
            add_to(b, 0, down)
            add_to(b, 1, down * (flat(z3a[here, some]) - par[0, b, 3:4]))
            add_to(b, 2, down * (flat(z1a[here, some]) - par[0, b, 4:5]))

        exchange_end(2, 0)
        turn_two(0)
        lax.fori_loop(0, per_batch, make_dz, 0)
        start_rims(rims_back, 0)
        exchange_pass(2, 1)
        if inner:
            backward_two(0, *inner)
        exchange_end(2, 1)
        turn_two(1)
        lax.fori_loop(per_batch, 2 * per_batch, make_dz, 0)
        start_rims(rims_back, 1)

        def mine(value):
            result = jnp.zeros((1, z.c_local), F32)
            for part in range(n):
                here = value[:, part * z.c_local : (part + 1) * z.c_local]
                result = result + jnp.where(sh == part, here, 0.0)
            return result

        shifts = mine(totals[2, 0, 0:1] + totals[2, 1, 0:1])
        for i in range(3):
            cross = [
                totals[2, b, 1 + i : 2 + i] * par[1, b, 7 + i : 8 + i] for b in range(MICRO)
            ]
            grad_gains_two[i : i + 1] = mine(cross[0] + cross[1])
            grad_shifts_two[i : i + 1] = shifts

        def put_two(t, value):
            value = value.astype(BF16)
            half, first = t // z.half, t % z.half * z.c_pad
            for part in range(n):
                done = 0
                while done < z.c_local:
                    block, offset = divmod(first + done, z.sub_two)
                    length = min(z.sub_two - offset, z.c_local - done)
                    start = ((half * depth + block) * n + part) * z.sub_two + offset
                    have = part * z.c_local + done
                    wide[start : start + length] = value[have : have + length]
                    done += length

        center = pl.ds(c_mid, c_mid)
        for d in range(3):
            value = dot_tn(flat(hid[:, d : d + rows]), flat(dz3[:, 1 : rows + 1, :, center]))
            for c in range(3):
                put_two(3 * d + c, value[c * c_mid : (c + 1) * c_mid])
        put_two(9, dot_tn(flat(hid[:, 1 : rows + 1, :, center]), flat(dz1[...])))
        red_two.start_pair()

        if inner:
            backward_two(1, *inner)
        red_two.start_first()
        red_two.send_first(0, n)
        for b in range(MICRO):
            take_rims(rims_back, b)
            spread_halo(dz3, 0, b)
            spread_halo(dz3, 1, b)
            for at in outer:
                backward_two(b, at, 1)
                if b and at == 0:
                    exchange_pass(3, 0)
            exchange_start(3, b)
        send_out(0, 1, 2)
        close_rims(rims)
        close_rims(rims_back)

    pl.run_scoped(
        second_part,
        pltpu.VMEM((images, rows + 2, KEPT, 3 * c_mid), BF16),
        pltpu.VMEM((3, 3 * c_mid, c_mid), BF16),
        pltpu.VMEM((c_mid, c_mid), BF16),
        pltpu.VMEM((images, rows, KEPT, c_mid), F32),
        pltpu.VMEM((images, rows + 2, KEPT, 3 * c_mid), BF16),
        pltpu.VMEM((images, rows, KEPT, c_mid), BF16),
    )

    def third_part(dz3, dz1, paired, staged, out_own, turned):
        def turn_one(b):
            pixels = par[0, b, 7:8]
            slopes = totals[3, b, 0:1]
            for i in range(2):
                rstd = par[0, b, 5 + i : 6 + i]
                cross = totals[3, b, 1 + i : 2 + i] * rstd
                scale = par[0, b, i : i + 1]
                tilt = -scale * rstd * cross / pixels
                par[3, b, 3 * i : 3 * i + 1] = scale
                par[3, b, 3 * i + 1 : 3 * i + 2] = tilt
                par[3, b, 3 * i + 2 : 3 * i + 3] = (
                    -scale * slopes / pixels - tilt * par[0, b, 3 + i : 4 + i]
                )

        rims = [
            remote(
                dz3.at[pl.ds(b * batch, batch), 0, :, pl.ds(0, c_mid)],
                halo.at[1, pl.ds(b * batch, batch)],
                e_sem.at[0, b],
                e_sem.at[1, b],
                above,
            )
            for b in range(MICRO)
        ]

        def turn_kernels():
            def tap(d, c):
                if c == 0:
                    return jnp.concatenate([k1_win[d, 256:384], k1_win[d, 192:256]], axis=0)
                return k1_win[d, 0:192] if c == 1 else k1_win[d, 384:576]

            order = [
                [tap(1, 1), p1_win[0:192]],
                [tap(1, 2), tap(1, 0)],
                [tap(2, 1), tap(0, 1)],
                [tap(2, 2), tap(2, 0)],
                [tap(0, 2), tap(0, 0)],
            ]
            for i, both in enumerate(order):
                for j, value in enumerate(both):
                    turned[i, j * c_mid : (j + 1) * c_mid] = value.T

        def make_dz(t, carry):
            here = images_at(t)
            b = t // per_batch
            m = mask_at(t)
            down = flat(slope[here])
            value = down * par[3, b, 0:1] + m * (flat(z3a[here]) * par[3, b, 1:2] + par[3, b, 2:3])
            after = pltpu.roll(value, value.shape[0] - 1, 0)
            dz3[here, 0:rows, :, 0:c_mid] = shaped(value.astype(BF16))
            dz3[here, 0:rows, :, c_mid : 2 * c_mid] = shaped(after.astype(BF16))
            value = down * par[3, b, 3:4] + m * (flat(z1a[here]) * par[3, b, 4:5] + par[3, b, 5:6])
            dz1[here] = shaped(value.astype(BF16))
            return carry

        def place_out(i, carry):
            for part in range(n):
                value = far[part, i].astype(F32)
                for r in range(rows):
                    place = pl.ds(part * rows + r, KEPT, stride=z.out_rows)
                    paired[0, 0, place, 0 : z.c_local] = value[
                        :, r * z.c_local : (r + 1) * z.c_local
                    ]
            value = paired[0, 0, 0 : z.cols * z.out_rows, 0 : z.c_local]
            out_own[i] = value.reshape(z.cols, z.out_rows, z.c_local).astype(BF16)
            return carry

        def take_out(b):
            for k in range(1, n):
                part = plane(k)
                there = far.at[part, pl.ds(b * batch, batch)]
                remote(
                    there, there, out_sem.at[0, b * n + k], out_sem.at[1, b * n + part], (dp, part)
                ).wait_recv()
                out_copy(b, k).wait_send()
            lax.fori_loop(b * batch, (b + 1) * batch, place_out, 0)

        turn_kernels()
        for b in range(MICRO):
            exchange_end(3, b)
            turn_one(b)
            lax.fori_loop(b * per_batch, (b + 1) * per_batch, make_dz, 0)
            pl.when(has_above)(rims[b].start)
            if b == 0:
                exchange_pass(3, 1)
                for part in range(1, n):
                    red_two.send_first(part, n)
        shifts = totals[3, 0, 0:1] + totals[3, 1, 0:1]
        for i in range(2):
            cross = [
                totals[3, b, 1 + i : 2 + i] * par[0, b, 5 + i : 6 + i] for b in range(MICRO)
            ]
            grad_gains_one[i : i + 1] = cross[0] + cross[1]
            grad_shifts_one[i : i + 1] = shifts

        def put_one(base, value):
            g_one[base : base + value.shape[0]] = value.astype(BF16)

        own = flat(dz3[:, 0:rows, :, 0:c_mid])
        for d in range(3):
            if d == 1:
                side = flat(even_win[...])
            else:
                side = flat(odd_win[:, d // 2 : d // 2 + rows])
            value = dot_tn(side, own)
            base = 3 * d * c_in
            put_one(base + c_in, value[0:192])
            put_one(base + 128, value[192:256])
            put_one(base, value[256:384])
            put_one(base + 2 * c_in, value[384:576])
        put_one(9 * c_in, dot_tn(flat(even_win[:, :, :, 0:256]), flat(dz1[...]))[0:192])
        if g_one.shape[0] > 10 * c_in:
            g_one[10 * c_in :] = jnp.zeros((g_one.shape[0] - 10 * c_in, c_mid), BF16)
        red_one.start_pair()
        for b in range(MICRO):
            pl.when(has_below)(rims[b].wait_recv)

        def spread(t, carry):
            here = images_at(t)
            value = flat(halo[1, here]).astype(F32)
            after = pltpu.roll(value, value.shape[0] - 1, 0)
            dz3[here, rows, :, 0:c_mid] = value.astype(BF16).reshape(tile, KEPT, c_mid)
            dz3[here, rows, :, c_mid : 2 * c_mid] = after.astype(BF16).reshape(tile, KEPT, c_mid)
            return carry

        lax.fori_loop(0, z.tiles, spread, 0)
        red_one.start_first()
        red_one.send_first(0, 1)
        send_out(1, 0, 2)
        send_out(1, 1, 2)

        some = staged.shape[1]
        steps = images // some

        def staged_copy(i, slot):
            return pltpu.make_async_copy(
                staged.at[slot],
                grad_in_hbm.at[pl.ds(i * some, some)],
                gi_sem.at[slot],
            )

        def input_grad(i, carry):
            here = pl.ds(i * some, some)
            slot = lax.rem(i, 2)
            own = flat(dz3[here, 0:rows])
            after = flat(dz3[here, 1 : rows + 1])
            own_c, after_c = own[:, 0:c_mid], after[:, 0:c_mid]
            value = [
                [
                    dot(own_c, turned[0, 0:c_mid]) + dot(flat(dz1[here]), turned[0, c_mid:]),
                    dot(own, turned[1]),
                ],
                [
                    dot(own_c, turned[2, 0:c_mid]) + dot(after_c, turned[2, c_mid:]),
                    dot(own, turned[3]) + dot(after, turned[4]),
                ],
            ]

            @pl.when(i >= 2)
            def _():
                staged_copy(i, slot).wait()

            for r in range(2):
                for c in range(2):
                    both = value[r][c].reshape(some, rows, KEPT, c_in)
                    for g in range(some):
                        for at in range(rows):
                            place = pl.ds(c * held + 2 * at + r, KEPT, stride=2 * held)
                            paired[0, g, place, :] = both[g, at, :, 0:128]
                            paired[1, g, place, 0:64] = both[g, at, :, 128:192]
            staged[slot, :, :, :, 0:128] = paired[0, :, 0:spread_rows].reshape(
                some, z.in_cols, held, 128
            )
            staged[slot, :, :, :, 128:192] = paired[1, :, 0:spread_rows, 0:64].reshape(
                some, z.in_cols, held, 64
            )
            staged_copy(i, slot).start()
            return carry

        cuts = [0, steps // 4, steps - steps // 4, steps]
        lax.fori_loop(cuts[0], cuts[2], input_grad, 0)
        red_one.start_second()
        lax.fori_loop(cuts[2], cuts[3], input_grad, 0)
        red_one.start_back()
        take_out(0)
        take_out(1)
        out_write = pltpu.make_async_copy(out_own, out_hbm, gi_sem.at[2])
        out_write.start()
        for i in range(max(0, steps - 2), steps):
            staged_copy(i, i % 2).wait()
        out_write.wait()
        for b in range(MICRO):
            pl.when(has_above)(rims[b].wait_send)

    some = max(1, min(images // 2, 256 // (rows * KEPT)))
    pl.run_scoped(
        third_part,
        pltpu.VMEM((images, rows + 1, KEPT, 2 * c_mid), BF16),
        pltpu.VMEM((images, rows, KEPT, c_mid), BF16),
        pltpu.VMEM((2, some, max(wide_rows_x, KEPT * z.out_rows), 128), F32),
        pltpu.VMEM((2, some, z.in_cols, held, c_in), F32),
        pltpu.VMEM((images, z.cols, z.out_rows, z.c_local), BF16),
        pltpu.VMEM((5, 2 * c_mid, c_in), BF16),
    )

    red_two.start_second()
    red_one.finish_back()
    def one_at(half, part):
        return grad_one_hbm.at[half, part]

    one_own = pltpu.make_async_copy(red_one.r4, one_at(core, sh), ar_one.at[8, 0])
    one_own.start()

    def one_pair_copy():
        return remote(
            red_one.r4, one_at(core, sh), ar_one.at[12, 0], ar_one.at[13, sh], sibling
        )

    def one_plane_copy(k):
        return remote(
            red_one.r4, one_at(core, sh), ar_one.at[9, k], ar_one.at[10, sh], (dp, plane(k))
        )

    def one_pass_copy(k):
        part = plane(k)
        at = one_at(core, part)
        return remote(at, at, ar_one.at[11, k], ar_one.at[13, part], sibling)

    if pair == 2:
        sender.start(one_pair_copy)
    for k in range(1, n):
        sender.start(one_plane_copy, k)
    red_two.start_back()
    red_two.finish_back()
    two_at = grad_two_hbm.at[core]
    two_own = pltpu.make_async_copy(red_two.r4, two_at, ar_two.at[8, 0])
    two_own.start()
    two_pair = remote(red_two.r4, two_at, ar_two.at[9, 0], ar_two.at[10, 0], sibling)
    if pair == 2:
        two_pair.start()
    for k in range(1, n):
        part = plane(k)
        at = one_at(core, part)
        remote(at, at, ar_one.at[9, k], ar_one.at[10, part], (dp, part)).wait_recv()
        if pair == 2:
            sender.start(one_pass_copy, k)
    if pair == 2:
        for k in range(n):
            part = plane(k)
            at = one_at(1 - core, part)
            remote(at, at, ar_one.at[11, k], ar_one.at[13, part], sibling).wait_recv()
        two_pair.wait_send()
        remote(
            red_two.r4, grad_two_hbm.at[1 - core], ar_two.at[9, 0], ar_two.at[10, 0], sibling
        ).wait_recv()
    two_own.wait()
    one_own.wait()
    sender.finish()


def build(mesh):
    def shards(
        x_input,
        image_counts,
        kernel_one,
        point_one,
        block_one_norm_gains,
        block_one_norm_shifts,
        kernel_two,
        point_two,
        block_two_norm_gains,
        shifts_two,
        cotangent,
    ):
        z = Sizes.__new__(Sizes)
        whole_x = jax.ShapeDtypeStruct(
            (
                x_input.shape[0] * mesh.shape["dp"],
                x_input.shape[1] * mesh.shape["shard"],
                *x_input.shape[2:],
            ),
            x_input.dtype,
        )
        z.__init__(mesh, whole_x, cotangent, point_one)
        n, pair, depth = z.parts, z.pair, z.depth
        x_turned = x_input.transpose(0, 2, 1, 3)
        if z.held_rows != z.in_rows:
            more = z.held_rows - z.in_rows
            x_turned = jnp.pad(x_turned, ((0, 0), (0, 0), (0, more), (0, 0)))
        if z.c_pad != z.c_local:
            more = z.c_pad - z.c_local
            kernel_two = jnp.pad(kernel_two, ((0, 0), (0, 0), (0, more), (0, 0)))
            point_two = jnp.pad(point_two, ((0, more), (0, 0)))

        vmem = pl.BlockSpec(memory_space=pltpu.VMEM)
        anywhere = pl.BlockSpec(memory_space=pl.ANY)
        image_rows = (z.images, z.rows, KEPT)
        dma = pltpu.SemaphoreType.DMA
        outs = pl.pallas_call(
            functools.partial(kernel, z),
            out_shape=(
                jax.ShapeDtypeStruct((z.images, z.cols, z.out_rows, z.c_local), BF16),
                jax.ShapeDtypeStruct((z.images, z.in_cols, z.held_rows, z.c_in), F32),
                jax.ShapeDtypeStruct((pair, n, depth, z.sub_one, z.c_mid), BF16),
                jax.ShapeDtypeStruct((pair, depth, z.sub_two, z.c_mid), BF16),
                jax.ShapeDtypeStruct((2, z.c_mid), F32),
                jax.ShapeDtypeStruct((2, z.c_mid), F32),
                jax.ShapeDtypeStruct((3, z.c_local), F32),
                jax.ShapeDtypeStruct((3, z.c_local), F32),
            ),
            in_specs=[
                pl.BlockSpec(memory_space=pltpu.SMEM),
                anywhere,
                anywhere,
                anywhere,
                vmem,
                vmem,
                anywhere,
                anywhere,
                vmem,
                vmem,
                anywhere,
            ],
            out_specs=(anywhere, anywhere, anywhere, anywhere, vmem, vmem, vmem, vmem),
            scratch_shapes=[
                pltpu.VMEM((z.images, z.rows + 1, KEPT, 640), BF16),
                pltpu.VMEM((*image_rows, 640), BF16),
                pltpu.VMEM((3, 640, z.c_mid), BF16),
                pltpu.VMEM((256, z.c_mid), BF16),
                pltpu.VMEM((*image_rows, z.c_mid), F32),
                pltpu.VMEM((*image_rows, z.c_mid), F32),
                pltpu.VMEM((z.images, KEPT, z.c_mid), BF16),
                pltpu.VMEM((2, z.images, KEPT, z.c_mid), BF16),
                pltpu.VMEM((pair * n * z.piece_two, z.c_mid), BF16),
                pltpu.VMEM((n, z.images, KEPT, z.rows * z.c_local), BF16),
                pltpu.VMEM((n, z.images, KEPT, z.rows * z.c_local), BF16),
                pltpu.VMEM((*image_rows, z.c_mid), F32),
                pltpu.VMEM((z.rows, KEPT, 128), F32),
                pltpu.VMEM((MICRO, 8, 8, z.c_mid), F32),
                pltpu.VMEM((4, MICRO, 16, z.c_mid), F32),
                pltpu.VMEM((4, MICRO, PAYLOAD, z.c_mid), F32),
                pltpu.VMEM((4, MICRO, pair * n, PAYLOAD, z.c_mid), F32),
                pltpu.VMEM((4, MICRO, depth, PAYLOAD, z.c_mid), F32),
                pltpu.VMEM((4, MICRO, PAYLOAD, z.c_mid), F32),
                pltpu.VMEM((pair * n * z.piece_one, z.c_mid), BF16),
                pltpu.VMEM((n, z.piece_one, z.c_mid), BF16),
                pltpu.VMEM((depth, z.sub_one, z.c_mid), BF16),
                pltpu.VMEM((depth, z.sub_one, z.c_mid), BF16),
                pltpu.VMEM((depth, z.sub_one, z.c_mid), BF16),
                pltpu.VMEM((n * max(z.piece_one, z.piece_two), z.c_mid), BF16),
                pltpu.VMEM((depth, n * z.sub_two, z.c_mid), BF16),
                pltpu.VMEM((n, z.sub_two, z.c_mid), BF16),
                pltpu.VMEM((n, z.sub_two, z.c_mid), BF16),
                pltpu.VMEM((depth, z.sub_two, z.c_mid), BF16),
                dma((24,)),
                dma((2, MICRO)),
                dma((4, MICRO)),
                dma((4, MICRO)),
                dma((2, MICRO)),
                dma((2, n)),
                dma((2, n)),
                dma((2, MICRO * n)),
                dma((2, MICRO * n)),
                dma((4 * MICRO, pair * n)),
                dma((4 * MICRO, pair * n)),
                dma((4 * MICRO, depth)),
                dma((4 * MICRO, depth)),
                dma((14, max(n, depth))),
                dma((14, max(n, depth))),
                dma((max(4, z.images // 8 + 1),)),
            ],
            compiler_params=pltpu.CompilerParams(
                collective_id=0, has_side_effects=True, vmem_limit_bytes=63 * 2**20
            ),
        )(
            image_counts,
            x_turned,
            kernel_one,
            point_one,
            block_one_norm_gains,
            block_one_norm_shifts,
            kernel_two,
            point_two,
            block_two_norm_gains,
            shifts_two,
            cotangent.transpose(0, 2, 1, 3),
        )
        block_out, grad_input, grad_one, grad_two, *small = outs
        block_out = block_out.transpose(0, 2, 1, 3).astype(F32)
        grad_input = grad_input[:, :, : z.in_rows].transpose(0, 2, 1, 3)
        grad_one = grad_one.reshape(-1, z.c_mid)
        grad_kernel_one = grad_one[: 9 * z.c_in].astype(F32).reshape(3, 3, z.c_in, z.c_mid)
        grad_point_one = grad_one[9 * z.c_in : 10 * z.c_in].astype(F32)
        grad_two = grad_two.reshape(pair, -1, z.c_mid)[:, : z.half * z.c_pad]
        grad_two = grad_two.reshape(pair * z.half, z.c_pad, z.c_mid)[:, : z.c_local].astype(F32)
        grad_kernel_two = grad_two[:9].reshape(3, 3, z.c_local, z.c_mid)
        return (
            block_out,
            grad_input,
            grad_kernel_one,
            grad_point_one,
            small[0],
            small[1],
            grad_kernel_two,
            grad_two[9],
            small[2],
            small[3],
        )

    return shards


def solution(mesh):
    placed = (
        P("dp", "shard", None, None),
        P("dp"),
        P(),
        P(),
        P(),
        P(),
        P(None, None, "shard", None),
        P("shard", None),
        P(None, "shard"),
        P(None, "shard"),
        P("dp", None, None, "shard"),
    )
    return jax.shard_map(
        build(mesh),
        mesh=mesh,
        in_specs=placed,
        out_specs=(
            P("dp", None, None, "shard"),
            P("dp", "shard", None, None),
            P(),
            P(),
            P(),
            P(),
            P(None, None, "shard", None),
            P("shard", None),
            P(None, "shard"),
            P(None, "shard"),
        ),
        check_vma=False,
    )
```

```python
import functools

import jax
import jax.numpy as jnp
from jax import lax
from jax.experimental import pallas as pl
from jax.experimental.pallas import tpu as pltpu
from jax.sharding import PartitionSpec as P

MICRO = 2
EPSILON = 1e-05
KEPT = 16
PAYLOAD = 16
MESH = pl.DeviceIdType.MESH
BF16 = jnp.bfloat16
F32 = jnp.float32


def up_to(value, step):
    return (value + step - 1) // step * step


def flat(value):
    return value.reshape(-1, value.shape[-1])


def dot(a, b):
    return jnp.dot(a, b, preferred_element_type=F32)


def dot_nt(a, b):
    return lax.dot_general(a, b, (((1,), (1,)), ((), ())), preferred_element_type=F32)


def dot_tn(a, b):
    return lax.dot_general(a, b, (((0,), (0,)), ((), ())), preferred_element_type=F32)


def eight(value):
    rows, lanes = value.shape
    return jnp.sum(value.reshape(rows // 8, 8, lanes), axis=0)


def sigmoid(value):
    return 0.5 * jnp.tanh(0.5 * value) + 0.5


class Sizes:
    def __init__(self, mesh, x_input, cotangent, point_one):
        self.groups, self.parts = mesh.shape["dp"], mesh.shape["shard"]
        self.images = x_input.shape[0] // self.groups
        self.in_rows = x_input.shape[1] // self.parts
        self.in_cols, self.c_in = x_input.shape[2:]
        self.rows = self.in_rows // 2
        self.cols = self.in_cols // 2
        self.c_mid = point_one.shape[1]
        self.c_local = self.c_mid // self.parts
        self.c_pad = up_to(self.c_local, 16)
        self.held_rows = up_to(self.in_rows, 8)
        self.out_rows = self.rows * self.parts
        self.batch = self.images // MICRO
        self.tile = max(1, min(self.batch, 512 // (self.rows * KEPT)))
        self.tiles = self.images // self.tile
        self.pair = 2 if self.groups % 2 == 0 else 1
        self.depth = self.groups // self.pair
        self.half = -(-10 // self.pair)
        self.sub_two = up_to(self.half * self.c_pad, 16 * self.depth) // self.depth
        self.piece_two = self.sub_two * self.depth
        self.gathered = self.half * self.c_pad
        self.block = int(0.55 * self.gathered) // (16 * self.depth) * 16
        self.plain = self.gathered - self.block * self.depth
        real = 10 * self.c_in
        self.sub_one = up_to(real, 16 * self.depth * self.parts * self.pair) // (
            self.depth * self.parts * self.pair
        )
        self.piece_one = self.sub_one * self.depth


class Sender:
    def __init__(self):
        self.open = []

    def start(self, make, *given, when=None):
        if when is None:
            make(*given).start()
        else:
            pl.when(when)(make(*given).start)
        self.open.append((make, given, when))

    def finish(self):
        for make, given, when in self.open:
            if when is None:
                make(*given).wait_send()
            else:
                pl.when(when)(make(*given).wait_send)
        self.open = []


def kernel(
    z,
    count,
    x_hbm,
    k1_hbm,
    p1_hbm,
    gains_one,
    shifts_one,
    k2_hbm,
    p2_hbm,
    gains_two,
    shifts_two,
    cot_hbm,
    out_hbm,
    grad_in_hbm,
    grad_one_hbm,
    grad_two_hbm,
    grad_gains_one,
    grad_shifts_one,
    grad_gains_two,
    grad_shifts_two,
    odd_win,
    even_win,
    k1_win,
    p1_win,
    z3a,
    z1a,
    x_rim,
    halo,
    wide,
    far,
    near,
    slope,
    mask,
    acc,
    par,
    pay,
    slots_a,
    slots_z,
    totals,
    g_one,
    one_r2,
    one_s,
    one_r3,
    one_r4,
    two_r1,
    two_r2,
    two_s,
    two_r3,
    two_r4,
    local_sem,
    x_sem,
    hid_sem,
    dz_sem,
    e_sem,
    ag_sem,
    ag_pair_sem,
    block_sem,
    cot_sem,
    out_sem,
    ea_send,
    ea_recv,
    ez_send,
    ez_recv,
    ar_one,
    ar_two,
    gi_sem,
):
    n, pair, depth = z.parts, z.pair, z.depth
    rows, c_mid, c_in, tile = z.rows, z.c_mid, z.c_in, z.tile
    batch, images = z.batch, z.images
    dp = lax.axis_index("dp")
    sh = lax.axis_index("shard")
    core = lax.rem(dp, pair)
    deep = lax.div(dp, pair)
    sibling = (dp + 1 - 2 * core, sh)
    me = core * n + sh
    has_above = sh > 0
    has_below = sh < n - 1
    above, below = (dp, sh - 1), (dp, sh + 1)
    per_batch = batch // tile

    def plane(k):
        return lax.rem(sh + k, n)

    def group_peer(k):
        slot = lax.rem(me + k, pair * n)
        return slot, (dp - core + lax.div(slot, n), lax.rem(slot, n))

    def deep_peer(k):
        other = lax.rem(deep + k, depth)
        return other, (other * pair + core, sh)

    def remote(src, dst, send, recv, device):
        return pltpu.make_async_remote_copy(
            src_ref=src,
            dst_ref=dst,
            send_sem=send,
            recv_sem=recv,
            device_id=device,
            device_id_type=MESH,
        )

    barrier = pltpu.get_barrier_semaphore()
    for k in range(1, pair * n):
        pl.semaphore_signal(barrier, 1, device_id=group_peer(k)[1], device_id_type=MESH)
    for k in range(1, depth):
        pl.semaphore_signal(barrier, 1, device_id=deep_peer(k)[1], device_id_type=MESH)

    own_loads = []

    def load(src, dst):
        copy = pltpu.make_async_copy(src, dst, local_sem.at[len(own_loads)])
        copy.start()
        own_loads.append(copy)

    def wide_rows(half, part, offset, length):
        start = (half * n + part) * z.piece_two + offset
        if not isinstance(start, int):
            start = pl.multiple_of(start, 16)
        return wide.at[pl.ds(start, length)]

    taps = [k2_hbm.at[t // 3, t % 3] for t in range(9)] + [p2_hbm]
    for t in range(10):
        load(taps[t], wide_rows(t // z.half, sh, t % z.half * z.c_pad, z.c_pad))
    n_wide = len(own_loads)
    for d in range(3):
        load(k1_hbm.at[d, 1], k1_win.at[d, pl.ds(0, 192)])
        load(k1_hbm.at[d, 0, pl.ds(128, 64)], k1_win.at[d, pl.ds(192, 64)])
        load(k1_hbm.at[d, 0, pl.ds(0, 128)], k1_win.at[d, pl.ds(256, 128)])
        load(k1_hbm.at[d, 2], k1_win.at[d, pl.ds(384, 192)])
    load(p1_hbm, p1_win.at[pl.ds(0, 192)])

    pl.semaphore_wait(barrier, pair * n - 1 + depth - 1)

    sender = Sender()
    gather = Sender()

    def x_copy(b):
        some = pl.ds(b * batch, batch)
        return remote(
            x_rim.at[some], halo.at[0, some], x_sem.at[0, b], x_sem.at[1, b], below
        )

    row_at = lax.broadcasted_iota(jnp.int32, mask.shape, 0) + sh * rows
    col_at = lax.broadcasted_iota(jnp.int32, mask.shape, 1)
    mask[...] = jnp.where((row_at < z.cols) & (col_at < z.cols), 1.0, 0.0)

    @pl.when(jnp.logical_not(has_above))
    def _():
        halo[0] = jnp.zeros(halo.shape[1:], BF16)

    @pl.when(jnp.logical_not(has_below))
    def _():
        halo[1] = jnp.zeros(halo.shape[1:], BF16)

    for d in range(3):
        k1_win[d, 576:640] = jnp.zeros((64, c_mid), BF16)
    p1_win[192:256] = jnp.zeros((64, c_mid), BF16)

    def gather_copy(k, first=0, length=z.plain):
        own = wide_rows(core, sh, first, length)
        return remote(own, own, ag_sem.at[0, k], ag_sem.at[1, sh], (dp, plane(k)))

    def gather_rows(first, last):
        for k in range(1, n):
            gather_copy(k, first, last - first).start()

    def blocks(half, level, part=0, parts=1, levels=1):
        start = ((half * depth + level) * n + part) * z.block
        if not isinstance(start, int):
            start = pl.multiple_of(start, 16)
        return two_r1.at[pl.ds(start, levels * parts * z.block)]

    def block_copy(k):
        return remote(
            wide_rows(core, sh, z.plain + deep * z.block, z.block),
            blocks(core, deep, sh),
            block_sem.at[0, k],
            block_sem.at[1, sh],
            (dp, plane(k)),
        )

    def level_copy(k, part=0, parts=n):
        own = blocks(core, deep, part, parts)
        return remote(own, own, block_sem.at[2, k], block_sem.at[3, deep], deep_peer(k)[1])

    def send_levels(first, last):
        for k in range(1, depth):
            level_copy(k, first, last - first).start()

    def take_blocks():
        blocks(core, deep, sh)[...] = wide_rows(
            core, sh, z.plain + deep * z.block, z.block
        )[...]
        for k in range(1, n):
            part = plane(k)
            there = blocks(core, deep, part)
            remote(there, there, block_sem.at[0, k], block_sem.at[1, part], (dp, part)).wait_recv()

    def level_pass():
        own = blocks(core, 0, 0, n, depth)
        return remote(own, own, block_sem.at[4, 0], block_sem.at[5, 0], sibling)

    def three(value):
        return jnp.concatenate([value] * (c_mid // 128), axis=-1)

    def images_at(t):
        return pl.ds(pl.multiple_of(t * tile, tile), tile)

    def kept(first, count_):
        return mask[first : first + count_][None]

    def mask_of(start, size, first=0, count_=rows):
        shape = (size, count_, KEPT, 128)
        image_at = lax.broadcasted_iota(jnp.int32, shape, 0) + start
        return three(flat(jnp.where(image_at < count[0], kept(first, count_), 0.0)))

    def mask_at(t):
        return mask_of(t * tile, tile)

    def pixels_at():
        return three(flat(jnp.broadcast_to(kept(0, rows), (tile, rows, KEPT, 128))))

    def shaped(value, count_=rows):
        return value.reshape(-1, count_, KEPT, value.shape[-1])

    def add_to(batch_at, at, value):
        acc[batch_at, at] = acc[batch_at, at] + eight(value)

    def group_copy(e, b, k):
        slot, device = group_peer(k)
        some = pl.ds(0, PAYLOAD if e + b == 0 else 8)
        return remote(
            pay.at[e, b, some],
            slots_a.at[e, b, me, some],
            ea_send.at[e * MICRO + b, k],
            ea_recv.at[e * MICRO + b, me],
            device,
        )

    def deep_sum(e, b, k):
        other, device = deep_peer(k)
        some = pl.ds(0, PAYLOAD if e + b == 0 else 8)
        own = slots_z.at[e, b, deep, some]
        return remote(
            own, own, ez_send.at[e * MICRO + b, k], ez_recv.at[e * MICRO + b, deep], device
        )

    def exchange_start(e, b):
        pay[e, b, 0:8] = jnp.sum(acc[b], axis=1)
        length = 8
        if e + b == 0:
            length = PAYLOAD
            lane = lax.broadcasted_iota(jnp.int32, (3, c_mid), 1)
            first = sh * z.c_local
            owned = (lane >= first) & (lane < first + z.c_local) & (dp == 0)
            for at, given in ((8, gains_two), (11, shifts_two)):
                spread_out = jnp.concatenate([given[...]] * n, axis=1)
                pay[e, b, at : at + 3] = jnp.where(owned, spread_out, 0.0)
            pay[e, b, 14:16] = jnp.zeros((2, c_mid), F32)
        slots_a[e, b, me, 0:length] = pay[e, b, 0:length]
        for k in range(1, pair * n):
            group_copy(e, b, k).start()
        acc[b] = jnp.zeros(acc.shape[1:], F32)

    def exchange_pass(e, b):
        at = e * MICRO + b
        length = PAYLOAD if e + b == 0 else 8
        some = pl.ds(0, length)
        for k in range(1, pair * n):
            slot, device = group_peer(k)
            remote(
                pay.at[e, b, some],
                slots_a.at[e, b, slot, some],
                ea_send.at[at, k],
                ea_recv.at[at, slot],
                device,
            ).wait_recv()
        total = slots_a[e, b, 0, 0:length]
        for slot in range(1, pair * n):
            total = total + slots_a[e, b, slot, 0:length]
        slots_z[e, b, deep, 0:length] = total
        for k in range(1, depth):
            deep_sum(e, b, k).start()

    def exchange_end(e, b):
        at = e * MICRO + b
        length = PAYLOAD if e + b == 0 else 8
        some = pl.ds(0, length)
        for k in range(1, depth):
            other, device = deep_peer(k)
            there = slots_z.at[e, b, other, some]
            remote(there, there, ez_send.at[at, k], ez_recv.at[at, other], device).wait_recv()
        total = slots_z[e, b, 0, 0:length]
        for other in range(1, depth):
            total = total + slots_z[e, b, other, 0:length]
        totals[e, b, 0:length] = total
        for k in range(1, pair * n):
            group_copy(e, b, k).wait_send()
        for k in range(1, depth):
            deep_sum(e, b, k).wait_send()

    def moments(e, b, at, pixels):
        center = totals[e, b, at : at + 1] / pixels
        square = totals[e, b, at + 1 : at + 2] / pixels
        return center, lax.rsqrt(square - center * center + EPSILON)

    held = z.held_rows
    group = 4

    def windows(even0, even1, odd0, odd1):
        before0, before1 = pltpu.roll(odd0, 1, 0), pltpu.roll(odd1, 1, 0)
        parts = [even0, even1 + pltpu.roll(before1, 64, 1), before0, odd0, odd1]
        return jnp.concatenate([v.astype(BF16) for v in parts], axis=1)

    def cot_copy(b, k, part=0, parts=1):
        to = plane(k)
        length = batch // parts
        some = pl.ds(b * batch + part * length, length)
        return remote(
            far.at[to, some],
            near.at[sh, some],
            cot_sem.at[0, b * n + k],
            cot_sem.at[1, b * n + sh],
            (dp, to),
        )

    for copy in own_loads[:n_wide]:
        copy.wait()
    if z.block:
        for k in range(1, n):
            block_copy(k).start()
    gather_rows(0, z.plain // 32 * 16)

    def extract_above(i, carry):
        here = pl.ds(i * 8, 8)
        value = flat(halo[0, here]).astype(F32)
        low = lax.broadcasted_iota(jnp.int32, (8 * KEPT, 128), 1) < 64
        mixed = value[:, 256:384]
        even1 = jnp.where(low, mixed, 0.0)
        odd1 = jnp.where(low, pltpu.roll(mixed, 64, 1), 0.0)
        value = windows(value[:, 0:128], even1, value[:, 128:256], odd1)
        odd_win[here, 0] = value.reshape(8, KEPT, 640)
        return carry

    def forward_one(b, first, count_):
        start = b * batch
        here = pl.ds(start, batch)
        side = flat(even_win[here, first : first + count_])
        three_branch = dot(flat(odd_win[here, first : first + count_]), k1_win[0])
        three_branch = three_branch + dot(side, k1_win[1])
        three_branch = three_branch + dot(
            flat(odd_win[here, first + 1 : first + 1 + count_]), k1_win[2]
        )
        point_branch = dot(side[:, 0:256], p1_win[...])
        z3a[here, first : first + count_] = shaped(three_branch, count_)
        z1a[here, first : first + count_] = shaped(point_branch, count_)
        m = mask_of(start, batch, first, count_)
        masked = three_branch * m
        add_to(b, 0, masked)
        add_to(b, 1, masked * three_branch)
        masked = point_branch * m
        add_to(b, 2, masked)
        add_to(b, 3, masked * point_branch)
        add_to(b, 4, m)

    def first_part(x_own, cot_own):
        loads = []
        step = 8
        for at in range(0, images, step):
            copy = pltpu.make_async_copy(
                x_hbm.at[pl.ds(at, step)], x_own.at[pl.ds(at, step)], gi_sem.at[at // step]
            )
            copy.start()
            loads.append(copy)
        cot_load = pltpu.make_async_copy(cot_hbm, cot_own, gi_sem.at[images // step])
        cot_load.start()

        def extract(i, carry):
            here = pl.ds(i * group, group)
            sides = []
            for g in range(group):
                value = x_own[i * group + g].astype(F32).reshape(z.cols, 2, held, c_in)
                none = jnp.zeros((KEPT - z.cols, held, c_in), F32)
                turned = [
                    jnp.swapaxes(jnp.concatenate([value[:, odd], none], axis=0), 0, 1)
                    for odd in (0, 1)
                ]
                sides.append([flat(v[0 : z.in_rows]) for v in turned])
            even, odd = (jnp.concatenate([v[i] for v in sides], axis=0) for i in (0, 1))
            even0, odd0 = even[:, 0:128], odd[:, 0:128]
            even1, odd1 = (jnp.pad(v[:, 128:192], ((0, 0), (0, 64))) for v in (even, odd))
            value = windows(even0, even1, odd0, odd1).reshape(group, rows, 2, KEPT, 640)
            even_win[here] = value[:, :, 0]
            odd_win[here, 1 : rows + 1] = value[:, :, 1]
            rim = jnp.concatenate([even0, odd0, even1 + pltpu.roll(odd1, 64, 1)], axis=1)
            rim = rim.reshape(group, z.in_rows, KEPT, 384)[:, z.in_rows - 1]
            x_rim[here] = rim.astype(BF16)
            return carry

        for at in range(0, images, step):
            loads[at // step].wait()
            lax.fori_loop(at // group, (at + step) // group, extract, 0)
            if (at + step) % batch == 0:
                sender.start(x_copy, at // batch, when=has_below)
            if z.block and at == 0:
                take_blocks()
                send_levels(0, n - 1)

        cot_load.wait()
        out_rows = z.out_rows

        def repack(i, carry):
            value = cot_own[i].astype(F32)
            none = jnp.zeros((KEPT - z.cols, out_rows, z.c_local), F32)
            value = jnp.swapaxes(jnp.concatenate([value, none], axis=0), 0, 1)
            for to in range(n):
                pieces = [value[to * rows + r] for r in range(rows)]
                far[to, i] = jnp.concatenate(pieces, axis=1).astype(BF16)
            return carry


        for copy in own_loads[n_wide:]:
            copy.wait()
        acc[...] = jnp.zeros_like(acc)
        for b in range(MICRO):
            for at in range(1, rows, 2):
                forward_one(b, at, min(2, rows - at))
        for b in range(MICRO):
            pl.when(has_above)(x_copy(b).wait_recv)
            lax.fori_loop(b * batch // 8, (b + 1) * batch // 8, extract_above, 0)
            forward_one(b, 0, 1)
            exchange_start(0, b)
        gather_rows(z.plain // 32 * 16, z.plain)
        lax.fori_loop(0, images // 4, repack, 0)
        for k in range(1, n):
            cot_copy(0, k, 0, 2).start()
        exchange_pass(0, 0)
        lax.fori_loop(images // 4, images // 2, repack, 0)
        exchange_pass(0, 1)
        if z.block:
            send_levels(n - 1, n)
        lax.fori_loop(images // 2, images, repack, 0)
        near[sh] = far[sh]

    pl.run_scoped(
        first_part,
        pltpu.VMEM((images, z.in_cols, held, c_in), BF16),
        pltpu.VMEM((images, z.cols, z.out_rows, z.c_local), BF16),
    )

    def pass_copy(k):
        part = plane(k)
        piece = wide_rows(core, part, 0, z.plain)
        return remote(piece, piece, ag_pair_sem.at[0, k], ag_pair_sem.at[1, part], sibling)

    def norm_one(b):
        pixels = totals[0, b, 4:5]
        center_three, rstd_three = moments(0, b, 0, pixels)
        center_point, rstd_point = moments(0, b, 2, pixels)
        scale_three = gains_one[0:1] * rstd_three
        scale_point = gains_one[1:2] * rstd_point
        par[0, b, 0:1] = scale_three
        par[0, b, 1:2] = scale_point
        par[0, b, 2:3] = (shifts_one[0:1] - center_three * scale_three) + (
            shifts_one[1:2] - center_point * scale_point
        )
        par[0, b, 3:4] = center_three
        par[0, b, 4:5] = center_point
        par[0, b, 5:6] = rstd_three
        par[0, b, 6:7] = rstd_point
        par[0, b, 7:8] = pixels

    def first_sum(here, b, first=0, count_=rows):
        some = slice(first, first + count_)
        return (
            flat(z3a[here, some]) * par[0, b, 0:1]
            + flat(z1a[here, some]) * par[0, b, 1:2]
            + par[0, b, 2:3]
        )

    def put_three(target, here, at, count_, value):
        length = value.shape[0]
        shape = (-1, count_, KEPT, c_mid)
        before = pltpu.roll(value, 1, 0)
        after = pltpu.roll(value, length - 1, 0)
        target[here, at : at + count_, :, 0:c_mid] = before.astype(BF16).reshape(shape)
        target[here, at : at + count_, :, c_mid : 2 * c_mid] = value.astype(BF16).reshape(shape)
        target[here, at : at + count_, :, 2 * c_mid : 3 * c_mid] = after.astype(BF16).reshape(shape)

    def send_rims(source, sems):
        copies = []
        center = pl.ds(c_mid, c_mid)
        for b in range(MICRO):
            some = pl.ds(b * batch, batch)
            copies.append(
                (
                    remote(
                        source.at[some, 1, :, center],
                        halo.at[1, some],
                        sems.at[0, b],
                        sems.at[1, b],
                        above,
                    ),
                    remote(
                        source.at[some, rows, :, center],
                        halo.at[0, some],
                        sems.at[2, b],
                        sems.at[3, b],
                        below,
                    ),
                )
            )
        return copies

    def spread_halo(target, side, b):
        def one(i, carry):
            here = pl.ds(b * batch + i * 8, 8)
            value = flat(halo[side, here]).astype(F32)
            put_three(target, here, 0 if side == 0 else rows + 1, 1, value)
            return carry

        lax.fori_loop(0, batch // 8, one, 0)

    def start_rims(copies, b):
        pl.when(has_above)(copies[b][0].start)
        pl.when(has_below)(copies[b][1].start)

    def take_rims(copies, b):
        pl.when(has_below)(copies[b][0].wait_recv)
        pl.when(has_above)(copies[b][1].wait_recv)

    def close_rims(copies):
        for b in range(MICRO):
            pl.when(has_above)(copies[b][0].wait_send)
            pl.when(has_below)(copies[b][1].wait_send)

    inner = (1, rows - 2) if rows > 2 else None
    outer = sorted({0, rows - 1})

    class Group:
        def __init__(self, size, own, peer):
            self.size, self.own, self.peer = size, own, peer

    by_plane = Group(n, sh, lambda k: (plane(k), (dp, plane(k))))
    by_depth = Group(depth, deep, deep_peer)

    class Reduce:
        def __init__(self, first, second, g, r1, r2, s, r3, r4, sems, sub):
            self.first, self.second = first, second
            self.g, self.r1, self.r2, self.s, self.r3, self.r4 = g, r1, r2, s, r3, r4
            self.sems, self.piece = sems, second.size * sub

        def at(self, half, i):
            start = (half * self.first.size + i) * self.piece
            return pl.ds(pl.multiple_of(start, 16), self.piece)

        def pair_copy(self):
            start = pl.multiple_of((1 - core) * self.first.size * self.piece, 16)
            return remote(
                self.g.at[pl.ds(start, self.first.size * self.piece)],
                self.r1,
                self.sems.at[0, 0],
                self.sems.at[1, 0],
                sibling,
            )

        def start_pair(self):
            if pair == 2:
                sender.start(self.pair_copy)

        def start_first(self):
            if pair == 2:
                self.pair_copy().wait_recv()

                def join(i, carry):
                    at = self.at(core, i)
                    arrived = self.r1[pl.ds(pl.multiple_of(i * self.piece, 16), self.piece)]
                    self.g[at] = (self.g[at].astype(F32) + arrived.astype(F32)).astype(BF16)
                    return carry

                lax.fori_loop(0, self.first.size, join, 0)

            self.r2[self.first.own] = self.g[self.at(core, self.first.own)]

        def first_copy(self, k, part=0, parts=1):
            to, device = self.first.peer(k)
            length = self.piece // parts
            start = (core * self.first.size + to) * self.piece + part * length
            return remote(
                self.g.at[pl.ds(pl.multiple_of(start, 16), length)],
                self.r2.at[self.first.own, pl.ds(part * length, length)],
                self.sems.at[2, k],
                self.sems.at[3, self.first.own],
                device,
            )

        def send_first(self, part, parts):
            for k in range(1, self.first.size):
                self.first_copy(k, part, parts).start()

        def start_second(self):
            for k in range(1, self.first.size):
                other, device = self.first.peer(k)
                there = self.r2.at[other]
                remote(
                    there, there, self.sems.at[2, k], self.sems.at[3, other], device
                ).wait_recv()
                self.first_copy(k).wait_send()
            total = self.r2[0].astype(F32)
            for i in range(1, self.first.size):
                total = total + self.r2[i].astype(F32)
            self.s[...] = total.astype(BF16).reshape(self.s.shape)

            def second_copy(k):
                to, device = self.second.peer(k)
                return remote(
                    self.s.at[to],
                    self.r3.at[self.second.own],
                    self.sems.at[4, k],
                    self.sems.at[5, self.second.own],
                    device,
                )

            for k in range(1, self.second.size):
                sender.start(second_copy, k)
            self.r3[self.second.own] = self.s[self.second.own]

        def start_back(self):
            for k in range(1, self.second.size):
                other, device = self.second.peer(k)
                there = self.r3.at[other]
                remote(
                    there, there, self.sems.at[4, k], self.sems.at[5, other], device
                ).wait_recv()
            total = self.r3[0].astype(F32)
            for i in range(1, self.second.size):
                total = total + self.r3[i].astype(F32)
            self.r4[deep] = total.astype(BF16)

            def back_copy(k):
                own = self.r4.at[deep]
                return remote(
                    own, own, self.sems.at[6, k], self.sems.at[7, deep], deep_peer(k)[1]
                )

            for k in range(1, depth):
                sender.start(back_copy, k)

        def finish_back(self):
            for k in range(1, depth):
                other, device = deep_peer(k)
                there = self.r4.at[other]
                remote(
                    there, there, self.sems.at[6, k], self.sems.at[7, other], device
                ).wait_recv()

    red_two = Reduce(
        by_depth,
        by_plane,
        wide,
        two_r1.at[pl.ds(0, n * z.piece_two)],
        two_r2,
        two_s,
        two_r3,
        two_r4,
        ar_two,
        z.sub_two,
    )
    red_one = Reduce(
        by_plane,
        by_depth,
        g_one,
        two_r1.at[pl.ds(0, n * z.piece_one)],
        one_r2,
        one_s,
        one_r3,
        one_r4,
        ar_one,
        z.sub_one,
    )

    def out_copy(b, k, part=0, parts=1):
        to = plane(k)
        length = batch // parts
        some = pl.ds(b * batch + part * length, length)
        return remote(
            near.at[to, some],
            far.at[sh, some],
            out_sem.at[0, b * n + k],
            out_sem.at[1, b * n + sh],
            (dp, to),
        )

    def send_out(b, part, parts):
        for k in range(1, n):
            out_copy(b, k, part, parts).start()

    def second_part(hid, k2, p2, z3b, dz3, dz1):
        rims = send_rims(hid, hid_sem)

        def make_hidden(t, carry):
            here = images_at(t)
            b = t // per_batch
            total = first_sum(here, b)
            put_three(hid, here, 1, rows, pixels_at() * (total * sigmoid(total)))
            return carry

        for b in range(MICRO):
            exchange_end(0, b)
            norm_one(b)
            lax.fori_loop(b * per_batch, (b + 1) * per_batch, make_hidden, 0)
            start_rims(rims, b)
        for k in range(1, n):
            part = plane(k)
            piece = wide_rows(core, part, 0, z.plain)
            remote(piece, piece, ag_sem.at[0, k], ag_sem.at[1, part], (dp, part)).wait_recv()
            if pair == 2:
                gather.start(pass_copy, k)
        if z.block:
            for k in range(1, depth):
                other, device = deep_peer(k)
                there = blocks(core, other, 0, n)
                remote(
                    there, there, block_sem.at[2, k], block_sem.at[3, other], device
                ).wait_recv()
            if pair == 2:
                gather.start(level_pass)
        if pair == 2:
            for k in range(1, n):
                part = plane(k)
                piece = wide_rows(1 - core, part, 0, z.plain)
                remote(
                    piece, piece, ag_pair_sem.at[0, k], ag_pair_sem.at[1, part], sibling
                ).wait_recv()
            if z.block:
                there = blocks(1 - core, 0, 0, n, depth)
                remote(
                    there, there, block_sem.at[4, 0], block_sem.at[5, 0], sibling
                ).wait_recv()
        gather.finish()
        for k in range(1, n):
            gather_copy(k).wait_send()
        if z.block:
            for k in range(1, n):
                block_copy(k).wait_send()
            for k in range(1, depth):
                level_copy(k).wait_send()
        for t in range(10):
            half, first = t // z.half, t % z.half * z.c_pad
            for part in range(n):
                done = 0
                while done < z.c_local:
                    at = first + done
                    if at < z.plain:
                        length = min(z.plain - at, z.c_local - done)
                        start = (half * n + part) * z.piece_two + at
                        value = wide[start : start + length]
                    else:
                        level, offset = divmod(at - z.plain, z.block)
                        length = min(z.block - offset, z.c_local - done)
                        start = ((half * depth + level) * n + part) * z.block + offset
                        value = two_r1[start : start + length]
                    base = part * z.c_local + done
                    if t < 9:
                        base += t % 3 * c_mid
                        k2[t // 3, base : base + length] = value
                    else:
                        p2[base : base + length] = value
                    done += length

        def forward_two(b, first, count_):
            start = b * batch
            here = pl.ds(start, batch)
            three_branch = dot(flat(hid[here, first : first + count_]), k2[0])
            for d in (1, 2):
                three_branch = three_branch + dot(
                    flat(hid[here, first + d : first + d + count_]), k2[d]
                )
            center = flat(hid[here, first + 1 : first + 1 + count_, :, c_mid : 2 * c_mid])
            point_branch = dot(center, p2[...])
            z3b[here, first : first + count_] = shaped(three_branch, count_)
            m = mask_of(start, batch, first, count_)
            masked = three_branch * m
            add_to(b, 0, masked)
            add_to(b, 1, masked * three_branch)
            masked = point_branch * m
            add_to(b, 2, masked)
            add_to(b, 3, masked * point_branch)
            center = center.astype(F32)
            masked = center * m
            add_to(b, 4, masked)
            add_to(b, 5, masked * center)

        if inner:
            for b in range(MICRO):
                forward_two(b, *inner)
        for b in range(MICRO):
            take_rims(rims, b)
            spread_halo(hid, 0, b)
            spread_halo(hid, 1, b)
            for at in outer:
                forward_two(b, at, 1)
                if b and at == 0:
                    exchange_pass(1, 0)
            exchange_start(1, b)
        for k in range(1, n):
            cot_copy(0, k, 1, 2).start()
        for k in range(1, n):
            cot_copy(1, k).start()

        def norm_two(b):
            pixels = par[0, b, 7:8]
            offset = 0.0
            for i in range(3):
                center, rstd = moments(1, b, 2 * i, pixels)
                scale = totals[0, 0, 8 + i : 9 + i] * rstd
                par[1, b, i : i + 1] = scale
                par[1, b, 4 + i : 5 + i] = center
                par[1, b, 7 + i : 8 + i] = rstd
                offset = offset + (totals[0, 0, 11 + i : 12 + i] - center * scale)
            par[1, b, 3:4] = offset

        def slope_two(t, carry):
            here = images_at(t)
            b = t // per_batch
            taken = [near[part, here] for part in range(n)]
            cot = jnp.stack(
                [
                    jnp.concatenate(
                        [v[:, :, r * z.c_local : (r + 1) * z.c_local] for v in taken], axis=2
                    )
                    for r in range(rows)
                ],
                axis=1,
            )
            v3 = flat(z3b[here])
            vi = flat(hid[here, 1 : rows + 1, :, c_mid : 2 * c_mid])
            v1 = dot(vi, p2[...])
            vi = vi.astype(F32)
            total = (
                v3 * par[1, b, 0:1] + v1 * par[1, b, 1:2] + vi * par[1, b, 2:3] + par[1, b, 3:4]
            )
            m = mask_at(t)
            gate = sigmoid(total)
            down = m * flat(cot).astype(F32) * (gate * (1.0 + total * (1.0 - gate)))
            slope[here] = shaped(down)
            add_to(b, 0, down)
            add_to(b, 1, down * (v3 - par[1, b, 4:5]))
            add_to(b, 2, down * (v1 - par[1, b, 5:6]))
            add_to(b, 3, down * (vi - par[1, b, 6:7]))
            out = shaped((m * (total * gate)).astype(BF16))
            for part in range(n):
                lanes = slice(part * z.c_local, (part + 1) * z.c_local)
                near[part, here] = jnp.concatenate(
                    [out[:, r, :, lanes] for r in range(rows)], axis=2
                )
            return carry

        def block(t):
            return t // 3, slice(t % 3 * c_mid, (t % 3 + 1) * c_mid)

        for t in range(5):
            one, other = k2[block(t)], k2[block(8 - t)]
            k2[block(t)] = other.T
            if t != 4:
                k2[block(8 - t)] = one.T

        for b in range(MICRO):
            exchange_end(1, b)
            norm_two(b)
            for k in range(1, n):
                part = plane(k)
                there = near.at[part, pl.ds(b * batch, batch)]
                remote(
                    there, there, cot_sem.at[0, b * n + k], cot_sem.at[1, b * n + part], (dp, part)
                ).wait_recv()
            for t in range(per_batch):
                slope_two(b * per_batch + t, 0)
                if t == 0:
                    exchange_pass(1, 1) if b == 0 else exchange_pass(2, 0)
            if b == 0:
                for k in range(1, n):
                    cot_copy(0, k).wait_send()
            exchange_start(2, b)
            if b == 0:
                for k in range(1, n):
                    cot_copy(1, k).wait_send()
        send_out(0, 0, 2)
        far[sh] = near[sh]

        def turn_two(b):
            pixels = par[0, b, 7:8]
            slopes = totals[2, b, 0:1]
            for i in range(3):
                rstd = par[1, b, 7 + i : 8 + i]
                cross = totals[2, b, 1 + i : 2 + i] * rstd
                scale = par[1, b, i : i + 1]
                tilt = -scale * rstd * cross / pixels
                par[2, b, 3 * i : 3 * i + 1] = scale
                par[2, b, 3 * i + 1 : 3 * i + 2] = tilt
                par[2, b, 3 * i + 2 : 3 * i + 3] = (
                    -scale * slopes / pixels - tilt * par[1, b, 4 + i : 5 + i]
                )

        rims_back = send_rims(dz3, dz_sem)

        def make_dz(t, carry):
            here = images_at(t)
            b = t // per_batch
            m = mask_at(t)
            down = flat(slope[here])
            value = down * par[2, b, 0:1] + m * (flat(z3b[here]) * par[2, b, 1:2] + par[2, b, 2:3])
            put_three(dz3, here, 1, rows, value)
            v1 = dot(flat(hid[here, 1 : rows + 1, :, c_mid : 2 * c_mid]), p2[...])
            value = down * par[2, b, 3:4] + m * (v1 * par[2, b, 4:5] + par[2, b, 5:6])
            dz1[here] = shaped(value.astype(BF16))
            return carry

        def backward_two(b, first, count_):
            start = b * batch
            here = pl.ds(start, batch)
            some = slice(first, first + count_)
            total = dot_nt(flat(dz1[here, some]), p2[...])
            for k in range(3):
                total = total + dot(flat(dz3[here, first + k : first + k + count_]), k2[k])
            m = mask_of(start, batch, first, count_)
            vi = flat(hid[here, first + 1 : first + 1 + count_, :, c_mid : 2 * c_mid]).astype(F32)
            total = total + (
                flat(slope[here, some]) * par[2, b, 6:7]
                + m * (vi * par[2, b, 7:8] + par[2, b, 8:9])
            )
            total = total.astype(BF16).astype(F32)
            summed = first_sum(here, b, first, count_)
            gate = sigmoid(summed)
            down = m * total * (gate * (1.0 + summed * (1.0 - gate)))
            slope[here, some] = shaped(down, count_)
            add_to(b, 0, down)
            add_to(b, 1, down * (flat(z3a[here, some]) - par[0, b, 3:4]))
            add_to(b, 2, down * (flat(z1a[here, some]) - par[0, b, 4:5]))

        exchange_end(2, 0)
        turn_two(0)
        lax.fori_loop(0, per_batch, make_dz, 0)
        start_rims(rims_back, 0)
        exchange_pass(2, 1)
        if inner:
            backward_two(0, *inner)
        exchange_end(2, 1)
        turn_two(1)
        lax.fori_loop(per_batch, 2 * per_batch, make_dz, 0)
        start_rims(rims_back, 1)

        def mine(value):
            result = jnp.zeros((1, z.c_local), F32)
            for part in range(n):
                here = value[:, part * z.c_local : (part + 1) * z.c_local]
                result = result + jnp.where(sh == part, here, 0.0)
            return result

        shifts = mine(totals[2, 0, 0:1] + totals[2, 1, 0:1])
        for i in range(3):
            cross = [
                totals[2, b, 1 + i : 2 + i] * par[1, b, 7 + i : 8 + i] for b in range(MICRO)
            ]
            grad_gains_two[i : i + 1] = mine(cross[0] + cross[1])
            grad_shifts_two[i : i + 1] = shifts

        def put_two(t, value):
            value = value.astype(BF16)
            half, first = t // z.half, t % z.half * z.c_pad
            for part in range(n):
                done = 0
                while done < z.c_local:
                    block, offset = divmod(first + done, z.sub_two)
                    length = min(z.sub_two - offset, z.c_local - done)
                    start = ((half * depth + block) * n + part) * z.sub_two + offset
                    have = part * z.c_local + done
                    wide[start : start + length] = value[have : have + length]
                    done += length

        center = pl.ds(c_mid, c_mid)
        for d in range(3):
            value = dot_tn(flat(hid[:, d : d + rows]), flat(dz3[:, 1 : rows + 1, :, center]))
            for c in range(3):
                put_two(3 * d + c, value[c * c_mid : (c + 1) * c_mid])
        put_two(9, dot_tn(flat(hid[:, 1 : rows + 1, :, center]), flat(dz1[...])))
        red_two.start_pair()

        if inner:
            backward_two(1, *inner)
        red_two.start_first()
        red_two.send_first(0, n)
        for b in range(MICRO):
            take_rims(rims_back, b)
            spread_halo(dz3, 0, b)
            spread_halo(dz3, 1, b)
            for at in outer:
                backward_two(b, at, 1)
                if b and at == 0:
                    exchange_pass(3, 0)
            exchange_start(3, b)
        send_out(0, 1, 2)
        close_rims(rims)
        close_rims(rims_back)

    pl.run_scoped(
        second_part,
        pltpu.VMEM((images, rows + 2, KEPT, 3 * c_mid), BF16),
        pltpu.VMEM((3, 3 * c_mid, c_mid), BF16),
        pltpu.VMEM((c_mid, c_mid), BF16),
        pltpu.VMEM((images, rows, KEPT, c_mid), F32),
        pltpu.VMEM((images, rows + 2, KEPT, 3 * c_mid), BF16),
        pltpu.VMEM((images, rows, KEPT, c_mid), BF16),
    )

    def third_part(dz3, dz1, one_acc, staged, out_own, turned):
        def turn_one(b):
            pixels = par[0, b, 7:8]
            slopes = totals[3, b, 0:1]
            for i in range(2):
                rstd = par[0, b, 5 + i : 6 + i]
                cross = totals[3, b, 1 + i : 2 + i] * rstd
                scale = par[0, b, i : i + 1]
                tilt = -scale * rstd * cross / pixels
                par[3, b, 3 * i : 3 * i + 1] = scale
                par[3, b, 3 * i + 1 : 3 * i + 2] = tilt
                par[3, b, 3 * i + 2 : 3 * i + 3] = (
                    -scale * slopes / pixels - tilt * par[0, b, 3 + i : 4 + i]
                )

        rims = [
            remote(
                dz3.at[pl.ds(b * batch, batch), 0, :, pl.ds(0, c_mid)],
                halo.at[1, pl.ds(b * batch, batch)],
                e_sem.at[0, b],
                e_sem.at[1, b],
                above,
            )
            for b in range(MICRO)
        ]

        def turn_kernels():
            def tap(d, c):
                if c == 0:
                    return jnp.concatenate([k1_win[d, 256:384], k1_win[d, 192:256]], axis=0)
                return k1_win[d, 0:192] if c == 1 else k1_win[d, 384:576]

            order = [
                [tap(1, 1), p1_win[0:192]],
                [tap(1, 2), tap(1, 0)],
                [tap(2, 1), tap(0, 1)],
                [tap(2, 2), tap(2, 0)],
                [tap(0, 2), tap(0, 0)],
            ]
            for i, both in enumerate(order):
                for j, value in enumerate(both):
                    turned[i, j * c_mid : (j + 1) * c_mid] = value.T

        def make_dz(t, carry):
            here = images_at(t)
            b = t // per_batch
            m = mask_at(t)
            down = flat(slope[here])
            value = down * par[3, b, 0:1] + m * (flat(z3a[here]) * par[3, b, 1:2] + par[3, b, 2:3])
            after = pltpu.roll(value, value.shape[0] - 1, 0)
            dz3[here, 0:rows, :, 0:c_mid] = shaped(value.astype(BF16))
            dz3[here, 0:rows, :, c_mid : 2 * c_mid] = shaped(after.astype(BF16))
            value = down * par[3, b, 3:4] + m * (flat(z1a[here]) * par[3, b, 4:5] + par[3, b, 5:6])
            dz1[here] = shaped(value.astype(BF16))
            return carry

        def place_out(i, carry):
            lines = []
            for part in range(n):
                value = far[part, i].astype(F32)
                lines += [value[:, r * z.c_local : (r + 1) * z.c_local] for r in range(rows)]
            value = jnp.swapaxes(jnp.stack(lines), 0, 1)[0 : z.cols]
            out_own[i] = value.astype(BF16)
            return carry

        def take_out(b):
            for k in range(1, n):
                part = plane(k)
                there = far.at[part, pl.ds(b * batch, batch)]
                remote(
                    there, there, out_sem.at[0, b * n + k], out_sem.at[1, b * n + part], (dp, part)
                ).wait_recv()
                out_copy(b, k).wait_send()
            lax.fori_loop(b * batch, (b + 1) * batch, place_out, 0)

        def put_one(b, base, value):
            there = slice(base, base + value.shape[0])
            if b:
                value = one_acc[there] + value
            if b < MICRO - 1:
                one_acc[there] = value
            else:
                g_one[there] = value.astype(BF16)

        def gradients_one(b):
            some = pl.ds(b * batch, batch)
            own = flat(dz3[some, 0:rows, :, 0:c_mid])
            for d in range(3):
                if d == 1:
                    side = flat(even_win[some])
                else:
                    side = flat(odd_win[some, d // 2 : d // 2 + rows])
                value = dot_tn(side, own)
                base = 3 * d * c_in
                put_one(b, base + c_in, value[0:192])
                put_one(b, base + 128, value[192:256])
                put_one(b, base, value[256:384])
                put_one(b, base + 2 * c_in, value[384:576])
            side = flat(even_win[some, :, :, 0:256])
            put_one(b, 9 * c_in, dot_tn(side, flat(dz1[some]))[0:192])

        if g_one.shape[0] > 10 * c_in:
            g_one[10 * c_in :] = jnp.zeros((g_one.shape[0] - 10 * c_in, c_mid), BF16)
        turn_kernels()
        for b in range(MICRO):
            exchange_end(3, b)
            turn_one(b)
            lax.fori_loop(b * per_batch, (b + 1) * per_batch, make_dz, 0)
            pl.when(has_above)(rims[b].start)
            if b == 0:
                exchange_pass(3, 1)
                for part in range(1, n):
                    red_two.send_first(part, n)
            gradients_one(b)
        shifts = totals[3, 0, 0:1] + totals[3, 1, 0:1]
        for i in range(2):
            cross = [
                totals[3, b, 1 + i : 2 + i] * par[0, b, 5 + i : 6 + i] for b in range(MICRO)
            ]
            grad_gains_one[i : i + 1] = cross[0] + cross[1]
            grad_shifts_one[i : i + 1] = shifts

        red_one.start_pair()
        for b in range(MICRO):
            pl.when(has_below)(rims[b].wait_recv)

        def spread(t, carry):
            here = images_at(t)
            value = flat(halo[1, here]).astype(F32)
            after = pltpu.roll(value, value.shape[0] - 1, 0)
            dz3[here, rows, :, 0:c_mid] = value.astype(BF16).reshape(tile, KEPT, c_mid)
            dz3[here, rows, :, c_mid : 2 * c_mid] = after.astype(BF16).reshape(tile, KEPT, c_mid)
            return carry

        lax.fori_loop(0, z.tiles, spread, 0)
        red_one.start_first()
        red_one.send_first(0, 1)
        send_out(1, 0, 2)
        send_out(1, 1, 2)

        some = staged.shape[1]
        steps = images // some

        def staged_copy(i, slot):
            return pltpu.make_async_copy(
                staged.at[slot],
                grad_in_hbm.at[pl.ds(i * some, some)],
                gi_sem.at[slot],
            )

        def input_grad(i, carry):
            here = pl.ds(i * some, some)
            slot = lax.rem(i, 2)
            own = flat(dz3[here, 0:rows])
            after = flat(dz3[here, 1 : rows + 1])
            own_c, after_c = own[:, 0:c_mid], after[:, 0:c_mid]
            value = [
                [
                    dot(own_c, turned[0, 0:c_mid]) + dot(flat(dz1[here]), turned[0, c_mid:]),
                    dot(own, turned[1]),
                ],
                [
                    dot(own_c, turned[2, 0:c_mid]) + dot(after_c, turned[2, c_mid:]),
                    dot(own, turned[3]) + dot(after, turned[4]),
                ],
            ]

            @pl.when(i >= 2)
            def _():
                staged_copy(i, slot).wait()

            none = [jnp.zeros((KEPT, c_in), F32)] * (held - z.in_rows)
            for g in range(some):
                sides = []
                for c in range(2):
                    lines = [
                        value[r][c].reshape(some, rows, KEPT, c_in)[g, at]
                        for at in range(rows)
                        for r in range(2)
                    ]
                    sides.append(jnp.swapaxes(jnp.stack(lines + none), 0, 1)[0 : z.cols])
                staged[slot, g] = jnp.stack(sides, axis=1).reshape(z.in_cols, held, c_in)
            staged_copy(i, slot).start()
            return carry

        cuts = [0, 0, steps - steps // 4, steps]
        lax.fori_loop(cuts[0], cuts[2], input_grad, 0)
        red_one.start_second()
        lax.fori_loop(cuts[2], cuts[3], input_grad, 0)
        take_out(0)
        red_one.start_back()
        take_out(1)
        out_write = pltpu.make_async_copy(out_own, out_hbm, gi_sem.at[2])
        out_write.start()
        for i in range(max(0, steps - 2), steps):
            staged_copy(i, i % 2).wait()
        out_write.wait()
        for b in range(MICRO):
            pl.when(has_above)(rims[b].wait_send)

    some = max(1, min(images // 2, 256 // (rows * KEPT)))
    pl.run_scoped(
        third_part,
        pltpu.VMEM((images, rows + 1, KEPT, 2 * c_mid), BF16),
        pltpu.VMEM((images, rows, KEPT, c_mid), BF16),
        pltpu.VMEM((10 * z.c_in, c_mid), F32),
        pltpu.VMEM((2, some, z.in_cols, held, c_in), F32),
        pltpu.VMEM((images, z.cols, z.out_rows, z.c_local), BF16),
        pltpu.VMEM((5, 2 * c_mid, c_in), BF16),
    )

    red_two.start_second()
    red_one.finish_back()
    def one_at(half, part):
        return grad_one_hbm.at[half, part]

    one_own = pltpu.make_async_copy(red_one.r4, one_at(core, sh), ar_one.at[8, 0])
    one_own.start()

    def one_pair_copy():
        return remote(
            red_one.r4, one_at(core, sh), ar_one.at[12, 0], ar_one.at[13, sh], sibling
        )

    def one_plane_copy(k):
        return remote(
            red_one.r4, one_at(core, sh), ar_one.at[9, k], ar_one.at[10, sh], (dp, plane(k))
        )

    def one_pass_copy(k):
        part = plane(k)
        at = one_at(core, part)
        return remote(at, at, ar_one.at[11, k], ar_one.at[13, part], sibling)

    if pair == 2:
        sender.start(one_pair_copy)
    for k in range(1, n):
        sender.start(one_plane_copy, k)
    red_two.start_back()
    red_two.finish_back()
    two_at = grad_two_hbm.at[core]
    two_own = pltpu.make_async_copy(red_two.r4, two_at, ar_two.at[8, 0])
    two_own.start()
    two_pair = remote(red_two.r4, two_at, ar_two.at[9, 0], ar_two.at[10, 0], sibling)
    if pair == 2:
        two_pair.start()
    for k in range(1, n):
        part = plane(k)
        at = one_at(core, part)
        remote(at, at, ar_one.at[9, k], ar_one.at[10, part], (dp, part)).wait_recv()
        if pair == 2:
            sender.start(one_pass_copy, k)
    if pair == 2:
        for k in range(n):
            part = plane(k)
            at = one_at(1 - core, part)
            remote(at, at, ar_one.at[11, k], ar_one.at[13, part], sibling).wait_recv()
        two_pair.wait_send()
        remote(
            red_two.r4, grad_two_hbm.at[1 - core], ar_two.at[9, 0], ar_two.at[10, 0], sibling
        ).wait_recv()
    two_own.wait()
    one_own.wait()
    sender.finish()


def build(mesh):
    def shards(
        x_input,
        image_counts,
        kernel_one,
        point_one,
        block_one_norm_gains,
        block_one_norm_shifts,
        kernel_two,
        point_two,
        block_two_norm_gains,
        shifts_two,
        cotangent,
    ):
        z = Sizes.__new__(Sizes)
        whole_x = jax.ShapeDtypeStruct(
            (
                x_input.shape[0] * mesh.shape["dp"],
                x_input.shape[1] * mesh.shape["shard"],
                *x_input.shape[2:],
            ),
            x_input.dtype,
        )
        z.__init__(mesh, whole_x, cotangent, point_one)
        n, pair, depth = z.parts, z.pair, z.depth
        x_turned = x_input.transpose(0, 2, 1, 3)
        if z.held_rows != z.in_rows:
            more = z.held_rows - z.in_rows
            x_turned = jnp.pad(x_turned, ((0, 0), (0, 0), (0, more), (0, 0)))
        if z.c_pad != z.c_local:
            more = z.c_pad - z.c_local
            kernel_two = jnp.pad(kernel_two, ((0, 0), (0, 0), (0, more), (0, 0)))
            point_two = jnp.pad(point_two, ((0, more), (0, 0)))

        vmem = pl.BlockSpec(memory_space=pltpu.VMEM)
        anywhere = pl.BlockSpec(memory_space=pl.ANY)
        image_rows = (z.images, z.rows, KEPT)
        dma = pltpu.SemaphoreType.DMA
        outs = pl.pallas_call(
            functools.partial(kernel, z),
            out_shape=(
                jax.ShapeDtypeStruct((z.images, z.cols, z.out_rows, z.c_local), BF16),
                jax.ShapeDtypeStruct((z.images, z.in_cols, z.held_rows, z.c_in), F32),
                jax.ShapeDtypeStruct((pair, n, depth, z.sub_one, z.c_mid), BF16),
                jax.ShapeDtypeStruct((pair, depth, z.sub_two, z.c_mid), BF16),
                jax.ShapeDtypeStruct((2, z.c_mid), F32),
                jax.ShapeDtypeStruct((2, z.c_mid), F32),
                jax.ShapeDtypeStruct((3, z.c_local), F32),
                jax.ShapeDtypeStruct((3, z.c_local), F32),
            ),
            in_specs=[
                pl.BlockSpec(memory_space=pltpu.SMEM),
                anywhere,
                anywhere,
                anywhere,
                vmem,
                vmem,
                anywhere,
                anywhere,
                vmem,
                vmem,
                anywhere,
            ],
            out_specs=(anywhere, anywhere, anywhere, anywhere, vmem, vmem, vmem, vmem),
            scratch_shapes=[
                pltpu.VMEM((z.images, z.rows + 1, KEPT, 640), BF16),
                pltpu.VMEM((*image_rows, 640), BF16),
                pltpu.VMEM((3, 640, z.c_mid), BF16),
                pltpu.VMEM((256, z.c_mid), BF16),
                pltpu.VMEM((*image_rows, z.c_mid), F32),
                pltpu.VMEM((*image_rows, z.c_mid), F32),
                pltpu.VMEM((z.images, KEPT, z.c_mid), BF16),
                pltpu.VMEM((2, z.images, KEPT, z.c_mid), BF16),
                pltpu.VMEM((pair * n * z.piece_two, z.c_mid), BF16),
                pltpu.VMEM((n, z.images, KEPT, z.rows * z.c_local), BF16),
                pltpu.VMEM((n, z.images, KEPT, z.rows * z.c_local), BF16),
                pltpu.VMEM((*image_rows, z.c_mid), F32),
                pltpu.VMEM((z.rows, KEPT, 128), F32),
                pltpu.VMEM((MICRO, 8, 8, z.c_mid), F32),
                pltpu.VMEM((4, MICRO, 16, z.c_mid), F32),
                pltpu.VMEM((4, MICRO, PAYLOAD, z.c_mid), F32),
                pltpu.VMEM((4, MICRO, pair * n, PAYLOAD, z.c_mid), F32),
                pltpu.VMEM((4, MICRO, depth, PAYLOAD, z.c_mid), F32),
                pltpu.VMEM((4, MICRO, PAYLOAD, z.c_mid), F32),
                pltpu.VMEM((pair * n * z.piece_one, z.c_mid), BF16),
                pltpu.VMEM((n, z.piece_one, z.c_mid), BF16),
                pltpu.VMEM((depth, z.sub_one, z.c_mid), BF16),
                pltpu.VMEM((depth, z.sub_one, z.c_mid), BF16),
                pltpu.VMEM((depth, z.sub_one, z.c_mid), BF16),
                pltpu.VMEM((n * max(z.piece_one, z.piece_two), z.c_mid), BF16),
                pltpu.VMEM((depth, n * z.sub_two, z.c_mid), BF16),
                pltpu.VMEM((n, z.sub_two, z.c_mid), BF16),
                pltpu.VMEM((n, z.sub_two, z.c_mid), BF16),
                pltpu.VMEM((depth, z.sub_two, z.c_mid), BF16),
                dma((24,)),
                dma((2, MICRO)),
                dma((4, MICRO)),
                dma((4, MICRO)),
                dma((2, MICRO)),
                dma((2, n)),
                dma((2, n)),
                dma((6, max(n, depth))),
                dma((2, MICRO * n)),
                dma((2, MICRO * n)),
                dma((4 * MICRO, pair * n)),
                dma((4 * MICRO, pair * n)),
                dma((4 * MICRO, depth)),
                dma((4 * MICRO, depth)),
                dma((14, max(n, depth))),
                dma((14, max(n, depth))),
                dma((max(4, z.images // 8 + 1),)),
            ],
            compiler_params=pltpu.CompilerParams(
                collective_id=0, has_side_effects=True, vmem_limit_bytes=63 * 2**20
            ),
        )(
            image_counts,
            x_turned,
            kernel_one,
            point_one,
            block_one_norm_gains,
            block_one_norm_shifts,
            kernel_two,
            point_two,
            block_two_norm_gains,
            shifts_two,
            cotangent.transpose(0, 2, 1, 3),
        )
        block_out, grad_input, grad_one, grad_two, *small = outs
        block_out = block_out.transpose(0, 2, 1, 3).astype(F32)
        grad_input = grad_input[:, :, : z.in_rows].transpose(0, 2, 1, 3)
        grad_one = grad_one.reshape(-1, z.c_mid)
        grad_kernel_one = grad_one[: 9 * z.c_in].astype(F32).reshape(3, 3, z.c_in, z.c_mid)
        grad_point_one = grad_one[9 * z.c_in : 10 * z.c_in].astype(F32)
        grad_two = grad_two.reshape(pair, -1, z.c_mid)[:, : z.half * z.c_pad]
        grad_two = grad_two.reshape(pair * z.half, z.c_pad, z.c_mid)[:, : z.c_local].astype(F32)
        grad_kernel_two = grad_two[:9].reshape(3, 3, z.c_local, z.c_mid)
        return (
            block_out,
            grad_input,
            grad_kernel_one,
            grad_point_one,
            small[0],
            small[1],
            grad_kernel_two,
            grad_two[9],
            small[2],
            small[3],
        )

    return shards


def solution(mesh):
    placed = (
        P("dp", "shard", None, None),
        P("dp"),
        P(),
        P(),
        P(),
        P(),
        P(None, None, "shard", None),
        P("shard", None),
        P(None, "shard"),
        P(None, "shard"),
        P("dp", None, None, "shard"),
    )
    return jax.shard_map(
        build(mesh),
        mesh=mesh,
        in_specs=placed,
        out_specs=(
            P("dp", None, None, "shard"),
            P("dp", "shard", None, None),
            P(),
            P(),
            P(),
            P(),
            P(None, None, "shard", None),
            P("shard", None),
            P(None, "shard"),
            P(None, "shard"),
        ),
        check_vma=False,
    )
```

```python
import functools

import jax
import jax.numpy as jnp
from jax import lax
from jax.experimental import pallas as pl
from jax.experimental.pallas import tpu as pltpu
from jax.sharding import PartitionSpec as P

MICRO = 2
EPSILON = 1e-05
KEPT = 16
PAYLOAD = 16
MESH = pl.DeviceIdType.MESH
BF16 = jnp.bfloat16
F32 = jnp.float32


def up_to(value, step):
    return (value + step - 1) // step * step


def flat(value):
    return value.reshape(-1, value.shape[-1])


def dot(a, b):
    return jnp.dot(a, b, preferred_element_type=F32)


def dot_nt(a, b):
    return lax.dot_general(a, b, (((1,), (1,)), ((), ())), preferred_element_type=F32)


def dot_tn(a, b):
    return lax.dot_general(a, b, (((0,), (0,)), ((), ())), preferred_element_type=F32)


def eight(value):
    rows, lanes = value.shape
    return jnp.sum(value.reshape(rows // 8, 8, lanes), axis=0)


def sigmoid(value):
    return 0.5 * jnp.tanh(0.5 * value) + 0.5


class Sizes:
    def __init__(self, mesh, x_input, cotangent, point_one):
        self.groups, self.parts = mesh.shape["dp"], mesh.shape["shard"]
        self.images = x_input.shape[0] // self.groups
        self.in_rows = x_input.shape[1] // self.parts
        self.in_cols, self.c_in = x_input.shape[2:]
        self.rows = self.in_rows // 2
        self.cols = self.in_cols // 2
        self.c_mid = point_one.shape[1]
        self.c_local = self.c_mid // self.parts
        self.c_pad = up_to(self.c_local, 16)
        self.held_rows = up_to(self.in_rows, 8)
        self.out_rows = self.rows * self.parts
        self.batch = self.images // MICRO
        self.tile = max(1, min(self.batch, 512 // (self.rows * KEPT)))
        self.tiles = self.images // self.tile
        self.pair = 2 if self.groups % 2 == 0 else 1
        self.depth = self.groups // self.pair
        self.half = -(-10 // self.pair)
        self.sub_two = up_to(self.half * self.c_pad, 16 * self.depth) // self.depth
        self.piece_two = self.sub_two * self.depth
        self.gathered = self.half * self.c_pad
        self.block = int(0.55 * self.gathered) // (16 * self.depth) * 16
        self.plain = self.gathered - self.block * self.depth
        real = 10 * self.c_in
        self.sub_one = up_to(real, 16 * self.depth * self.parts * self.pair) // (
            self.depth * self.parts * self.pair
        )
        self.piece_one = self.sub_one * self.depth


class Sender:
    def __init__(self):
        self.open = []

    def start(self, make, *given, when=None):
        if when is None:
            make(*given).start()
        else:
            pl.when(when)(make(*given).start)
        self.open.append((make, given, when))

    def finish(self):
        for make, given, when in self.open:
            if when is None:
                make(*given).wait_send()
            else:
                pl.when(when)(make(*given).wait_send)
        self.open = []


def kernel(
    z,
    count,
    x_hbm,
    k1_hbm,
    p1_hbm,
    gains_one,
    shifts_one,
    k2_hbm,
    p2_hbm,
    gains_two,
    shifts_two,
    cot_hbm,
    out_hbm,
    grad_in_hbm,
    grad_one_hbm,
    grad_two_hbm,
    grad_gains_one,
    grad_shifts_one,
    grad_gains_two,
    grad_shifts_two,
    odd_win,
    even_win,
    k1_win,
    p1_win,
    z3a,
    z1a,
    x_rim,
    halo,
    wide,
    far,
    near,
    slope,
    mask,
    acc,
    par,
    pay,
    slots_a,
    slots_z,
    totals,
    g_one,
    one_r2,
    one_s,
    one_r3,
    one_r4,
    two_r1,
    two_r2,
    two_s,
    two_r3,
    two_r4,
    local_sem,
    x_sem,
    hid_sem,
    dz_sem,
    e_sem,
    ag_sem,
    ag_pair_sem,
    block_sem,
    cot_sem,
    out_sem,
    ea_send,
    ea_recv,
    ez_send,
    ez_recv,
    ar_one,
    ar_two,
    gi_sem,
):
    n, pair, depth = z.parts, z.pair, z.depth
    rows, c_mid, c_in, tile = z.rows, z.c_mid, z.c_in, z.tile
    batch, images = z.batch, z.images
    dp = lax.axis_index("dp")
    sh = lax.axis_index("shard")
    core = lax.rem(dp, pair)
    deep = lax.div(dp, pair)
    sibling = (dp + 1 - 2 * core, sh)
    me = core * n + sh
    has_above = sh > 0
    has_below = sh < n - 1
    above, below = (dp, sh - 1), (dp, sh + 1)
    per_batch = batch // tile

    def plane(k):
        return lax.rem(sh + k, n)

    def group_peer(k):
        slot = lax.rem(me + k, pair * n)
        return slot, (dp - core + lax.div(slot, n), lax.rem(slot, n))

    def deep_peer(k):
        other = lax.rem(deep + k, depth)
        return other, (other * pair + core, sh)

    def remote(src, dst, send, recv, device):
        return pltpu.make_async_remote_copy(
            src_ref=src,
            dst_ref=dst,
            send_sem=send,
            recv_sem=recv,
            device_id=device,
            device_id_type=MESH,
        )

    barrier = pltpu.get_barrier_semaphore()
    for k in range(1, pair * n):
        pl.semaphore_signal(barrier, 1, device_id=group_peer(k)[1], device_id_type=MESH)
    for k in range(1, depth):
        pl.semaphore_signal(barrier, 1, device_id=deep_peer(k)[1], device_id_type=MESH)

    own_loads = []

    def load(src, dst):
        copy = pltpu.make_async_copy(src, dst, local_sem.at[len(own_loads)])
        copy.start()
        own_loads.append(copy)

    def wide_rows(half, part, offset, length):
        start = (half * n + part) * z.piece_two + offset
        if not isinstance(start, int):
            start = pl.multiple_of(start, 16)
        return wide.at[pl.ds(start, length)]

    taps = [k2_hbm.at[t // 3, t % 3] for t in range(9)] + [p2_hbm]
    for t in range(10):
        load(taps[t], wide_rows(t // z.half, sh, t % z.half * z.c_pad, z.c_pad))
    n_wide = len(own_loads)
    for d in range(3):
        load(k1_hbm.at[d, 1], k1_win.at[d, pl.ds(0, 192)])
        load(k1_hbm.at[d, 0, pl.ds(128, 64)], k1_win.at[d, pl.ds(192, 64)])
        load(k1_hbm.at[d, 0, pl.ds(0, 128)], k1_win.at[d, pl.ds(256, 128)])
        load(k1_hbm.at[d, 2], k1_win.at[d, pl.ds(384, 192)])
    load(p1_hbm, p1_win.at[pl.ds(0, 192)])

    pl.semaphore_wait(barrier, pair * n - 1 + depth - 1)

    sender = Sender()
    gather = Sender()

    def x_copy(b):
        some = pl.ds(b * batch, batch)
        return remote(
            x_rim.at[some], halo.at[0, some], x_sem.at[0, b], x_sem.at[1, b], below
        )

    row_at = lax.broadcasted_iota(jnp.int32, mask.shape, 0) + sh * rows
    col_at = lax.broadcasted_iota(jnp.int32, mask.shape, 1)
    mask[...] = jnp.where((row_at < z.cols) & (col_at < z.cols), 1.0, 0.0)

    @pl.when(jnp.logical_not(has_above))
    def _():
        halo[0] = jnp.zeros(halo.shape[1:], BF16)

    @pl.when(jnp.logical_not(has_below))
    def _():
        halo[1] = jnp.zeros(halo.shape[1:], BF16)

    for d in range(3):
        k1_win[d, 576:640] = jnp.zeros((64, c_mid), BF16)
    p1_win[192:256] = jnp.zeros((64, c_mid), BF16)

    def gather_copy(k, first=0, length=z.plain):
        own = wide_rows(core, sh, first, length)
        return remote(own, own, ag_sem.at[0, k], ag_sem.at[1, sh], (dp, plane(k)))

    def gather_rows(first, last):
        for k in range(1, n):
            gather_copy(k, first, last - first).start()

    def blocks(half, level, part=0, parts=1, levels=1):
        start = ((half * depth + level) * n + part) * z.block
        if not isinstance(start, int):
            start = pl.multiple_of(start, 16)
        return two_r1.at[pl.ds(start, levels * parts * z.block)]

    def block_copy(k):
        return remote(
            wide_rows(core, sh, z.plain + deep * z.block, z.block),
            blocks(core, deep, sh),
            block_sem.at[0, k],
            block_sem.at[1, sh],
            (dp, plane(k)),
        )

    def level_copy(k, part=0, parts=n):
        own = blocks(core, deep, part, parts)
        return remote(own, own, block_sem.at[2, k], block_sem.at[3, deep], deep_peer(k)[1])

    def send_levels(first, last):
        for k in range(1, depth):
            level_copy(k, first, last - first).start()

    def take_blocks():
        blocks(core, deep, sh)[...] = wide_rows(
            core, sh, z.plain + deep * z.block, z.block
        )[...]
        for k in range(1, n):
            part = plane(k)
            there = blocks(core, deep, part)
            remote(there, there, block_sem.at[0, k], block_sem.at[1, part], (dp, part)).wait_recv()

    def level_pass():
        own = blocks(core, 0, 0, n, depth)
        return remote(own, own, block_sem.at[4, 0], block_sem.at[5, 0], sibling)

    def three(value):
        return jnp.concatenate([value] * (c_mid // 128), axis=-1)

    def images_at(t):
        return pl.ds(pl.multiple_of(t * tile, tile), tile)

    def kept(first, count_):
        return mask[first : first + count_][None]

    def mask_of(start, size, first=0, count_=rows):
        shape = (size, count_, KEPT, 128)
        image_at = lax.broadcasted_iota(jnp.int32, shape, 0) + start
        return three(flat(jnp.where(image_at < count[0], kept(first, count_), 0.0)))

    def mask_at(t):
        return mask_of(t * tile, tile)

    def pixels_at():
        return three(flat(jnp.broadcast_to(kept(0, rows), (tile, rows, KEPT, 128))))

    def shaped(value, count_=rows):
        return value.reshape(-1, count_, KEPT, value.shape[-1])

    def add_to(batch_at, at, value):
        acc[batch_at, at] = acc[batch_at, at] + eight(value)

    def group_copy(e, b, k):
        slot, device = group_peer(k)
        some = pl.ds(0, PAYLOAD if e + b == 0 else 8)
        return remote(
            pay.at[e, b, some],
            slots_a.at[e, b, me, some],
            ea_send.at[e * MICRO + b, k],
            ea_recv.at[e * MICRO + b, me],
            device,
        )

    def deep_sum(e, b, k):
        other, device = deep_peer(k)
        some = pl.ds(0, PAYLOAD if e + b == 0 else 8)
        own = slots_z.at[e, b, deep, some]
        return remote(
            own, own, ez_send.at[e * MICRO + b, k], ez_recv.at[e * MICRO + b, deep], device
        )

    def exchange_start(e, b):
        pay[e, b, 0:8] = jnp.sum(acc[b], axis=1)
        length = 8
        if e + b == 0:
            length = PAYLOAD
            lane = lax.broadcasted_iota(jnp.int32, (3, c_mid), 1)
            first = sh * z.c_local
            owned = (lane >= first) & (lane < first + z.c_local) & (dp == 0)
            for at, given in ((8, gains_two), (11, shifts_two)):
                spread_out = jnp.concatenate([given[...]] * n, axis=1)
                pay[e, b, at : at + 3] = jnp.where(owned, spread_out, 0.0)
            pay[e, b, 14:16] = jnp.zeros((2, c_mid), F32)
        slots_a[e, b, me, 0:length] = pay[e, b, 0:length]
        for k in range(1, pair * n):
            group_copy(e, b, k).start()
        acc[b] = jnp.zeros(acc.shape[1:], F32)

    def exchange_pass(e, b):
        at = e * MICRO + b
        length = PAYLOAD if e + b == 0 else 8
        some = pl.ds(0, length)
        for k in range(1, pair * n):
            slot, device = group_peer(k)
            remote(
                pay.at[e, b, some],
                slots_a.at[e, b, slot, some],
                ea_send.at[at, k],
                ea_recv.at[at, slot],
                device,
            ).wait_recv()
        total = slots_a[e, b, 0, 0:length]
        for slot in range(1, pair * n):
            total = total + slots_a[e, b, slot, 0:length]
        slots_z[e, b, deep, 0:length] = total
        for k in range(1, depth):
            deep_sum(e, b, k).start()

    def exchange_end(e, b):
        at = e * MICRO + b
        length = PAYLOAD if e + b == 0 else 8
        some = pl.ds(0, length)
        for k in range(1, depth):
            other, device = deep_peer(k)
            there = slots_z.at[e, b, other, some]
            remote(there, there, ez_send.at[at, k], ez_recv.at[at, other], device).wait_recv()
        total = slots_z[e, b, 0, 0:length]
        for other in range(1, depth):
            total = total + slots_z[e, b, other, 0:length]
        totals[e, b, 0:length] = total
        for k in range(1, pair * n):
            group_copy(e, b, k).wait_send()
        for k in range(1, depth):
            deep_sum(e, b, k).wait_send()

    def moments(e, b, at, pixels):
        center = totals[e, b, at : at + 1] / pixels
        square = totals[e, b, at + 1 : at + 2] / pixels
        return center, lax.rsqrt(square - center * center + EPSILON)

    held = z.held_rows
    group = 4

    def windows(even0, even1, odd0, odd1):
        before0, before1 = pltpu.roll(odd0, 1, 0), pltpu.roll(odd1, 1, 0)
        parts = [even0, even1 + pltpu.roll(before1, 64, 1), before0, odd0, odd1]
        return jnp.concatenate([v.astype(BF16) for v in parts], axis=1)

    def cot_copy(b, k, part=0, parts=1):
        to = plane(k)
        length = batch // parts
        some = pl.ds(b * batch + part * length, length)
        return remote(
            far.at[to, some],
            near.at[sh, some],
            cot_sem.at[0, b * n + k],
            cot_sem.at[1, b * n + sh],
            (dp, to),
        )

    for copy in own_loads[:n_wide]:
        copy.wait()
    if z.block:
        for k in range(1, n):
            block_copy(k).start()
    gather_rows(0, z.plain // 32 * 16)

    def extract_above(i, carry):
        here = pl.ds(i * 8, 8)
        value = flat(halo[0, here]).astype(F32)
        low = lax.broadcasted_iota(jnp.int32, (8 * KEPT, 128), 1) < 64
        mixed = value[:, 256:384]
        even1 = jnp.where(low, mixed, 0.0)
        odd1 = jnp.where(low, pltpu.roll(mixed, 64, 1), 0.0)
        value = windows(value[:, 0:128], even1, value[:, 128:256], odd1)
        odd_win[here, 0] = value.reshape(8, KEPT, 640)
        return carry

    def forward_one(b, first, count_):
        start = b * batch
        here = pl.ds(start, batch)
        side = flat(even_win[here, first : first + count_])
        three_branch = dot(flat(odd_win[here, first : first + count_]), k1_win[0])
        three_branch = three_branch + dot(side, k1_win[1])
        three_branch = three_branch + dot(
            flat(odd_win[here, first + 1 : first + 1 + count_]), k1_win[2]
        )
        point_branch = dot(side[:, 0:256], p1_win[...])
        z3a[here, first : first + count_] = shaped(three_branch, count_)
        z1a[here, first : first + count_] = shaped(point_branch, count_)
        m = mask_of(start, batch, first, count_)
        masked = three_branch * m
        add_to(b, 0, masked)
        add_to(b, 1, masked * three_branch)
        masked = point_branch * m
        add_to(b, 2, masked)
        add_to(b, 3, masked * point_branch)
        add_to(b, 4, m)

    def first_part(x_own, cot_own):
        loads = []
        step = 8
        for at in range(0, images, step):
            copy = pltpu.make_async_copy(
                x_hbm.at[pl.ds(at, step)], x_own.at[pl.ds(at, step)], gi_sem.at[at // step]
            )
            copy.start()
            loads.append(copy)
        cot_load = pltpu.make_async_copy(cot_hbm, cot_own, gi_sem.at[images // step])
        cot_load.start()

        def extract(i, carry):
            here = pl.ds(i * group, group)
            sides = []
            for g in range(group):
                value = x_own[i * group + g].astype(F32).reshape(z.cols, 2, held, c_in)
                none = jnp.zeros((KEPT - z.cols, held, c_in), F32)
                turned = [
                    jnp.swapaxes(jnp.concatenate([value[:, odd], none], axis=0), 0, 1)
                    for odd in (0, 1)
                ]
                sides.append([flat(v[0 : z.in_rows]) for v in turned])
            even, odd = (jnp.concatenate([v[i] for v in sides], axis=0) for i in (0, 1))
            even0, odd0 = even[:, 0:128], odd[:, 0:128]
            even1, odd1 = (jnp.pad(v[:, 128:192], ((0, 0), (0, 64))) for v in (even, odd))
            value = windows(even0, even1, odd0, odd1).reshape(group, rows, 2, KEPT, 640)
            even_win[here] = value[:, :, 0]
            odd_win[here, 1 : rows + 1] = value[:, :, 1]
            rim = jnp.concatenate([even0, odd0, even1 + pltpu.roll(odd1, 64, 1)], axis=1)
            rim = rim.reshape(group, z.in_rows, KEPT, 384)[:, z.in_rows - 1]
            x_rim[here] = rim.astype(BF16)
            return carry

        for at in range(0, images, step):
            loads[at // step].wait()
            lax.fori_loop(at // group, (at + step) // group, extract, 0)
            if (at + step) % batch == 0:
                sender.start(x_copy, at // batch, when=has_below)
            if z.block and at == 0:
                take_blocks()
                send_levels(0, n - 1)

        cot_load.wait()
        out_rows = z.out_rows

        def repack(i, carry):
            value = cot_own[i].astype(F32)
            none = jnp.zeros((KEPT - z.cols, out_rows, z.c_local), F32)
            value = jnp.swapaxes(jnp.concatenate([value, none], axis=0), 0, 1)
            for to in range(n):
                pieces = [value[to * rows + r] for r in range(rows)]
                far[to, i] = jnp.concatenate(pieces, axis=1).astype(BF16)
            return carry


        for copy in own_loads[n_wide:]:
            copy.wait()
        acc[...] = jnp.zeros_like(acc)
        for b in range(MICRO):
            for at in range(1, rows, 2):
                forward_one(b, at, min(2, rows - at))
        for b in range(MICRO):
            pl.when(has_above)(x_copy(b).wait_recv)
            lax.fori_loop(b * batch // 8, (b + 1) * batch // 8, extract_above, 0)
            forward_one(b, 0, 1)
            exchange_start(0, b)
        gather_rows(z.plain // 32 * 16, z.plain)
        lax.fori_loop(0, images // 4, repack, 0)
        for k in range(1, n):
            cot_copy(0, k, 0, 2).start()
        exchange_pass(0, 0)
        lax.fori_loop(images // 4, images // 2, repack, 0)
        exchange_pass(0, 1)
        if z.block:
            send_levels(n - 1, n)
        lax.fori_loop(images // 2, images, repack, 0)
        near[sh] = far[sh]

    pl.run_scoped(
        first_part,
        pltpu.VMEM((images, z.in_cols, held, c_in), BF16),
        pltpu.VMEM((images, z.cols, z.out_rows, z.c_local), BF16),
    )

    def pass_copy(k):
        part = plane(k)
        piece = wide_rows(core, part, 0, z.plain)
        return remote(piece, piece, ag_pair_sem.at[0, k], ag_pair_sem.at[1, part], sibling)

    def norm_one(b):
        pixels = totals[0, b, 4:5]
        center_three, rstd_three = moments(0, b, 0, pixels)
        center_point, rstd_point = moments(0, b, 2, pixels)
        scale_three = gains_one[0:1] * rstd_three
        scale_point = gains_one[1:2] * rstd_point
        par[0, b, 0:1] = scale_three
        par[0, b, 1:2] = scale_point
        par[0, b, 2:3] = (shifts_one[0:1] - center_three * scale_three) + (
            shifts_one[1:2] - center_point * scale_point
        )
        par[0, b, 3:4] = center_three
        par[0, b, 4:5] = center_point
        par[0, b, 5:6] = rstd_three
        par[0, b, 6:7] = rstd_point
        par[0, b, 7:8] = pixels

    def first_sum(here, b, first=0, count_=rows):
        some = slice(first, first + count_)
        return (
            flat(z3a[here, some]) * par[0, b, 0:1]
            + flat(z1a[here, some]) * par[0, b, 1:2]
            + par[0, b, 2:3]
        )

    def put_three(target, here, at, count_, value):
        length = value.shape[0]
        shape = (-1, count_, KEPT, c_mid)
        before = pltpu.roll(value, 1, 0)
        after = pltpu.roll(value, length - 1, 0)
        target[here, at : at + count_, :, 0:c_mid] = before.astype(BF16).reshape(shape)
        target[here, at : at + count_, :, c_mid : 2 * c_mid] = value.astype(BF16).reshape(shape)
        target[here, at : at + count_, :, 2 * c_mid : 3 * c_mid] = after.astype(BF16).reshape(shape)

    def send_rims(source, sems):
        copies = []
        center = pl.ds(c_mid, c_mid)
        for b in range(MICRO):
            some = pl.ds(b * batch, batch)
            copies.append(
                (
                    remote(
                        source.at[some, 1, :, center],
                        halo.at[1, some],
                        sems.at[0, b],
                        sems.at[1, b],
                        above,
                    ),
                    remote(
                        source.at[some, rows, :, center],
                        halo.at[0, some],
                        sems.at[2, b],
                        sems.at[3, b],
                        below,
                    ),
                )
            )
        return copies

    def spread_halo(target, side, b):
        def one(i, carry):
            here = pl.ds(b * batch + i * 8, 8)
            value = flat(halo[side, here]).astype(F32)
            put_three(target, here, 0 if side == 0 else rows + 1, 1, value)
            return carry

        lax.fori_loop(0, batch // 8, one, 0)

    def start_rims(copies, b):
        pl.when(has_above)(copies[b][0].start)
        pl.when(has_below)(copies[b][1].start)

    def take_rims(copies, b):
        pl.when(has_below)(copies[b][0].wait_recv)
        pl.when(has_above)(copies[b][1].wait_recv)

    def close_rims(copies):
        for b in range(MICRO):
            pl.when(has_above)(copies[b][0].wait_send)
            pl.when(has_below)(copies[b][1].wait_send)

    inner = (1, rows - 2) if rows > 2 else None
    outer = sorted({0, rows - 1})

    class Group:
        def __init__(self, size, own, peer):
            self.size, self.own, self.peer = size, own, peer

    by_plane = Group(n, sh, lambda k: (plane(k), (dp, plane(k))))
    by_depth = Group(depth, deep, deep_peer)

    class Reduce:
        def __init__(self, first, second, g, r1, r2, s, r3, r4, sems, sub):
            self.first, self.second = first, second
            self.g, self.r1, self.r2, self.s, self.r3, self.r4 = g, r1, r2, s, r3, r4
            self.sems, self.piece = sems, second.size * sub

        def at(self, half, i):
            start = (half * self.first.size + i) * self.piece
            return pl.ds(pl.multiple_of(start, 16), self.piece)

        def pair_copy(self):
            start = pl.multiple_of((1 - core) * self.first.size * self.piece, 16)
            return remote(
                self.g.at[pl.ds(start, self.first.size * self.piece)],
                self.r1,
                self.sems.at[0, 0],
                self.sems.at[1, 0],
                sibling,
            )

        def start_pair(self):
            if pair == 2:
                sender.start(self.pair_copy)

        def start_first(self):
            if pair == 2:
                self.pair_copy().wait_recv()

                def join(i, carry):
                    at = self.at(core, i)
                    arrived = self.r1[pl.ds(pl.multiple_of(i * self.piece, 16), self.piece)]
                    self.g[at] = (self.g[at].astype(F32) + arrived.astype(F32)).astype(BF16)
                    return carry

                lax.fori_loop(0, self.first.size, join, 0)

            self.r2[self.first.own] = self.g[self.at(core, self.first.own)]

        def first_copy(self, k, part=0, parts=1):
            to, device = self.first.peer(k)
            length = self.piece // parts
            start = (core * self.first.size + to) * self.piece + part * length
            return remote(
                self.g.at[pl.ds(pl.multiple_of(start, 16), length)],
                self.r2.at[self.first.own, pl.ds(part * length, length)],
                self.sems.at[2, k],
                self.sems.at[3, self.first.own],
                device,
            )

        def send_first(self, part, parts):
            for k in range(1, self.first.size):
                self.first_copy(k, part, parts).start()

        def start_second(self):
            for k in range(1, self.first.size):
                other, device = self.first.peer(k)
                there = self.r2.at[other]
                remote(
                    there, there, self.sems.at[2, k], self.sems.at[3, other], device
                ).wait_recv()
                self.first_copy(k).wait_send()
            total = self.r2[0].astype(F32)
            for i in range(1, self.first.size):
                total = total + self.r2[i].astype(F32)
            self.s[...] = total.astype(BF16).reshape(self.s.shape)

            def second_copy(k):
                to, device = self.second.peer(k)
                return remote(
                    self.s.at[to],
                    self.r3.at[self.second.own],
                    self.sems.at[4, k],
                    self.sems.at[5, self.second.own],
                    device,
                )

            for k in range(1, self.second.size):
                sender.start(second_copy, k)
            self.r3[self.second.own] = self.s[self.second.own]

        def start_back(self):
            for k in range(1, self.second.size):
                other, device = self.second.peer(k)
                there = self.r3.at[other]
                remote(
                    there, there, self.sems.at[4, k], self.sems.at[5, other], device
                ).wait_recv()
            total = self.r3[0].astype(F32)
            for i in range(1, self.second.size):
                total = total + self.r3[i].astype(F32)
            self.r4[deep] = total.astype(BF16)

            def back_copy(k):
                own = self.r4.at[deep]
                return remote(
                    own, own, self.sems.at[6, k], self.sems.at[7, deep], deep_peer(k)[1]
                )

            for k in range(1, depth):
                sender.start(back_copy, k)

        def finish_back(self):
            for k in range(1, depth):
                other, device = deep_peer(k)
                there = self.r4.at[other]
                remote(
                    there, there, self.sems.at[6, k], self.sems.at[7, other], device
                ).wait_recv()

    red_two = Reduce(
        by_depth,
        by_plane,
        wide,
        two_r1.at[pl.ds(0, n * z.piece_two)],
        two_r2,
        two_s,
        two_r3,
        two_r4,
        ar_two,
        z.sub_two,
    )
    red_one = Reduce(
        by_plane,
        by_depth,
        g_one,
        two_r1.at[pl.ds(0, n * z.piece_one)],
        one_r2,
        one_s,
        one_r3,
        one_r4,
        ar_one,
        z.sub_one,
    )

    def out_copy(b, k, part=0, parts=1):
        to = plane(k)
        length = batch // parts
        some = pl.ds(b * batch + part * length, length)
        return remote(
            near.at[to, some],
            far.at[sh, some],
            out_sem.at[0, b * n + k],
            out_sem.at[1, b * n + sh],
            (dp, to),
        )

    def send_out(b, part, parts):
        for k in range(1, n):
            out_copy(b, k, part, parts).start()

    def second_part(hid, k2, p2, z3b, dz3, dz1):
        rims = send_rims(hid, hid_sem)

        def make_hidden(t, carry):
            here = images_at(t)
            b = t // per_batch
            total = first_sum(here, b)
            put_three(hid, here, 1, rows, pixels_at() * (total * sigmoid(total)))
            return carry

        for b in range(MICRO):
            exchange_end(0, b)
            norm_one(b)
            lax.fori_loop(b * per_batch, (b + 1) * per_batch, make_hidden, 0)
            start_rims(rims, b)
        for k in range(1, n):
            part = plane(k)
            piece = wide_rows(core, part, 0, z.plain)
            remote(piece, piece, ag_sem.at[0, k], ag_sem.at[1, part], (dp, part)).wait_recv()
            if pair == 2:
                gather.start(pass_copy, k)
        if z.block:
            for k in range(1, depth):
                other, device = deep_peer(k)
                there = blocks(core, other, 0, n)
                remote(
                    there, there, block_sem.at[2, k], block_sem.at[3, other], device
                ).wait_recv()
            if pair == 2:
                gather.start(level_pass)
        if pair == 2:
            for k in range(1, n):
                part = plane(k)
                piece = wide_rows(1 - core, part, 0, z.plain)
                remote(
                    piece, piece, ag_pair_sem.at[0, k], ag_pair_sem.at[1, part], sibling
                ).wait_recv()
            if z.block:
                there = blocks(1 - core, 0, 0, n, depth)
                remote(
                    there, there, block_sem.at[4, 0], block_sem.at[5, 0], sibling
                ).wait_recv()
        gather.finish()
        for k in range(1, n):
            gather_copy(k).wait_send()
        if z.block:
            for k in range(1, n):
                block_copy(k).wait_send()
            for k in range(1, depth):
                level_copy(k).wait_send()
        for t in range(10):
            half, first = t // z.half, t % z.half * z.c_pad
            for part in range(n):
                done = 0
                while done < z.c_local:
                    at = first + done
                    if at < z.plain:
                        length = min(z.plain - at, z.c_local - done)
                        start = (half * n + part) * z.piece_two + at
                        value = wide[start : start + length]
                    else:
                        level, offset = divmod(at - z.plain, z.block)
                        length = min(z.block - offset, z.c_local - done)
                        start = ((half * depth + level) * n + part) * z.block + offset
                        value = two_r1[start : start + length]
                    base = part * z.c_local + done
                    if t < 9:
                        base += t % 3 * c_mid
                        k2[t // 3, base : base + length] = value
                    else:
                        p2[base : base + length] = value
                    done += length

        def forward_two(b, first, count_):
            start = b * batch
            here = pl.ds(start, batch)
            three_branch = dot(flat(hid[here, first : first + count_]), k2[0])
            for d in (1, 2):
                three_branch = three_branch + dot(
                    flat(hid[here, first + d : first + d + count_]), k2[d]
                )
            center = flat(hid[here, first + 1 : first + 1 + count_, :, c_mid : 2 * c_mid])
            point_branch = dot(center, p2[...])
            z3b[here, first : first + count_] = shaped(three_branch, count_)
            m = mask_of(start, batch, first, count_)
            masked = three_branch * m
            add_to(b, 0, masked)
            add_to(b, 1, masked * three_branch)
            masked = point_branch * m
            add_to(b, 2, masked)
            add_to(b, 3, masked * point_branch)
            center = center.astype(F32)
            masked = center * m
            add_to(b, 4, masked)
            add_to(b, 5, masked * center)

        if inner:
            for b in range(MICRO):
                forward_two(b, *inner)
        for b in range(MICRO):
            take_rims(rims, b)
            spread_halo(hid, 0, b)
            spread_halo(hid, 1, b)
            for at in outer:
                forward_two(b, at, 1)
                if b and at == 0:
                    exchange_pass(1, 0)
            exchange_start(1, b)
        for k in range(1, n):
            cot_copy(0, k, 1, 2).start()
        for k in range(1, n):
            cot_copy(1, k).start()

        def norm_two(b):
            pixels = par[0, b, 7:8]
            offset = 0.0
            for i in range(3):
                center, rstd = moments(1, b, 2 * i, pixels)
                scale = totals[0, 0, 8 + i : 9 + i] * rstd
                par[1, b, i : i + 1] = scale
                par[1, b, 4 + i : 5 + i] = center
                par[1, b, 7 + i : 8 + i] = rstd
                offset = offset + (totals[0, 0, 11 + i : 12 + i] - center * scale)
            par[1, b, 3:4] = offset

        def slope_two(t, carry):
            here = images_at(t)
            b = t // per_batch
            taken = [near[part, here] for part in range(n)]
            cot = jnp.stack(
                [
                    jnp.concatenate(
                        [v[:, :, r * z.c_local : (r + 1) * z.c_local] for v in taken], axis=2
                    )
                    for r in range(rows)
                ],
                axis=1,
            )
            v3 = flat(z3b[here])
            vi = flat(hid[here, 1 : rows + 1, :, c_mid : 2 * c_mid])
            v1 = dot(vi, p2[...])
            vi = vi.astype(F32)
            total = (
                v3 * par[1, b, 0:1] + v1 * par[1, b, 1:2] + vi * par[1, b, 2:3] + par[1, b, 3:4]
            )
            m = mask_at(t)
            gate = sigmoid(total)
            down = m * flat(cot).astype(F32) * (gate * (1.0 + total * (1.0 - gate)))
            slope[here] = shaped(down)
            add_to(b, 0, down)
            add_to(b, 1, down * (v3 - par[1, b, 4:5]))
            add_to(b, 2, down * (v1 - par[1, b, 5:6]))
            add_to(b, 3, down * (vi - par[1, b, 6:7]))
            out = shaped((m * (total * gate)).astype(BF16))
            for part in range(n):
                lanes = slice(part * z.c_local, (part + 1) * z.c_local)
                near[part, here] = jnp.concatenate(
                    [out[:, r, :, lanes] for r in range(rows)], axis=2
                )
            return carry

        def block(t):
            return t // 3, slice(t % 3 * c_mid, (t % 3 + 1) * c_mid)

        for t in range(5):
            one, other = k2[block(t)], k2[block(8 - t)]
            k2[block(t)] = other.T
            if t != 4:
                k2[block(8 - t)] = one.T

        for b in range(MICRO):
            exchange_end(1, b)
            norm_two(b)
            for k in range(1, n):
                part = plane(k)
                there = near.at[part, pl.ds(b * batch, batch)]
                remote(
                    there, there, cot_sem.at[0, b * n + k], cot_sem.at[1, b * n + part], (dp, part)
                ).wait_recv()
            for t in range(per_batch):
                slope_two(b * per_batch + t, 0)
                if t == 0:
                    exchange_pass(1, 1) if b == 0 else exchange_pass(2, 0)
            if b == 0:
                for k in range(1, n):
                    cot_copy(0, k).wait_send()
            exchange_start(2, b)
            if b == 0:
                for k in range(1, n):
                    cot_copy(1, k).wait_send()
        send_out(0, 0, 2)
        far[sh] = near[sh]

        def turn_two(b):
            pixels = par[0, b, 7:8]
            slopes = totals[2, b, 0:1]
            for i in range(3):
                rstd = par[1, b, 7 + i : 8 + i]
                cross = totals[2, b, 1 + i : 2 + i] * rstd
                scale = par[1, b, i : i + 1]
                tilt = -scale * rstd * cross / pixels
                par[2, b, 3 * i : 3 * i + 1] = scale
                par[2, b, 3 * i + 1 : 3 * i + 2] = tilt
                par[2, b, 3 * i + 2 : 3 * i + 3] = (
                    -scale * slopes / pixels - tilt * par[1, b, 4 + i : 5 + i]
                )

        rims_back = send_rims(dz3, dz_sem)

        def make_dz(t, carry):
            here = images_at(t)
            b = t // per_batch
            m = mask_at(t)
            down = flat(slope[here])
            value = down * par[2, b, 0:1] + m * (flat(z3b[here]) * par[2, b, 1:2] + par[2, b, 2:3])
            put_three(dz3, here, 1, rows, value)
            v1 = dot(flat(hid[here, 1 : rows + 1, :, c_mid : 2 * c_mid]), p2[...])
            value = down * par[2, b, 3:4] + m * (v1 * par[2, b, 4:5] + par[2, b, 5:6])
            dz1[here] = shaped(value.astype(BF16))
            return carry

        def backward_two(b, first, count_):
            start = b * batch
            here = pl.ds(start, batch)
            some = slice(first, first + count_)
            total = dot_nt(flat(dz1[here, some]), p2[...])
            for k in range(3):
                total = total + dot(flat(dz3[here, first + k : first + k + count_]), k2[k])
            m = mask_of(start, batch, first, count_)
            vi = flat(hid[here, first + 1 : first + 1 + count_, :, c_mid : 2 * c_mid]).astype(F32)
            total = total + (
                flat(slope[here, some]) * par[2, b, 6:7]
                + m * (vi * par[2, b, 7:8] + par[2, b, 8:9])
            )
            total = total.astype(BF16).astype(F32)
            summed = first_sum(here, b, first, count_)
            gate = sigmoid(summed)
            down = m * total * (gate * (1.0 + summed * (1.0 - gate)))
            slope[here, some] = shaped(down, count_)
            add_to(b, 0, down)
            add_to(b, 1, down * (flat(z3a[here, some]) - par[0, b, 3:4]))
            add_to(b, 2, down * (flat(z1a[here, some]) - par[0, b, 4:5]))

        exchange_end(2, 0)
        turn_two(0)
        lax.fori_loop(0, per_batch, make_dz, 0)
        start_rims(rims_back, 0)
        exchange_pass(2, 1)
        if inner:
            backward_two(0, *inner)
        exchange_end(2, 1)
        turn_two(1)
        lax.fori_loop(per_batch, 2 * per_batch, make_dz, 0)
        start_rims(rims_back, 1)

        def mine(value):
            result = jnp.zeros((1, z.c_local), F32)
            for part in range(n):
                here = value[:, part * z.c_local : (part + 1) * z.c_local]
                result = result + jnp.where(sh == part, here, 0.0)
            return result

        shifts = mine(totals[2, 0, 0:1] + totals[2, 1, 0:1])
        for i in range(3):
            cross = [
                totals[2, b, 1 + i : 2 + i] * par[1, b, 7 + i : 8 + i] for b in range(MICRO)
            ]
            grad_gains_two[i : i + 1] = mine(cross[0] + cross[1])
            grad_shifts_two[i : i + 1] = shifts

        def put_two(t, value):
            value = value.astype(BF16)
            half, first = t // z.half, t % z.half * z.c_pad
            for part in range(n):
                done = 0
                while done < z.c_local:
                    block, offset = divmod(first + done, z.sub_two)
                    length = min(z.sub_two - offset, z.c_local - done)
                    start = ((half * depth + block) * n + part) * z.sub_two + offset
                    have = part * z.c_local + done
                    wide[start : start + length] = value[have : have + length]
                    done += length

        center = pl.ds(c_mid, c_mid)
        for d in range(3):
            value = dot_tn(flat(hid[:, d : d + rows]), flat(dz3[:, 1 : rows + 1, :, center]))
            for c in range(3):
                put_two(3 * d + c, value[c * c_mid : (c + 1) * c_mid])
        put_two(9, dot_tn(flat(hid[:, 1 : rows + 1, :, center]), flat(dz1[...])))
        red_two.start_pair()

        if inner:
            backward_two(1, *inner)
        red_two.start_first()
        red_two.send_first(0, n)
        for b in range(MICRO):
            take_rims(rims_back, b)
            spread_halo(dz3, 0, b)
            spread_halo(dz3, 1, b)
            for at in outer:
                backward_two(b, at, 1)
                if b and at == 0:
                    exchange_pass(3, 0)
            exchange_start(3, b)
        send_out(0, 1, 2)
        close_rims(rims)
        close_rims(rims_back)

    pl.run_scoped(
        second_part,
        pltpu.VMEM((images, rows + 2, KEPT, 3 * c_mid), BF16),
        pltpu.VMEM((3, 3 * c_mid, c_mid), BF16),
        pltpu.VMEM((c_mid, c_mid), BF16),
        pltpu.VMEM((images, rows, KEPT, c_mid), F32),
        pltpu.VMEM((images, rows + 2, KEPT, 3 * c_mid), BF16),
        pltpu.VMEM((images, rows, KEPT, c_mid), BF16),
    )

    def third_part(dz3, dz1, one_acc, staged, out_own, turned):
        def turn_one(b):
            pixels = par[0, b, 7:8]
            slopes = totals[3, b, 0:1]
            for i in range(2):
                rstd = par[0, b, 5 + i : 6 + i]
                cross = totals[3, b, 1 + i : 2 + i] * rstd
                scale = par[0, b, i : i + 1]
                tilt = -scale * rstd * cross / pixels
                par[3, b, 3 * i : 3 * i + 1] = scale
                par[3, b, 3 * i + 1 : 3 * i + 2] = tilt
                par[3, b, 3 * i + 2 : 3 * i + 3] = (
                    -scale * slopes / pixels - tilt * par[0, b, 3 + i : 4 + i]
                )

        rims = [
            remote(
                dz3.at[pl.ds(b * batch, batch), 0, :, pl.ds(0, c_mid)],
                halo.at[1, pl.ds(b * batch, batch)],
                e_sem.at[0, b],
                e_sem.at[1, b],
                above,
            )
            for b in range(MICRO)
        ]

        def turn_kernels():
            def tap(d, c):
                if c == 0:
                    return jnp.concatenate([k1_win[d, 256:384], k1_win[d, 192:256]], axis=0)
                return k1_win[d, 0:192] if c == 1 else k1_win[d, 384:576]

            order = [
                [tap(1, 1), p1_win[0:192]],
                [tap(1, 2), tap(1, 0)],
                [tap(2, 1), tap(0, 1)],
                [tap(2, 2), tap(2, 0)],
                [tap(0, 2), tap(0, 0)],
            ]
            for i, both in enumerate(order):
                for j, value in enumerate(both):
                    turned[i, j * c_mid : (j + 1) * c_mid] = value.T

        def make_dz(t, carry):
            here = images_at(t)
            b = t // per_batch
            m = mask_at(t)
            down = flat(slope[here])
            value = down * par[3, b, 0:1] + m * (flat(z3a[here]) * par[3, b, 1:2] + par[3, b, 2:3])
            after = pltpu.roll(value, value.shape[0] - 1, 0)
            dz3[here, 0:rows, :, 0:c_mid] = shaped(value.astype(BF16))
            dz3[here, 0:rows, :, c_mid : 2 * c_mid] = shaped(after.astype(BF16))
            value = down * par[3, b, 3:4] + m * (flat(z1a[here]) * par[3, b, 4:5] + par[3, b, 5:6])
            dz1[here] = shaped(value.astype(BF16))
            return carry

        def place_out(i, carry):
            lines = []
            for part in range(n):
                value = far[part, i].astype(F32)
                lines += [value[:, r * z.c_local : (r + 1) * z.c_local] for r in range(rows)]
            value = jnp.swapaxes(jnp.stack(lines), 0, 1)[0 : z.cols]
            out_own[i] = value.astype(BF16)
            return carry

        def take_out(b):
            for k in range(1, n):
                part = plane(k)
                there = far.at[part, pl.ds(b * batch, batch)]
                remote(
                    there, there, out_sem.at[0, b * n + k], out_sem.at[1, b * n + part], (dp, part)
                ).wait_recv()
                out_copy(b, k).wait_send()
            lax.fori_loop(b * batch, (b + 1) * batch, place_out, 0)

        def put_one(b, base, value):
            there = slice(base, base + value.shape[0])
            if b:
                value = one_acc[there] + value
            if b < MICRO - 1:
                one_acc[there] = value
            else:
                g_one[there] = value.astype(BF16)

        def gradients_one(b):
            some = pl.ds(b * batch, batch)
            own = flat(dz3[some, 0:rows, :, 0:c_mid])
            for d in range(3):
                if d == 1:
                    side = flat(even_win[some])
                else:
                    side = flat(odd_win[some, d // 2 : d // 2 + rows])
                value = dot_tn(side, own)
                base = 3 * d * c_in
                put_one(b, base + c_in, value[0:192])
                put_one(b, base + 128, value[192:256])
                put_one(b, base, value[256:384])
                put_one(b, base + 2 * c_in, value[384:576])
            side = flat(even_win[some, :, :, 0:256])
            put_one(b, 9 * c_in, dot_tn(side, flat(dz1[some]))[0:192])

        if g_one.shape[0] > 10 * c_in:
            g_one[10 * c_in :] = jnp.zeros((g_one.shape[0] - 10 * c_in, c_mid), BF16)
        turn_kernels()
        for b in range(MICRO):
            exchange_end(3, b)
            turn_one(b)
            lax.fori_loop(b * per_batch, (b + 1) * per_batch, make_dz, 0)
            pl.when(has_above)(rims[b].start)
            if b == 0:
                exchange_pass(3, 1)
                for part in range(1, n):
                    red_two.send_first(part, n)
            gradients_one(b)
        shifts = totals[3, 0, 0:1] + totals[3, 1, 0:1]
        for i in range(2):
            cross = [
                totals[3, b, 1 + i : 2 + i] * par[0, b, 5 + i : 6 + i] for b in range(MICRO)
            ]
            grad_gains_one[i : i + 1] = cross[0] + cross[1]
            grad_shifts_one[i : i + 1] = shifts

        red_one.start_pair()
        for b in range(MICRO):
            pl.when(has_below)(rims[b].wait_recv)

        def spread(t, carry):
            here = images_at(t)
            value = flat(halo[1, here]).astype(F32)
            after = pltpu.roll(value, value.shape[0] - 1, 0)
            dz3[here, rows, :, 0:c_mid] = value.astype(BF16).reshape(tile, KEPT, c_mid)
            dz3[here, rows, :, c_mid : 2 * c_mid] = after.astype(BF16).reshape(tile, KEPT, c_mid)
            return carry

        lax.fori_loop(0, z.tiles, spread, 0)
        red_one.start_first()
        red_one.send_first(0, 1)
        send_out(1, 0, 2)
        send_out(1, 1, 2)

        some = staged.shape[1]
        steps = images // some

        def staged_copy(i, slot):
            return pltpu.make_async_copy(
                staged.at[slot],
                grad_in_hbm.at[pl.ds(i * some, some)],
                gi_sem.at[slot],
            )

        def input_grad(i, carry):
            here = pl.ds(i * some, some)
            slot = lax.rem(i, 2)
            own = flat(dz3[here, 0:rows])
            after = flat(dz3[here, 1 : rows + 1])
            own_c, after_c = own[:, 0:c_mid], after[:, 0:c_mid]
            value = [
                [
                    dot(own_c, turned[0, 0:c_mid]) + dot(flat(dz1[here]), turned[0, c_mid:]),
                    dot(own, turned[1]),
                ],
                [
                    dot(own_c, turned[2, 0:c_mid]) + dot(after_c, turned[2, c_mid:]),
                    dot(own, turned[3]) + dot(after, turned[4]),
                ],
            ]

            @pl.when(i >= 2)
            def _():
                staged_copy(i, slot).wait()

            none = [jnp.zeros((KEPT, c_in), F32)] * (held - z.in_rows)
            for g in range(some):
                sides = []
                for c in range(2):
                    lines = [
                        value[r][c].reshape(some, rows, KEPT, c_in)[g, at]
                        for at in range(rows)
                        for r in range(2)
                    ]
                    sides.append(jnp.swapaxes(jnp.stack(lines + none), 0, 1)[0 : z.cols])
                staged[slot, g] = jnp.stack(sides, axis=1).reshape(z.in_cols, held, c_in)
            staged_copy(i, slot).start()
            return carry

        cuts = [0, 0, steps - steps // 4, steps]
        lax.fori_loop(cuts[0], cuts[2], input_grad, 0)
        red_one.start_second()
        lax.fori_loop(cuts[2], cuts[3], input_grad, 0)
        take_out(0)
        red_two.start_second()
        red_one.start_back()
        take_out(1)
        out_write = pltpu.make_async_copy(out_own, out_hbm, gi_sem.at[2])
        out_write.start()
        for i in range(max(0, steps - 2), steps):
            staged_copy(i, i % 2).wait()
        out_write.wait()
        for b in range(MICRO):
            pl.when(has_above)(rims[b].wait_send)

    some = max(1, min(images // 2, 256 // (rows * KEPT)))
    pl.run_scoped(
        third_part,
        pltpu.VMEM((images, rows + 1, KEPT, 2 * c_mid), BF16),
        pltpu.VMEM((images, rows, KEPT, c_mid), BF16),
        pltpu.VMEM((10 * z.c_in, c_mid), F32),
        pltpu.VMEM((2, some, z.in_cols, held, c_in), F32),
        pltpu.VMEM((images, z.cols, z.out_rows, z.c_local), BF16),
        pltpu.VMEM((5, 2 * c_mid, c_in), BF16),
    )

    red_one.finish_back()
    def one_at(half, part):
        return grad_one_hbm.at[half, part]

    one_own = pltpu.make_async_copy(red_one.r4, one_at(core, sh), ar_one.at[8, 0])
    one_own.start()

    def one_pair_copy():
        return remote(
            red_one.r4, one_at(core, sh), ar_one.at[12, 0], ar_one.at[13, sh], sibling
        )

    def one_plane_copy(k):
        return remote(
            red_one.r4, one_at(core, sh), ar_one.at[9, k], ar_one.at[10, sh], (dp, plane(k))
        )

    def one_pass_copy(k):
        part = plane(k)
        at = one_at(core, part)
        return remote(at, at, ar_one.at[11, k], ar_one.at[13, part], sibling)

    if pair == 2:
        sender.start(one_pair_copy)
    for k in range(1, n):
        sender.start(one_plane_copy, k)
    red_two.start_back()
    red_two.finish_back()
    two_at = grad_two_hbm.at[core]
    two_own = pltpu.make_async_copy(red_two.r4, two_at, ar_two.at[8, 0])
    two_own.start()
    two_pair = remote(red_two.r4, two_at, ar_two.at[9, 0], ar_two.at[10, 0], sibling)
    if pair == 2:
        two_pair.start()
    for k in range(1, n):
        part = plane(k)
        at = one_at(core, part)
        remote(at, at, ar_one.at[9, k], ar_one.at[10, part], (dp, part)).wait_recv()
        if pair == 2:
            sender.start(one_pass_copy, k)
    if pair == 2:
        for k in range(n):
            part = plane(k)
            at = one_at(1 - core, part)
            remote(at, at, ar_one.at[11, k], ar_one.at[13, part], sibling).wait_recv()
        two_pair.wait_send()
        remote(
            red_two.r4, grad_two_hbm.at[1 - core], ar_two.at[9, 0], ar_two.at[10, 0], sibling
        ).wait_recv()
    two_own.wait()
    one_own.wait()
    sender.finish()


def build(mesh):
    def shards(
        x_input,
        image_counts,
        kernel_one,
        point_one,
        block_one_norm_gains,
        block_one_norm_shifts,
        kernel_two,
        point_two,
        block_two_norm_gains,
        shifts_two,
        cotangent,
    ):
        z = Sizes.__new__(Sizes)
        whole_x = jax.ShapeDtypeStruct(
            (
                x_input.shape[0] * mesh.shape["dp"],
                x_input.shape[1] * mesh.shape["shard"],
                *x_input.shape[2:],
            ),
            x_input.dtype,
        )
        z.__init__(mesh, whole_x, cotangent, point_one)
        n, pair, depth = z.parts, z.pair, z.depth
        x_turned = x_input.transpose(0, 2, 1, 3)
        if z.held_rows != z.in_rows:
            more = z.held_rows - z.in_rows
            x_turned = jnp.pad(x_turned, ((0, 0), (0, 0), (0, more), (0, 0)))
        if z.c_pad != z.c_local:
            more = z.c_pad - z.c_local
            kernel_two = jnp.pad(kernel_two, ((0, 0), (0, 0), (0, more), (0, 0)))
            point_two = jnp.pad(point_two, ((0, more), (0, 0)))

        vmem = pl.BlockSpec(memory_space=pltpu.VMEM)
        anywhere = pl.BlockSpec(memory_space=pl.ANY)
        image_rows = (z.images, z.rows, KEPT)
        dma = pltpu.SemaphoreType.DMA
        outs = pl.pallas_call(
            functools.partial(kernel, z),
            out_shape=(
                jax.ShapeDtypeStruct((z.images, z.cols, z.out_rows, z.c_local), BF16),
                jax.ShapeDtypeStruct((z.images, z.in_cols, z.held_rows, z.c_in), F32),
                jax.ShapeDtypeStruct((pair, n, depth, z.sub_one, z.c_mid), BF16),
                jax.ShapeDtypeStruct((pair, depth, z.sub_two, z.c_mid), BF16),
                jax.ShapeDtypeStruct((2, z.c_mid), F32),
                jax.ShapeDtypeStruct((2, z.c_mid), F32),
                jax.ShapeDtypeStruct((3, z.c_local), F32),
                jax.ShapeDtypeStruct((3, z.c_local), F32),
            ),
            in_specs=[
                pl.BlockSpec(memory_space=pltpu.SMEM),
                anywhere,
                anywhere,
                anywhere,
                vmem,
                vmem,
                anywhere,
                anywhere,
                vmem,
                vmem,
                anywhere,
            ],
            out_specs=(anywhere, anywhere, anywhere, anywhere, vmem, vmem, vmem, vmem),
            scratch_shapes=[
                pltpu.VMEM((z.images, z.rows + 1, KEPT, 640), BF16),
                pltpu.VMEM((*image_rows, 640), BF16),
                pltpu.VMEM((3, 640, z.c_mid), BF16),
                pltpu.VMEM((256, z.c_mid), BF16),
                pltpu.VMEM((*image_rows, z.c_mid), F32),
                pltpu.VMEM((*image_rows, z.c_mid), F32),
                pltpu.VMEM((z.images, KEPT, z.c_mid), BF16),
                pltpu.VMEM((2, z.images, KEPT, z.c_mid), BF16),
                pltpu.VMEM((pair * n * z.piece_two, z.c_mid), BF16),
                pltpu.VMEM((n, z.images, KEPT, z.rows * z.c_local), BF16),
                pltpu.VMEM((n, z.images, KEPT, z.rows * z.c_local), BF16),
                pltpu.VMEM((*image_rows, z.c_mid), F32),
                pltpu.VMEM((z.rows, KEPT, 128), F32),
                pltpu.VMEM((MICRO, 8, 8, z.c_mid), F32),
                pltpu.VMEM((4, MICRO, 16, z.c_mid), F32),
                pltpu.VMEM((4, MICRO, PAYLOAD, z.c_mid), F32),
                pltpu.VMEM((4, MICRO, pair * n, PAYLOAD, z.c_mid), F32),
                pltpu.VMEM((4, MICRO, depth, PAYLOAD, z.c_mid), F32),
                pltpu.VMEM((4, MICRO, PAYLOAD, z.c_mid), F32),
                pltpu.VMEM((pair * n * z.piece_one, z.c_mid), BF16),
                pltpu.VMEM((n, z.piece_one, z.c_mid), BF16),
                pltpu.VMEM((depth, z.sub_one, z.c_mid), BF16),
                pltpu.VMEM((depth, z.sub_one, z.c_mid), BF16),
                pltpu.VMEM((depth, z.sub_one, z.c_mid), BF16),
                pltpu.VMEM((n * max(z.piece_one, z.piece_two), z.c_mid), BF16),
                pltpu.VMEM((depth, n * z.sub_two, z.c_mid), BF16),
                pltpu.VMEM((n, z.sub_two, z.c_mid), BF16),
                pltpu.VMEM((n, z.sub_two, z.c_mid), BF16),
                pltpu.VMEM((depth, z.sub_two, z.c_mid), BF16),
                dma((24,)),
                dma((2, MICRO)),
                dma((4, MICRO)),
                dma((4, MICRO)),
                dma((2, MICRO)),
                dma((2, n)),
                dma((2, n)),
                dma((6, max(n, depth))),
                dma((2, MICRO * n)),
                dma((2, MICRO * n)),
                dma((4 * MICRO, pair * n)),
                dma((4 * MICRO, pair * n)),
                dma((4 * MICRO, depth)),
                dma((4 * MICRO, depth)),
                dma((14, max(n, depth))),
                dma((14, max(n, depth))),
                dma((max(4, z.images // 8 + 1),)),
            ],
            compiler_params=pltpu.CompilerParams(
                collective_id=0, has_side_effects=True, vmem_limit_bytes=63 * 2**20
            ),
        )(
            image_counts,
            x_turned,
            kernel_one,
            point_one,
            block_one_norm_gains,
            block_one_norm_shifts,
            kernel_two,
            point_two,
            block_two_norm_gains,
            shifts_two,
            cotangent.transpose(0, 2, 1, 3),
        )
        block_out, grad_input, grad_one, grad_two, *small = outs
        block_out = block_out.transpose(0, 2, 1, 3).astype(F32)
        grad_input = grad_input[:, :, : z.in_rows].transpose(0, 2, 1, 3)
        grad_one = grad_one.reshape(-1, z.c_mid)
        grad_kernel_one = grad_one[: 9 * z.c_in].astype(F32).reshape(3, 3, z.c_in, z.c_mid)
        grad_point_one = grad_one[9 * z.c_in : 10 * z.c_in].astype(F32)
        grad_two = grad_two.reshape(pair, -1, z.c_mid)[:, : z.half * z.c_pad]
        grad_two = grad_two.reshape(pair * z.half, z.c_pad, z.c_mid)[:, : z.c_local].astype(F32)
        grad_kernel_two = grad_two[:9].reshape(3, 3, z.c_local, z.c_mid)
        return (
            block_out,
            grad_input,
            grad_kernel_one,
            grad_point_one,
            small[0],
            small[1],
            grad_kernel_two,
            grad_two[9],
            small[2],
            small[3],
        )

    return shards


def solution(mesh):
    placed = (
        P("dp", "shard", None, None),
        P("dp"),
        P(),
        P(),
        P(),
        P(),
        P(None, None, "shard", None),
        P("shard", None),
        P(None, "shard"),
        P(None, "shard"),
        P("dp", None, None, "shard"),
    )
    return jax.shard_map(
        build(mesh),
        mesh=mesh,
        in_specs=placed,
        out_specs=(
            P("dp", None, None, "shard"),
            P("dp", "shard", None, None),
            P(),
            P(),
            P(),
            P(),
            P(None, None, "shard", None),
            P("shard", None),
            P(None, "shard"),
            P(None, "shard"),
        ),
        check_vma=False,
    )
```
